128 devices in a mesh: lat: 8 (over x, core), lon: 16 (over y, z).
Axes of the slice: x: 4, y: 4, z: 4, core: 2. Of those that a mesh axis runs over, the one named last changes fastest.
Arguments:
- footprints: bfloat16 [65536, 1024], P(('lat', 'lon')), may hold values from 0.0019989014 to 0.099609375
- dual_weights: bfloat16 [65536, 4], P(('lat', 'lon')), may hold values from -6 to 6
- target_device: int32 [65536, 1], P(('lat', 'lon')), may hold values from 0 to 127; in each aligned block of 512 rows (0 to 511, 512 to 1023, ...) at most 8 rows name the same one
- target_block: int32 [65536], P(('lat', 'lon')), may hold values from 0 to 255
- obs_slot: int32 [65536], P(('lat', 'lon')), may hold values from 0 to 7
- diffusivity: float32 [2048, 2048], P('lat', 'lon'), may hold values from 0.02 to 0.25
Outputs:
- dual_product: float32 [65536, 4], P(('lat', 'lon'))
The draws below stay inside these ranges and needn't reach their ends.
Inputs may be any that keep to these rules, and one draw needn't show every extreme that they name: `target_device`: among the 512 observations of one device, at most 8 name the same device, and exactly 8 do so for some device.
All inputs are finite; a program needn't handle non-finite values.
Results may differ from the reference program's by a relative error of at most 0.0006.
Values may be sent and summed in bfloat16 or wider, within the bound.
No kernel may reach another device: no remote copies, remote signals or barrier semaphores. Data moves between devices by JAX's collectives and lax.ppermute only.
A program may use at most 128 MiB of HBM per device.

```python
import math
import jax
import jax.numpy as jnp
import numpy as np
from jax import lax

SLOTS = 8
RHS = 4
CLON = 128
CLAT = 256
OBS_DEV = 512
PASSES = 4
CAP = 8
NOBS = 65536
NLAT = 2048
NLON = 2048
N_LAT = 8
N_LON = 16
DEVICES = 128


def plant(entries, stream_key, least, high):
    spot = [jax.random.randint(jax.random.fold_in(stream_key, axis), (), 0, length) for axis, length in enumerate(entries.shape)]
    main_axis = entries.shape.index(max(entries.shape))
    beside = spot[:main_axis] + [(spot[main_axis] + 1) % entries.shape[main_axis]] + spot[main_axis + 1:]
    return entries.at[tuple(spot)].set(least).at[tuple(beside)].set(high)


def levels(key, dims, pieces, least, high):
    gain = 1.0
    for axis_at, shards_of in pieces:
        steps = jax.random.uniform(jax.random.fold_in(jax.random.fold_in(key, 6), axis_at), (shards_of,), jnp.float32, least / len(pieces), high / len(pieces))
        gain = gain * jnp.repeat(jnp.exp(steps), dims[axis_at] // shards_of).reshape((-1,) + (1,) * (len(dims) - 1 - axis_at))
    return gain


def assign_block(stream_key, own, number, rows, count, top, bound, skew):
    ranking = jax.random.permutation(stream_key, count)
    packed, ordinary = load_shares(count, rows * top, bound, skew, True), load_shares(count, rows * top, bound, skew, False)
    places = jnp.arange(count)

    def named(sizes, turn):
        used = int((sizes > 0).sum())
        fixed = max(1, used // 4)
        moved = fixed + (places - fixed + turn * (used - fixed)) % max(1, count - fixed)
        return jnp.zeros((count,), jnp.int32).at[ranking[jnp.where(places < fixed, places, moved)]].set(jnp.asarray(sizes, jnp.int32))

    sizes = jnp.where(number % 4 == 0, named(packed, number // 4), named(ordinary, number - number // 4 - 1))
    mixed = jax.random.permutation(jax.random.fold_in(own, 3), count)
    source_of, receiver = mixed[0:count // 2 * 2:2], mixed[1:count // 2 * 2:2]
    slack = jnp.minimum(sizes[source_of] - 1, bound - sizes[receiver]) // 2
    slack = jnp.where((source_of == ranking[0]) | (receiver == ranking[0]) | (sizes[receiver] == 0), 0, jnp.maximum(slack, 0))
    moved = jax.random.randint(jax.random.fold_in(own, 4), (count // 2,), 0, 1 << 20) % (slack + 1)
    sizes = sizes.at[source_of].add(-moved).at[receiver].add(moved)
    members = jnp.searchsorted(jnp.cumsum(sizes), jnp.arange(rows * top), side="right").astype(jnp.int32)
    listing = members.reshape(top, rows).T
    listing = listing[jax.random.permutation(jax.random.fold_in(own, 1), rows)]
    turn = jax.random.randint(jax.random.fold_in(own, 2), (rows, 1), 0, top)
    return jnp.take_along_axis(listing, (jnp.arange(top)[None, :] + turn) % top, axis=1)


def load_shares(amount, total, most, lean, full):
    weights = [(1 << 20) // math.isqrt(grade ** lean) + 1 for grade in range(1, amount + 1)]
    largest = most if full else min(most, max(-(-total // amount), total * weights[0] // sum(weights)))
    least = 1 if total - largest >= amount - 1 else 0
    holding, rest = [largest] + [least] * (amount - 1), total - largest - least * (amount - 1)
    while rest > 0:
        candidates = [i for i in range(1, amount) if holding[i] < largest] or [i for i in range(1, amount) if holding[i] < most]
        whole, left = sum([weights[i] for i in candidates]), rest
        for i in candidates:
            extra = min(most - holding[i], max(1, left * weights[i] // whole), rest)
            holding[i] = holding[i] + extra
            rest = rest - extra
    return np.array(holding)


def gaussian(own_key, extent, width, most, pieces=(), kind=jnp.bfloat16):
    loudness = levels(own_key, extent, pieces, -0.22, 0.18) if pieces else 1.0
    array = jax.random.normal(own_key, extent, jnp.float32) * width * loudness
    return jnp.minimum(jnp.maximum(array, -most), most).astype(kind)


def setup_inputs(seed: int = 0) -> dict:
    arg_keys = jax.random.split(jax.random.key(seed), 7)
    footprints = jnp.clip(jnp.exp(math.log(0.099609375) - 3.9086586 * jax.random.uniform(arg_keys[0], (NOBS, SLOTS * CLON), jnp.float32) ** levels(arg_keys[0], (NOBS, SLOTS * CLON), ((0, 128),), -0.2, 0.2)), 0.0019989014, 0.099609375).astype(jnp.bfloat16)
    dual_weights = gaussian(arg_keys[1], (NOBS, RHS), 1.0, 6.0, ((0, 128),))
    target_device_keys = jax.random.split(jax.random.fold_in(arg_keys[2], 1), NOBS // OBS_DEV)
    target_device_turns = jax.random.permutation(jax.random.fold_in(arg_keys[2], 3), NOBS // OBS_DEV)
    target_device = jax.vmap(lambda own, number: assign_block(jax.random.fold_in(arg_keys[2], 2), own, number, OBS_DEV, DEVICES, 1, CAP, 2))(target_device_keys, target_device_turns).reshape((NOBS, 1))
    target_block = plant(jax.random.randint(arg_keys[3], (NOBS,), 0, CLAT), jax.random.fold_in(arg_keys[3], 1), 0, CLAT - 1).astype(jnp.int32)
    obs_slot = plant(jax.random.randint(arg_keys[4], (NOBS,), 0, SLOTS), jax.random.fold_in(arg_keys[4], 1), 0, SLOTS - 1).astype(jnp.int32)
    diffusivity = jnp.clip(jnp.exp(math.log(0.25) - 2.5257287 * jax.random.uniform(arg_keys[5], (NLAT, NLON), jnp.float32) ** levels(arg_keys[5], (NLAT, NLON), ((0, 8), (1, 16)), -0.2, 0.2)), 0.02, 0.25)
    return dict(footprints=footprints, dual_weights=dual_weights, target_device=target_device, target_block=target_block, obs_slot=obs_slot, diffusivity=diffusivity)


def diffuse(field, kap):
    north = jnp.sqrt(kap[:, 1:] * kap[:, :-1])
    east = jnp.sqrt(kap[..., 1:] * kap[..., :-1])
    centre = field[:, 1:-1, :, 1:-1]
    result = centre + north[:, 1:, :, 1:-1] * (field[:, 2:, :, 1:-1] - centre)
    result = result + north[:, :-1, :, 1:-1] * (field[:, :-2, :, 1:-1] - centre)
    result = result + east[:, 1:-1, :, 1:] * (field[:, 1:-1, :, 2:] - centre)
    result = result + east[:, 1:-1, :, :-1] * (field[:, 1:-1, :, :-2] - centre)
    return result

def pad_once(field):
    wrapped = jnp.pad(field, ((0, 0), (0, 0), (0, 0), (1, 1)), mode='wrap')
    return jnp.pad(wrapped, ((0, 0), (1, 1), (0, 0), (0, 0)))

def reference(footprints, dual_weights, target_device, target_block, obs_slot, diffusivity):
    devices = N_LAT * N_LON
    shaped = footprints.reshape(-1, SLOTS, CLON)
    live = jnp.arange(SLOTS, dtype=jnp.int32)[None, :, None] <= obs_slot[:, None, None]
    masked = jnp.where(live, shaped, jnp.zeros((), shaped.dtype))
    rows_all = target_device[:, 0] // N_LON * CLAT + target_block
    tiles_all = target_device[:, 0] % N_LON
    masked_c = masked.reshape(devices, OBS_DEV, SLOTS, CLON)
    weights_c = dual_weights.reshape(devices, OBS_DEV, RHS)
    rows_c = rows_all.reshape(devices, OBS_DEV).astype(jnp.int32)
    tiles_c = tiles_all.reshape(devices, OBS_DEV).astype(jnp.int32)

    def add_block(field, items):
        piece, weights, rows, tiles = items
        contrib = jnp.einsum('or,osc->orsc', weights.astype(jnp.float32), piece.astype(jnp.float32))
        return (field.at[:, rows, :, tiles, :].add(contrib), None)
    start = jnp.zeros((RHS, CLAT * N_LAT, SLOTS, N_LON, CLON), jnp.float32)
    adjoint, _ = lax.scan(add_block, start, (masked_c, weights_c, rows_c, tiles_c))
    field = adjoint.reshape(RHS, CLAT * N_LAT, SLOTS, N_LON * CLON)
    kap = pad_once(diffusivity[None, :, None, :])
    for step in range(PASSES):
        field = diffuse(pad_once(field), kap)
    smoothed = field.astype(jnp.bfloat16).reshape(RHS, CLAT * N_LAT, SLOTS, N_LON, CLON)

    def project(carry, items):
        piece, rows, tiles = items
        local = smoothed[:, rows, :, tiles, :]
        values = jnp.einsum('osc,orsc->or', piece.astype(jnp.float32), local.astype(jnp.float32))
        return (carry, values)
    _, values = lax.scan(project, jnp.zeros((), jnp.float32), (masked_c, rows_c, tiles_c))
    return values.reshape(devices * OBS_DEV, RHS)
```

```python
import jax
import jax.numpy as jnp
from jax import lax
from jax.experimental import pallas as pl
from jax.experimental.pallas import tpu as pltpu
from jax.sharding import PartitionSpec as P

SLOTS = 8
CLON = 128
PASSES = 4
RHS = 4
OBS = 512
CAP = 8
DEVICES = 128
LON = 16
ROWS = 256
CHUNKS = 8
DEPTH = ROWS // CHUNKS
TALL = DEPTH + 2 * PASSES
SPAN = SLOTS * CLON
EDGE = SLOTS * 32
WIDE = SPAN + EDGE
TOTAL = DEVICES * CAP
BF = jnp.bfloat16
F32 = jnp.float32
VMEM_LIMIT = 48 * 1024 * 1024


def iota(shape, dim):
    return lax.broadcasted_iota(jnp.int32, shape, dim)


def pick(cond):
    return jnp.where(cond, 1.0, 0.0).astype(BF)


def mm(a, b, dims=((1,), (0,))):
    return lax.dot_general(a, b, (dims, ((), ())), preferred_element_type=F32)


NT = ((1,), (1,))
TN = ((0,), (0,))


def thirds(x):
    hi = x.astype(BF)
    rest = x - hi.astype(F32)
    mid = rest.astype(BF)
    return hi, mid, (rest - mid.astype(F32)).astype(BF)


def params(**kw):
    return pltpu.CompilerParams(vmem_limit_bytes=VMEM_LIMIT, **kw)


def pack_kernel(prints, weights, target, block, slot, out, rank_out, masked, meta):
    t = target[...]
    hit = pick(iota((DEVICES, OBS), 0) == t)
    before = pick(iota((OBS, OBS), 0) < iota((OBS, OBS), 1))
    earlier = mm(hit, before)
    rank = jnp.sum(hit.astype(F32) * earlier, axis=0, keepdims=True)
    rank_out[...] = jnp.broadcast_to(rank, (8, OBS))
    place = t * CAP + rank.astype(jnp.int32)
    blk = block[...]
    meta[...] = jnp.zeros_like(meta)
    meta[0:RHS, :] = weights[...].astype(F32)
    meta[4:5, :] = ((blk % DEPTH) * CHUNKS + blk // DEPTH).astype(F32)
    meta[5:6, :] = slot[...].astype(F32)
    facts = meta[...].astype(BF)
    slots = mm(facts, pick(iota((8, 128), 0) == 5), TN).astype(BF)
    for s in range(SLOTS):
        live = slots >= jnp.asarray(s, BF)
        piece = prints[:, s * CLON:(s + 1) * CLON]
        masked[:, s * CLON:(s + 1) * CLON] = jnp.where(live, piece, jnp.zeros_like(piece))
    where = pick(iota((TOTAL, OBS), 0) == place)
    out[:, :SPAN] = mm(where, masked[...]).astype(BF)
    col, lane = iota((SPAN, 128), 0), iota((SPAN, 128), 1)
    east = (lane < 32) & (col == (lane // 4) * CLON + (CLON - 4) + lane % 4)
    west = (lane >= 32) & (lane < 64) & (col == (lane // 4 - 8) * CLON + lane % 4)
    extra = mm(masked[...], pick(east | west))
    col, lane = iota((8, 128), 0), iota((8, 128), 1)
    spot = lane - 64
    extra = extra + mm(facts, pick((spot >= 0) & (spot < 15) & (spot % 5 == col)), TN)
    moved = mm(where, extra.astype(BF)).reshape(DEVICES // LON, LON * CAP, 128)
    up = jnp.concatenate([moved[:, -CAP:], moved[:, :-CAP]], axis=1)
    down = jnp.concatenate([moved[:, CAP:], moved[:, :CAP]], axis=1)
    lane = iota((1, 1, 128), 2)
    from_west = (lane < 32) | ((lane >= 69) & (lane < 74))
    from_east = ((lane >= 32) & (lane < 64)) | ((lane >= 74) & (lane < 79))
    tail = jnp.where(from_west, up, jnp.where(from_east, down, moved))
    out[:, SPAN:] = tail.reshape(TOTAL, 128).astype(BF)


def pack(prints, weights, target, block, slot):
    return pl.pallas_call(
        pack_kernel,
        out_shape=(
            jax.ShapeDtypeStruct((TOTAL, SPAN + 128), BF),
            jax.ShapeDtypeStruct((8, OBS), F32),
        ),
        scratch_shapes=[pltpu.VMEM((OBS, SPAN), BF), pltpu.VMEM((8, OBS), F32)],
        compiler_params=params(),
        cost_estimate=pl.CostEstimate(flops=2 * TOTAL * OBS * SPAN, bytes_accessed=3 << 20, transcendentals=0),
        name="pack",
    )(prints, weights, target, block, slot)


def faces_kernel(own, top, bottom, left, right, out, tall, strip):
    tall[0:8, :] = jnp.zeros((8, CLON), F32)
    tall[4:8, :] = top[...]
    tall[8:8 + ROWS, :] = own[...]
    tall[8 + ROWS:12 + ROWS, :] = bottom[...]
    tall[12 + ROWS:16 + ROWS, :] = jnp.zeros((4, CLON), F32)
    whole = tall[4:12 + ROWS, :]
    src, lane = iota((CLON, 128), 0), iota((CLON, 128), 1) % 32
    inner = ((lane >= 4) & (lane < 12) & (src == lane - 4)) | ((lane >= 16) & (lane < 24) & (src == CLON - 8 + lane - 16))
    src, lane = iota((4, 128), 0), iota((4, 128), 1) % 32
    one = lambda c: jnp.where(c, 1.0, 0.0)
    high = lax.Precision.HIGHEST
    strip[0:ROWS + 8, :] = (
        jnp.dot(whole, one(inner), precision=high, preferred_element_type=F32)
        + jnp.dot(left[...], one((lane < 4) & (src == lane)), precision=high, preferred_element_type=F32)
        + jnp.dot(right[...], one((lane >= 24) & (lane < 28) & (src == lane - 24)), precision=high, preferred_element_type=F32)
    )
    for kind, (ref, base) in enumerate(((tall, 4), (strip, 0))):
        def level(e):
            return ref[pl.ds(base + e, CHUNKS, stride=DEPTH), :]

        for e in range(TALL):
            here = level(e)
            north = jnp.sqrt(here * level(e + 1)) if e + 1 < TALL else jnp.zeros_like(here)
            south = jnp.sqrt(here * level(e - 1)) if e else jnp.zeros_like(here)
            east = jnp.sqrt(here * pltpu.roll(here, 127, 1))
            west = pltpu.roll(east, 1, 1)
            rows = slice(e * CHUNKS, (e + 1) * CHUNKS)
            out[kind, 0, rows, :] = 1.0 - ((north + south) + (east + west))
            out[kind, 1, rows, :] = north
            out[kind, 2, rows, :] = east
            out[kind, 3, rows, :] = west


def faces(own, top, bottom, left, right):
    return pl.pallas_call(
        faces_kernel,
        out_shape=jax.ShapeDtypeStruct((2, 4, TALL * CHUNKS, CLON), F32),
        scratch_shapes=[pltpu.VMEM((ROWS + 16, CLON), F32), pltpu.VMEM((ROWS + 8, CLON), F32)],
        compiler_params=params(),
        cost_estimate=pl.CostEstimate(flops=1 << 22, bytes_accessed=2 << 20, transcendentals=1 << 18),
        name="faces",
    )(own, top, bottom, left, right)


def adjoint_kernel(got, field, low, high, facts_out, edges_out, edges_w, edges_e):
    r = pl.program_id(0)

    @pl.when(r == 0)
    def _():
        extra = got[:, SPAN:]
        col, lane = iota((16, 128), 0), iota((16, 128), 1)
        facts_out[...] = mm(pick((lane == 64 + col) & (col < 15)), extra, NT)
        col, lane = iota((SPAN, EDGE), 0), iota((SPAN, EDGE), 1)
        spot, base = lane % 32, (lane // 32) * CLON
        inner = ((spot >= 4) & (spot < 12) & (col == base + spot - 4)) | (
            (spot >= 16) & (spot < 24) & (col == base + (CLON - 8 - 16) + spot)
        )
        edges_out[...] = mm(got[:, :SPAN], pick(inner)).astype(BF)
        col, lane = iota((128, EDGE), 0), iota((128, EDGE), 1)
        spot, base = lane % 32, (lane // 32) * 4
        edges_w[...] = mm(extra, pick((spot < 4) & (col == base + spot))).astype(BF)
        edges_e[...] = mm(extra, pick((spot >= 24) & (spot < 28) & (col == 32 + base + spot - 24))).astype(BF)

    row = iota((ROWS, TOTAL), 0).astype(F32)

    def spread(first):
        w = facts_out[pl.ds(first + r, 1), :]
        b = facts_out[pl.ds(first + RHS, 1), :]
        return jnp.where(row == b, w, 0.0).astype(BF)

    mine = spread(0)
    field[0, :, :SPAN] = mm(mine, got[:, :SPAN])
    field[0, :, SPAN:] = mm(mine, edges_out[...]) + (mm(spread(5), edges_w[...]) + mm(spread(10), edges_e[...]))
    for e in range(PASSES):
        low[0, e:e + 1, :] = field[0, e * CHUNKS:e * CHUNKS + 1, :]
        last = (DEPTH - PASSES + e + 1) * CHUNKS - 1
        high[0, e:e + 1, :] = field[0, last:last + 1, :]


def adjoint(got):
    whole = lambda shape: pl.BlockSpec(shape, lambda r: (0,) * len(shape))
    return pl.pallas_call(
        adjoint_kernel,
        grid=(RHS,),
        in_specs=[whole((TOTAL, SPAN + 128))],
        out_specs=(
            pl.BlockSpec((1, ROWS, WIDE), lambda r: (r, 0, 0)),
            pl.BlockSpec((1, PASSES, WIDE), lambda r: (r, 0, 0)),
            pl.BlockSpec((1, PASSES, WIDE), lambda r: (r, 0, 0)),
            whole((16, TOTAL)),
            whole((TOTAL, EDGE)),
        ),
        out_shape=(
            jax.ShapeDtypeStruct((RHS, ROWS, WIDE), F32),
            jax.ShapeDtypeStruct((RHS, PASSES, WIDE), F32),
            jax.ShapeDtypeStruct((RHS, PASSES, WIDE), F32),
            jax.ShapeDtypeStruct((16, TOTAL), F32),
            jax.ShapeDtypeStruct((TOTAL, EDGE), BF),
        ),
        scratch_shapes=[pltpu.VMEM((TOTAL, EDGE), BF), pltpu.VMEM((TOTAL, EDGE), BF)],
        compiler_params=params(),
        cost_estimate=pl.CostEstimate(flops=4 << 30, bytes_accessed=8 << 20, transcendentals=0),
        name="adjoint",
    )(got)


def project_kernel(field, south, north, coef, got, edges, facts, out, ends, one, two, smooth, values):
    r = pl.program_id(0)
    tiles = WIDE // 128
    kinds = [0] * SLOTS + [1] * (tiles - SLOTS)
    side = 6 * CHUNKS

    sub = iota((CHUNKS, 1), 0)
    for e in range(PASSES):
        rows = slice((DEPTH - PASSES + e) * CHUNKS, (DEPTH - PASSES + e + 1) * CHUNKS)
        turned = pltpu.roll(field[0, rows, :], 1, 0)
        ends[e * CHUNKS:(e + 1) * CHUNKS, :] = jnp.where(sub == 0, south[0, e:e + 1, :], turned)
        turned = pltpu.roll(field[0, e * CHUNKS:(e + 1) * CHUNKS, :], CHUNKS - 1, 0)
        at = side + (2 + e) * CHUNKS
        ends[at:at + CHUNKS, :] = jnp.where(sub == CHUNKS - 1, north[0, e:e + 1, :], turned)
    ends[PASSES * CHUNKS:side, :] = field[0, :2 * CHUNKS, :]
    ends[side:side + 2 * CHUNKS, :] = field[0, (DEPTH - 2) * CHUNKS:, :]

    def level(load, e):
        at = pl.multiple_of(e * CHUNKS, CHUNKS)
        before = pl.multiple_of((e - 1) * CHUNKS, CHUNKS)
        c = [
            (coef[k, 0, pl.ds(at, CHUNKS), :], coef[k, 1, pl.ds(at, CHUNKS), :], coef[k, 1, pl.ds(before, CHUNKS), :],
             coef[k, 2, pl.ds(at, CHUNKS), :], coef[k, 3, pl.ds(at, CHUNKS), :])
            for k in range(2)
        ]
        result = []
        for tile in range(tiles):
            mid, nor, sou, eas, wes = c[kinds[tile]]
            cols = slice(tile * 128, (tile + 1) * 128)
            v = load(e, cols)
            near = nor * load(e + 1, cols) + sou * load(e - 1, cols)
            near = near + (eas * pltpu.roll(v, 127, 1) + wes * pltpu.roll(v, 1, 1))
            result.append(mid * v + near)
        return result

    def loader(ref, shift, lead=()):
        def load(e, cols):
            at = (e + shift) * CHUNKS
            if not isinstance(at, int):
                at = pl.multiple_of(at, CHUNKS)
            return ref[lead + (pl.ds(at, CHUNKS), cols)]

        return load

    def sweep(load, target, first, last):
        def step(e, _):
            at = pl.multiple_of(e * CHUNKS, CHUNKS)
            for tile, value in enumerate(level(load, e)):
                target[pl.ds(at, CHUNKS), tile * 128:(tile + 1) * 128] = value
            return 0

        lax.fori_loop(first, last, step, 0, unroll=2)

    sweep(loader(ends, 0), one, 1, 5)
    sweep(loader(field, -PASSES, (0,)), one, 5, TALL - 5)
    sweep(loader(ends, -28), one, TALL - 5, TALL - 1)
    sweep(loader(one, 0), two, 2, TALL - 2)
    sweep(loader(two, 0), one, 3, TALL - 3)

    lane = iota((1, 128), 1)
    keep = [(lane >= PASSES) & (lane < CLON - PASSES), (lane % 16 >= PASSES) & (lane % 16 < 2 * PASSES)]

    def final(pair, _):
        e = PASSES + 2 * pair
        first, second = level(loader(one, 0), e), level(loader(one, 0), e + 1)
        at = pl.multiple_of(pair * 2 * CHUNKS, 2 * CHUNKS)
        for tile in range(tiles):
            both = jnp.concatenate([first[tile], second[tile]], axis=0)
            both = jnp.where(keep[kinds[tile]], both, 0.0).astype(BF)
            smooth[pl.ds(at, 2 * CHUNKS), tile * 128:(tile + 1) * 128] = both
        return 0

    lax.fori_loop(0, DEPTH // 2, final, 0)
    shares = mm(smooth[:, :SPAN], got[:, :SPAN], NT) + mm(smooth[:, SPAN:], edges[...], NT)
    chosen = iota((ROWS, TOTAL), 0).astype(F32) == facts[RHS:RHS + 1, :]
    values[pl.ds(r, 1), :] = jnp.sum(jnp.where(chosen, shares, 0.0), axis=0, keepdims=True)

    @pl.when(r == RHS - 1)
    def _():
        total = jnp.zeros((DEVICES, 128), F32)
        turn = iota((128, TOTAL), 0)
        mine = (iota((128, TOTAL), 1) % CAP == turn // RHS)
        owner = pick(iota((DEVICES, TOTAL), 1) // CAP == iota((DEVICES, TOTAL), 0))
        fan = pick(iota((128, RHS), 0) % RHS == iota((128, RHS), 1))
        for part in thirds(values[0:RHS, :]):
            many = jnp.where(mine, mm(fan, part), 0.0).astype(BF)
            total = total + mm(owner, many, NT)
        out[...] = total


def project(field, south, north, coef, got, edges, facts):
    whole = lambda shape: pl.BlockSpec(shape, lambda r: (0,) * len(shape))
    return pl.pallas_call(
        project_kernel,
        grid=(RHS,),
        in_specs=[
            pl.BlockSpec((1, ROWS, WIDE), lambda r: (r, 0, 0)),
            pl.BlockSpec((1, PASSES, WIDE), lambda r: (r, 0, 0)),
            pl.BlockSpec((1, PASSES, WIDE), lambda r: (r, 0, 0)),
            whole((2, 4, TALL * CHUNKS, CLON)),
            whole((TOTAL, SPAN + 128)),
            whole((TOTAL, EDGE)),
            whole((16, TOTAL)),
        ],
        out_specs=whole((DEVICES, 128)),
        out_shape=jax.ShapeDtypeStruct((DEVICES, 128), F32),
        scratch_shapes=[
            pltpu.VMEM((12 * CHUNKS, WIDE), F32),
            pltpu.VMEM((TALL * CHUNKS, WIDE), F32),
            pltpu.VMEM((TALL * CHUNKS, WIDE), F32),
            pltpu.VMEM((ROWS, WIDE), BF),
            pltpu.VMEM((8, TOTAL), F32),
        ],
        compiler_params=params(),
        cost_estimate=pl.CostEstimate(flops=4 << 30, bytes_accessed=10 << 20, transcendentals=0),
        name="project",
    )(field, south, north, coef, got, edges, facts)


def unpack_kernel(values, target, rank, out):
    hit = pick(iota((DEVICES, OBS), 0) == target[...])
    total = jnp.zeros((CAP * RHS, OBS), F32)
    for part in thirds(values[:, :CAP * RHS]):
        total = total + mm(part, hit, TN)
    total = jnp.where((iota((CAP * RHS, OBS), 0) // RHS).astype(F32) == rank[0:1, :], total, 0.0)
    pair = (total[0:8] + total[8:16]) + (total[16:24] + total[24:32])
    out[...] = pair[0:RHS] + pair[RHS:]


def unpack(values, target, rank):
    return pl.pallas_call(
        unpack_kernel,
        out_shape=jax.ShapeDtypeStruct((RHS, OBS), F32),
        compiler_params=params(),
        name="unpack",
    )(values, target, rank)


def shift(x, axis, step, closed):
    count = lax.axis_size(axis)
    pairs = [(i, (i + step) % count) for i in range(count) if closed or 0 <= i + step < count]
    return lax.ppermute(x, axis, pairs)


def body(footprints, dual_weights, target_device, target_block, obs_slot, diffusivity):
    target = target_device.reshape(1, OBS)
    packed, rank = pack(footprints, dual_weights.T, target, target_block.reshape(1, OBS), obs_slot.reshape(1, OBS))
    top = shift(diffusivity[ROWS - PASSES:], "lat", 1, False)
    bottom = shift(diffusivity[:PASSES], "lat", -1, False)
    tall = jnp.concatenate([top, diffusivity, bottom], axis=0)
    left = shift(tall[:, CLON - PASSES:], "lon", 1, True)
    right = shift(tall[:, :PASSES], "lon", -1, True)
    coef = faces(diffusivity, top, bottom, left, right)
    got = lax.all_to_all(packed, ("lat", "lon"), split_axis=0, concat_axis=0, tiled=True)
    field, low, high, facts, edges = adjoint(got)
    south = shift(high, "lat", 1, False)
    north = shift(low, "lat", -1, False)
    values = project(field, south, north, coef, got, edges, facts)
    returned = lax.all_to_all(values, ("lat", "lon"), split_axis=0, concat_axis=0, tiled=True)
    return unpack(returned, target, rank).T


def solution(mesh):
    placed = (
        P(("lat", "lon"), None),
        P(("lat", "lon"), None),
        P(("lat", "lon"), None),
        P(("lat", "lon")),
        P(("lat", "lon")),
        P("lat", "lon"),
    )
    return jax.shard_map(
        body, mesh=mesh, in_specs=placed, out_specs=P(("lat", "lon"), None), check_vma=False
    )
```

```python
import jax
import jax.numpy as jnp
from jax import lax
from jax.experimental import pallas as pl
from jax.experimental.pallas import tpu as pltpu
from jax.sharding import PartitionSpec as P

SLOTS = 8
CLON = 128
PASSES = 4
RHS = 4
OBS = 512
CAP = 8
DEVICES = 128
LON = 16
ROWS = 256
CHUNKS = 8
DEPTH = ROWS // CHUNKS
TALL = DEPTH + 2 * PASSES
RUN = 9
SPAN = SLOTS * CLON
WIDE = RUN * 128
EAST = CLON + PASSES
TOTAL = DEVICES * CAP
BF = jnp.bfloat16
F32 = jnp.float32
NT = ((1,), (1,))
TN = ((0,), (0,))


def iota(shape, dim):
    return lax.broadcasted_iota(jnp.int32, shape, dim)


def pick(cond):
    return jnp.where(cond, 1.0, 0.0).astype(BF)


def mm(a, b, dims=((1,), (0,))):
    return lax.dot_general(a, b, (dims, ((), ())), preferred_element_type=F32)


def thirds(x):
    hi = x.astype(BF)
    rest = x - hi.astype(F32)
    mid = rest.astype(BF)
    return hi, mid, (rest - mid.astype(F32)).astype(BF)


def params(mib):
    return pltpu.CompilerParams(vmem_limit_bytes=mib * 1024 * 1024)


def cost(flops, size):
    return pl.CostEstimate(flops=flops, bytes_accessed=size, transcendentals=0)


def lanes(shape, dim):
    lane = iota(shape, dim)
    q, k, s = lane // 128, lane % 128 // 8, lane % 8
    return k * RUN + q, s, q, k


def rolled(x, step):
    return pltpu.roll(x, step % 128, 1)


def pack_kernel(prints_hbm, weights_hbm, target_hbm, block_hbm, slot_hbm, out, rank_out,
                prints, weights, target, block, slot, masked, meta, sems):
    pairs = ((target_hbm, target), (weights_hbm, weights), (block_hbm, block), (slot_hbm, slot), (prints_hbm, prints))
    copies = [pltpu.make_async_copy(a, b, sems.at[i]) for i, (a, b) in enumerate(pairs)]
    for copy in copies:
        copy.start()
    for copy in copies[:4]:
        copy.wait()
    t = target[...]
    hit = pick(iota((DEVICES, OBS), 0) == t)
    before = pick(iota((OBS, OBS), 0) < iota((OBS, OBS), 1))
    earlier = mm(hit, before)
    rank = jnp.sum(hit.astype(F32) * earlier, axis=0, keepdims=True)
    rank_out[...] = jnp.broadcast_to(rank, (8, OBS))
    place = t * CAP + rank.astype(jnp.int32)
    blk = block[...]
    meta[...] = jnp.zeros_like(meta)
    meta[0:RHS, :] = weights[...].astype(F32)
    meta[4:5, :] = ((blk % DEPTH) * CHUNKS + blk // DEPTH).astype(F32)
    meta[5:6, :] = slot[...].astype(F32)
    facts = meta[...].astype(BF)
    slots = mm(facts, pick(iota((8, 128), 0) == 5), TN).astype(BF)
    where = pick(iota((TOTAL, OBS), 0) == place)
    copies[4].wait()
    for s in range(SLOTS):
        live = slots >= jnp.asarray(s, BF)
        piece = prints[:, s * CLON:(s + 1) * CLON]
        masked[:, s * CLON:(s + 1) * CLON] = jnp.where(live, piece, jnp.zeros_like(piece))
    e, s, q, k = lanes((1, WIDE), 1)
    base = s * CLON + e
    source = jnp.where(e < PASSES, base + CLON - PASSES, jnp.where(e < EAST, base - PASSES, base - EAST))
    source = jnp.where(e < EAST + PASSES, source, -1)
    spread = pick(iota((SPAN, WIDE), 0) == source)
    fact = jnp.where((k == 15) & (q >= 1) & (q <= 3) & (s < 5), s, -1)
    wide = mm(masked[...], spread) + mm(facts, pick(iota((8, WIDE), 0) == fact), TN)
    moved = mm(where, wide.astype(BF)).reshape(DEVICES // LON, LON * CAP, WIDE)
    up = jnp.concatenate([moved[:, -CAP:], moved[:, :-CAP]], axis=1)
    down = jnp.concatenate([moved[:, CAP:], moved[:, :CAP]], axis=1)
    e, s, q, k = lanes((1, 1, WIDE), 2)
    from_west = (e < PASSES) | ((k == 15) & (q == 2))
    from_east = ((e >= EAST) & (e < EAST + PASSES)) | ((k == 15) & (q == 3))
    out[...] = jnp.where(from_west, up, jnp.where(from_east, down, moved)).reshape(TOTAL, WIDE).astype(BF)


def pack(prints, weights, target, block, slot):
    return pl.pallas_call(
        pack_kernel,
        in_specs=[pl.BlockSpec(memory_space=pltpu.HBM)] * 5,
        out_shape=(
            jax.ShapeDtypeStruct((TOTAL, WIDE), BF),
            jax.ShapeDtypeStruct((8, OBS), F32),
        ),
        scratch_shapes=[
            pltpu.VMEM((OBS, SPAN), BF),
            pltpu.VMEM((RHS, OBS), BF),
            pltpu.VMEM((1, OBS), jnp.int32),
            pltpu.VMEM((1, OBS), jnp.int32),
            pltpu.VMEM((1, OBS), jnp.int32),
            pltpu.VMEM((OBS, SPAN), BF),
            pltpu.VMEM((8, OBS), F32),
            pltpu.SemaphoreType.DMA((5,)),
        ],
        compiler_params=params(32),
        cost_estimate=cost(2 * TOTAL * OBS * SPAN, 3 << 20),
        name="pack",
    )(prints, weights, target, block, slot)


def faces_kernel(own, top, bottom, left, right, out, tall, wide):
    tall[0:4, :] = top[...]
    tall[4:4 + ROWS, :] = own[...]
    tall[4 + ROWS:8 + ROWS, :] = bottom[...]
    e, _, _, _ = lanes((1, WIDE), 1)

    def place(x, first, count):
        one = jnp.where((iota((count, WIDE), 0) == e - first) & (e >= first) & (e < first + count), 1.0, 0.0)
        return jnp.dot(x, one, precision=lax.Precision.HIGHEST, preferred_element_type=F32)

    flat = place(tall[...], PASSES, CLON) + (place(left[...], 0, PASSES) + place(right[...], EAST, PASSES))
    for q in range(RUN):
        wide[q] = flat[:, q * 128:(q + 1) * 128]

    def level(e):
        return [wide[q, pl.ds(e, CHUNKS, stride=DEPTH), :] for q in range(RUN)]

    none = [jnp.zeros((CHUNKS, 128), F32)] * RUN
    here, south = level(0), none
    for e in range(TALL):
        after = level(e + 1) if e + 1 < TALL else none
        north = [jnp.sqrt(x * y) for x, y in zip(here, after)]
        ahead = here[1:] + [rolled(here[0], -SLOTS)]
        east = [jnp.sqrt(x * y) for x, y in zip(here, ahead)]
        west = [rolled(east[-1], SLOTS)] + east[:-1]
        rows = slice(e * CHUNKS, (e + 1) * CHUNKS)
        for q in range(RUN):
            cols = slice(q * 128, (q + 1) * 128)
            out[0, rows, cols] = 1.0 - ((north[q] + south[q]) + (east[q] + west[q]))
            out[1, rows, cols] = north[q]
            out[2, rows, cols] = east[q]
        here, south = after, north


def faces(own, top, bottom, left, right):
    return pl.pallas_call(
        faces_kernel,
        out_shape=jax.ShapeDtypeStruct((3, TALL * CHUNKS, WIDE), F32),
        scratch_shapes=[pltpu.VMEM((ROWS + 8, CLON), F32), pltpu.VMEM((RUN, ROWS + 8, 128), F32)],
        compiler_params=params(20),
        cost_estimate=cost(1 << 30, 6 << 20),
        name="faces",
    )(own, top, bottom, left, right)


def adjoint_kernel(got, coef, field, low, high, facts_out, own, west, east):
    column, fact = iota((16, 128), 0), iota((16, 128), 1) - 120
    facts = mm(pick((fact == column) & (column < 5)), got[:, 128:256], NT)
    facts = facts + mm(pick((fact == column - 5) & (column >= 5) & (column < 10)), got[:, 256:384], NT)
    facts = facts + mm(pick((fact == column - 10) & (column >= 10) & (column < 15)), got[:, 384:512], NT)
    facts_out[...] = facts
    for q in range(RUN):
        piece = got[:, q * 128:(q + 1) * 128]
        e = (iota((1, 128), 1) // 8) * RUN + q
        ones = lambda cond: jnp.broadcast_to(pick(cond), piece.shape)
        own[:, q * 128:(q + 1) * 128] = piece * ones((e >= PASSES) & (e < EAST))
        if q < PASSES:
            west[:, q * 128:(q + 1) * 128] = piece * ones(e < PASSES)
        if q in EASTERN:
            at = EASTERN.index(q) * 128
            east[:, at:at + 128] = piece * ones((e >= EAST) & (e < EAST + PASSES))
    row = iota((ROWS, TOTAL), 0).astype(F32)

    def spread(first, r):
        return jnp.where(row == facts[first + RHS:first + RHS + 1], facts[first + r:first + r + 1], 0.0).astype(BF)

    for r in range(RHS):
        field[r] = mm(spread(0, r), own[...])
        field[r, :, :PASSES * 128] += mm(spread(5, r), west[...])
        more = mm(spread(10, r), east[...])
        for at, q in enumerate(EASTERN):
            field[r, :, q * 128:(q + 1) * 128] += more[:, at * 128:(at + 1) * 128]
        for e in range(PASSES):
            low[r, e:e + 1, :] = field[r, e * CHUNKS:e * CHUNKS + 1, :]
            last = (DEPTH - PASSES + e + 1) * CHUNKS - 1
            high[r, e:e + 1, :] = field[r, last:last + 1, :]


EASTERN = [(EAST + i) % RUN for i in range(PASSES)]


def adjoint(got, coef):
    return pl.pallas_call(
        adjoint_kernel,
        in_specs=[pl.BlockSpec(memory_space=pltpu.VMEM), pl.BlockSpec(memory_space=pl.ANY)],
        out_shape=(
            jax.ShapeDtypeStruct((RHS, ROWS, WIDE), F32),
            jax.ShapeDtypeStruct((RHS, PASSES, WIDE), F32),
            jax.ShapeDtypeStruct((RHS, PASSES, WIDE), F32),
            jax.ShapeDtypeStruct((16, TOTAL), F32),
        ),
        scratch_shapes=[
            pltpu.VMEM((TOTAL, WIDE), BF),
            pltpu.VMEM((TOTAL, PASSES * 128), BF),
            pltpu.VMEM((TOTAL, PASSES * 128), BF),
        ],
        compiler_params=params(28),
        cost_estimate=cost(5 << 30, 8 << 20),
        name="adjoint",
    )(got, coef)


def project_kernel(field, south, north, coef, got, facts, out, ends, one, two, smooth, values):
    side = 6 * CHUNKS
    sub = iota((CHUNKS, 1), 0)
    for r in range(RHS):
        for e in range(PASSES):
            rows = slice((DEPTH - PASSES + e) * CHUNKS, (DEPTH - PASSES + e + 1) * CHUNKS)
            turned = pltpu.roll(field[r, rows, :], 1, 0)
            ends[r, e * CHUNKS:(e + 1) * CHUNKS, :] = jnp.where(sub == 0, south[r, e:e + 1, :], turned)
            turned = pltpu.roll(field[r, e * CHUNKS:(e + 1) * CHUNKS, :], CHUNKS - 1, 0)
            at = side + (2 + e) * CHUNKS
            ends[r, at:at + CHUNKS, :] = jnp.where(sub == CHUNKS - 1, north[r, e:e + 1, :], turned)
        ends[r, PASSES * CHUNKS:side, :] = field[r, :2 * CHUNKS, :]
        ends[r, side:side + 2 * CHUNKS, :] = field[r, (DEPTH - 2) * CHUNKS:, :]

    def rows_of(e):
        at = e * CHUNKS
        return pl.ds(at if isinstance(at, int) else pl.multiple_of(at, CHUNKS), CHUNKS)

    def level(ref, base, e, store):
        def load(r, at, q):
            return ref[r, rows_of(at + base), q * 128:(q + 1) * 128]

        def face(kind, at, q):
            return coef[kind, rows_of(at), q * 128:(q + 1) * 128]

        for r in range(RHS):
            here = [load(r, e, q) for q in range(RUN)]
            ahead = here[1:] + [rolled(here[0], -SLOTS)]
            behind = [rolled(here[-1], SLOTS)] + here[:-1]
            east = [face(2, e, q) for q in range(RUN)]
            west = [rolled(east[-1], SLOTS)] + east[:-1]
            for q in range(RUN):
                near = face(1, e, q) * load(r, e + 1, q) + face(1, e - 1, q) * load(r, e - 1, q)
                near = near + (east[q] * ahead[q] + west[q] * behind[q])
                store(r, q, face(0, e, q) * here[q] + near)

    def sweep(ref, base, target, first, last):
        def step(e, _):
            def store(r, q, value):
                target[r, rows_of(e), q * 128:(q + 1) * 128] = value

            level(ref, base, e, store)
            return 0

        lax.fori_loop(first, last, step, 0)

    sweep(ends, 0, one, 1, 5)
    sweep(field, -PASSES, one, 5, TALL - 5)
    sweep(ends, -28, one, TALL - 5, TALL - 1)
    sweep(one, 0, two, 2, TALL - 2)
    sweep(two, 0, one, 3, TALL - 3)

    keep = []
    for q in range(RUN):
        e = (iota((1, 128), 1) // 8) * RUN + q
        keep.append((e >= PASSES) & (e < EAST))

    def final(pair, _):
        e = PASSES + 2 * pair
        first = {}
        level(one, 0, e, lambda r, q, value: first.__setitem__((r, q), value))

        def store(r, q, value):
            both = jnp.concatenate([first[r, q], value], axis=0)
            at = pl.ds(pl.multiple_of(pair * 2 * CHUNKS, 2 * CHUNKS), 2 * CHUNKS)
            smooth[r, at, q * 128:(q + 1) * 128] = jnp.where(keep[q], both, 0.0).astype(BF)

        level(one, 0, e + 1, store)
        return 0

    lax.fori_loop(0, DEPTH // 2, final, 0)
    chosen = iota((ROWS, TOTAL), 0).astype(F32) == facts[RHS:RHS + 1, :]
    for r in range(RHS):
        shares = mm(smooth[r], got[...], NT)
        values[r:r + 1, :] = jnp.sum(jnp.where(chosen, shares, 0.0), axis=0, keepdims=True)
    total = jnp.zeros((DEVICES, 128), F32)
    mine = iota((128, TOTAL), 1) % CAP == iota((128, TOTAL), 0) // RHS
    owner = pick(iota((DEVICES, TOTAL), 1) // CAP == iota((DEVICES, TOTAL), 0))
    fan = pick(iota((128, RHS), 0) % RHS == iota((128, RHS), 1))
    for part in thirds(values[0:RHS, :]):
        many = jnp.where(mine, mm(fan, part), 0.0).astype(BF)
        total = total + mm(owner, many, NT)
    out[...] = total


def project(field, south, north, coef, got, facts):
    return pl.pallas_call(
        project_kernel,
        out_shape=jax.ShapeDtypeStruct((DEVICES, 128), F32),
        scratch_shapes=[
            pltpu.VMEM((RHS, 12 * CHUNKS, WIDE), F32),
            pltpu.VMEM((RHS, TALL * CHUNKS, WIDE), F32),
            pltpu.VMEM((RHS, TALL * CHUNKS, WIDE), F32),
            pltpu.VMEM((RHS, ROWS, WIDE), BF),
            pltpu.VMEM((8, TOTAL), F32),
        ],
        compiler_params=params(32),
        cost_estimate=cost(5 << 30, 10 << 20),
        name="project",
    )(field, south, north, coef, got, facts)


def unpack_kernel(values, target, rank, out):
    hit = pick(iota((DEVICES, OBS), 0) == target[...])
    total = jnp.zeros((CAP * RHS, OBS), F32)
    for part in thirds(values[:, :CAP * RHS]):
        total = total + mm(part, hit, TN)
    total = jnp.where((iota((CAP * RHS, OBS), 0) // RHS).astype(F32) == rank[0:1, :], total, 0.0)
    pair = (total[0:8] + total[8:16]) + (total[16:24] + total[24:32])
    out[...] = pair[0:RHS] + pair[RHS:]


def unpack(values, target, rank):
    return pl.pallas_call(
        unpack_kernel,
        out_shape=jax.ShapeDtypeStruct((RHS, OBS), F32),
        compiler_params=params(16),
        name="unpack",
    )(values, target, rank)


def shift(x, axis, step, closed):
    count = lax.axis_size(axis)
    pairs = [(i, (i + step) % count) for i in range(count) if closed or 0 <= i + step < count]
    return lax.ppermute(x, axis, pairs)


def body(footprints, dual_weights, target_device, target_block, obs_slot, diffusivity):
    target = target_device.reshape(1, OBS)
    packed, rank = pack(footprints, dual_weights.T, target, target_block.reshape(1, OBS), obs_slot.reshape(1, OBS))
    top = shift(diffusivity[ROWS - PASSES:], "lat", 1, False)
    bottom = shift(diffusivity[:PASSES], "lat", -1, False)
    tall = jnp.concatenate([top, diffusivity, bottom], axis=0)
    left = shift(tall[:, CLON - PASSES:], "lon", 1, True)
    right = shift(tall[:, :PASSES], "lon", -1, True)
    coef = faces(diffusivity, top, bottom, left, right)
    got = lax.all_to_all(packed, ("lat", "lon"), split_axis=0, concat_axis=0, tiled=True)
    field, low, high, facts = adjoint(got, coef)
    south = shift(high, "lat", 1, False)
    north = shift(low, "lat", -1, False)
    values = project(field, south, north, coef, got, facts)
    returned = lax.all_to_all(values, ("lat", "lon"), split_axis=0, concat_axis=0, tiled=True)
    return unpack(returned, target, rank).T


def solution(mesh):
    placed = (
        P(("lat", "lon"), None),
        P(("lat", "lon"), None),
        P(("lat", "lon"), None),
        P(("lat", "lon")),
        P(("lat", "lon")),
        P("lat", "lon"),
    )
    return jax.shard_map(
        body, mesh=mesh, in_specs=placed, out_specs=P(("lat", "lon"), None), check_vma=False
    )
```

```python
import jax
import jax.numpy as jnp
from jax import lax
from jax.experimental import pallas as pl
from jax.experimental.pallas import tpu as pltpu
from jax.sharding import PartitionSpec as P

SLOTS = 8
CLON = 128
PASSES = 4
RHS = 4
OBS = 512
CAP = 8
DEVICES = 128
LON = 16
ROWS = 256
CHUNKS = 8
DEPTH = ROWS // CHUNKS
TALL = DEPTH + 2 * PASSES
RUN = 9
SPAN = SLOTS * CLON
WIDE = RUN * 128
EAST = CLON + PASSES
TOTAL = DEVICES * CAP
RIM = 2 * PASSES
OUTER = 2 * PASSES * CHUNKS
MIDDLE = ROWS - OUTER
BF = jnp.bfloat16
F32 = jnp.float32
NT = ((1,), (1,))
TN = ((0,), (0,))


def iota(shape, dim):
    return lax.broadcasted_iota(jnp.int32, shape, dim)


def pick(cond):
    return jnp.where(cond, 1.0, 0.0).astype(BF)


def mm(a, b, dims=((1,), (0,))):
    return lax.dot_general(a, b, (dims, ((), ())), preferred_element_type=F32)


def thirds(x):
    hi = x.astype(BF)
    rest = x - hi.astype(F32)
    mid = rest.astype(BF)
    return hi, mid, (rest - mid.astype(F32)).astype(BF)


def params(mib):
    return pltpu.CompilerParams(vmem_limit_bytes=mib * 1024 * 1024)


def cost(flops, size):
    return pl.CostEstimate(flops=flops, bytes_accessed=size, transcendentals=0)


def lanes(shape, dim, first=0):
    lane = iota(shape, dim) + first
    q, k, s = lane // 128, lane % 128 // 8, lane % 8
    return k * RUN + q, s, q, k


def rolled(x, step):
    return pltpu.roll(x, step % 128, 1)


def beside(row):
    return row[1:] + [rolled(row[0], -SLOTS)], [rolled(row[-1], SLOTS)] + row[:-1]


PIECES = [(at, min(256, WIDE - at)) for at in range(0, WIDE, 256)]


def pack_kernel(prints_hbm, weights_hbm, target_hbm, block_hbm, slot_hbm, out_hbm, rank_out,
                prints, weights, target, block, slot, masked, meta, out, sems, out_sems):
    pairs = ((target_hbm, target), (weights_hbm, weights), (block_hbm, block), (slot_hbm, slot), (prints_hbm, prints))
    copies = [pltpu.make_async_copy(a, b, sems.at[i]) for i, (a, b) in enumerate(pairs)]
    for copy in copies:
        copy.start()
    for copy in copies[:4]:
        copy.wait()
    t = target[...]
    hit = pick(iota((DEVICES, OBS), 0) == t)
    before = pick(iota((OBS, OBS), 0) < iota((OBS, OBS), 1))
    earlier = mm(hit, before)
    rank = jnp.sum(hit.astype(F32) * earlier, axis=0, keepdims=True)
    rank_out[...] = jnp.broadcast_to(rank, (8, OBS))
    place = t * CAP + rank.astype(jnp.int32)
    blk = block[...]
    meta[...] = jnp.zeros_like(meta)
    meta[0:RHS, :] = weights[...].astype(F32)
    meta[4:5, :] = ((blk % DEPTH) * CHUNKS + blk // DEPTH).astype(F32)
    meta[5:6, :] = slot[...].astype(F32)
    facts = meta[...].astype(BF)
    slots = mm(facts, pick(iota((8, 128), 0) == 5), TN).astype(BF)
    where = pick(iota((TOTAL, OBS), 0) == place)
    copies[4].wait()
    for s in range(SLOTS):
        live = slots >= jnp.asarray(s, BF)
        piece = prints[:, s * CLON:(s + 1) * CLON]
        masked[:, s * CLON:(s + 1) * CLON] = jnp.where(live, piece, jnp.zeros_like(piece))
    sends = []
    for i, (at, size) in enumerate(PIECES):
        e, s, q, k = lanes((1, size), 1, at)
        base = s * CLON + e
        source = jnp.where(e < PASSES, base + CLON - PASSES, jnp.where(e < EAST, base - PASSES, base - EAST))
        source = jnp.where(e < EAST + PASSES, source, -1)
        spread = pick(iota((SPAN, size), 0) == source)
        fact = jnp.where((k == 15) & (q >= 1) & (q <= 3) & (s < 5), s, -1)
        wide = mm(masked[...], spread) + mm(facts, pick(iota((8, size), 0) == fact), TN)
        moved = mm(where, wide.astype(BF)).reshape(DEVICES // LON, LON * CAP, size)
        up = jnp.concatenate([moved[:, -CAP:], moved[:, :-CAP]], axis=1)
        down = jnp.concatenate([moved[:, CAP:], moved[:, :CAP]], axis=1)
        e, s, q, k = lanes((1, 1, size), 2, at)
        from_west = (e < PASSES) | ((k == 15) & (q == 2))
        from_east = ((e >= EAST) & (e < EAST + PASSES)) | ((k == 15) & (q == 3))
        result = jnp.where(from_west, up, jnp.where(from_east, down, moved))
        out[:, at:at + size] = result.reshape(TOTAL, size).astype(BF)
        sends.append(pltpu.make_async_copy(out.at[:, at:at + size], out_hbm.at[:, at:at + size], out_sems.at[i]))
        sends[-1].start()
    for send in sends:
        send.wait()


def pack(prints, weights, target, block, slot):
    hbm = pl.BlockSpec(memory_space=pltpu.HBM)
    return pl.pallas_call(
        pack_kernel,
        in_specs=[hbm] * 5,
        out_specs=(hbm, pl.BlockSpec(memory_space=pltpu.VMEM)),
        out_shape=(
            jax.ShapeDtypeStruct((TOTAL, WIDE), BF),
            jax.ShapeDtypeStruct((8, OBS), F32),
        ),
        scratch_shapes=[
            pltpu.VMEM((OBS, SPAN), BF),
            pltpu.VMEM((RHS, OBS), BF),
            pltpu.VMEM((1, OBS), jnp.int32),
            pltpu.VMEM((1, OBS), jnp.int32),
            pltpu.VMEM((1, OBS), jnp.int32),
            pltpu.VMEM((OBS, SPAN), BF),
            pltpu.VMEM((8, OBS), F32),
            pltpu.VMEM((TOTAL, WIDE), BF),
            pltpu.SemaphoreType.DMA((5,)),
            pltpu.SemaphoreType.DMA((len(PIECES),)),
        ],
        compiler_params=params(60),
        cost_estimate=cost(2 * TOTAL * OBS * SPAN, 3 << 20),
        name="pack",
    )(prints, weights, target, block, slot)


def faces_kernel(own, left, right, out, rim, wide):
    e, _, _, _ = lanes((1, WIDE), 1)

    def place(x, first, count):
        one = jnp.where((iota((count, WIDE), 0) == e - first) & (e >= first) & (e < first + count), 1.0, 0.0)
        return jnp.dot(x, one, precision=lax.Precision.HIGHEST, preferred_element_type=F32)

    flat = place(own[...], PASSES, CLON) + (place(left[...], 0, PASSES) + place(right[...], EAST, PASSES))
    beyond = jnp.zeros((PASSES, 128), F32)
    for q in range(RUN):
        wide[q, :PASSES, :] = beyond
        wide[q, PASSES:PASSES + ROWS, :] = flat[:, q * 128:(q + 1) * 128]
        wide[q, PASSES + ROWS:, :] = beyond
    for j in range(RIM):
        rim[j, :RHS, :] = jnp.broadcast_to(flat[j:j + 1], (RHS, WIDE))
        rim[j, RHS:, :] = jnp.broadcast_to(flat[ROWS - 1 - j:ROWS - j], (RHS, WIDE))

    def level(e):
        return [wide[q, pl.ds(e, CHUNKS, stride=DEPTH), :] for q in range(RUN)]

    none = [jnp.zeros((CHUNKS, 128), F32)] * RUN
    here, south = level(0), none
    for e in range(TALL):
        after = level(e + 1) if e + 1 < TALL else none
        north = [jnp.sqrt(x * y) for x, y in zip(here, after)]
        ahead, _ = beside(here)
        east = [jnp.sqrt(x * y) for x, y in zip(here, ahead)]
        _, west = beside(east)
        rows = slice(e * CHUNKS, (e + 1) * CHUNKS)
        for q in range(RUN):
            cols = slice(q * 128, (q + 1) * 128)
            out[0, rows, cols] = 1.0 - ((north[q] + south[q]) + (east[q] + west[q]))
            out[1, rows, cols] = north[q]
            out[2, rows, cols] = east[q]
        here, south = after, north


def faces(own, left, right):
    return pl.pallas_call(
        faces_kernel,
        out_shape=(
            jax.ShapeDtypeStruct((3, TALL * CHUNKS, WIDE), F32),
            jax.ShapeDtypeStruct((RIM, 2 * RHS, WIDE), F32),
        ),
        scratch_shapes=[pltpu.VMEM((RUN, ROWS + 8, 128), F32)],
        compiler_params=params(16),
        cost_estimate=cost(1 << 30, 6 << 20),
        name="faces",
    )(own, left, right)


def adjoint_kernel(got, kappa, field, rim, low, high, facts_out, own, west, east):
    column, fact = iota((16, 128), 0), iota((16, 128), 1) - 120
    facts = mm(pick((fact == column) & (column < 5)), got[:, 128:256], NT)
    facts = facts + mm(pick((fact == column - 5) & (column >= 5) & (column < 10)), got[:, 256:384], NT)
    facts = facts + mm(pick((fact == column - 10) & (column >= 10) & (column < 15)), got[:, 384:512], NT)
    facts_out[...] = facts
    for q in range(RUN):
        piece = got[:, q * 128:(q + 1) * 128]
        e = (iota((1, 128), 1) // 8) * RUN + q
        ones = lambda cond: jnp.broadcast_to(pick(cond), piece.shape)
        own[:, q * 128:(q + 1) * 128] = piece * ones((e >= PASSES) & (e < EAST))
        if q < PASSES:
            west[:, q * 128:(q + 1) * 128] = piece * ones(e < PASSES)
        if q in EASTERN:
            at = EASTERN.index(q) * 128
            east[:, at:at + 128] = piece * ones((e >= EAST) & (e < EAST + PASSES))
    row = iota((ROWS, TOTAL), 0).astype(F32)

    def spread(first, r):
        return jnp.where(row == facts[first + RHS:first + RHS + 1], facts[first + r:first + r + 1], 0.0).astype(BF)

    for r in range(RHS):
        field[r] = mm(spread(0, r), own[...])
        field[r, :, :PASSES * 128] += mm(spread(5, r), west[...])
        more = mm(spread(10, r), east[...])
        for at, q in enumerate(EASTERN):
            field[r, :, q * 128:(q + 1) * 128] += more[:, at * 128:(at + 1) * 128]
        for j in range(RIM):
            rim[j, r:r + 1, :] = field[r, j * CHUNKS:j * CHUNKS + 1, :]
            last = (DEPTH - j) * CHUNKS - 1
            rim[j, RHS + r:RHS + r + 1, :] = field[r, last:last + 1, :]
    for j in range(PASSES):
        low[j], high[j] = rim[j, :RHS, :], rim[j, RHS:, :]
        low[PASSES + j], high[PASSES + j] = kappa[j, :RHS, :], kappa[j, RHS:, :]


EASTERN = [(EAST + i) % RUN for i in range(PASSES)]


def adjoint(got, kappa):
    return pl.pallas_call(
        adjoint_kernel,
        out_shape=(
            jax.ShapeDtypeStruct((RHS, ROWS, WIDE), F32),
            jax.ShapeDtypeStruct((RIM, 2 * RHS, WIDE), F32),
            jax.ShapeDtypeStruct((2 * PASSES, RHS, WIDE), F32),
            jax.ShapeDtypeStruct((2 * PASSES, RHS, WIDE), F32),
            jax.ShapeDtypeStruct((16, TOTAL), F32),
        ),
        scratch_shapes=[
            pltpu.VMEM((TOTAL, WIDE), BF),
            pltpu.VMEM((TOTAL, PASSES * 128), BF),
            pltpu.VMEM((TOTAL, PASSES * 128), BF),
        ],
        compiler_params=params(20),
        cost_estimate=cost(5 << 30, 8 << 20),
        name="adjoint",
    )(got, kappa)


def inside(q):
    e = (iota((1, 128), 1) // 8) * RUN + q
    return (e >= PASSES) & (e < EAST)


def diffuse_kernel(field, coef, smooth, outer, ends, one, two):
    side = 6 * CHUNKS
    for r in range(RHS):
        for e in range(PASSES):
            rows = slice((DEPTH - PASSES + e) * CHUNKS, (DEPTH - PASSES + e + 1) * CHUNKS)
            ends[r, e * CHUNKS:(e + 1) * CHUNKS, :] = pltpu.roll(field[r, rows, :], 1, 0)
            at = side + (2 + e) * CHUNKS
            ends[r, at:at + CHUNKS, :] = pltpu.roll(field[r, e * CHUNKS:(e + 1) * CHUNKS, :], CHUNKS - 1, 0)
        ends[r, PASSES * CHUNKS:side, :] = field[r, :2 * CHUNKS, :]
        ends[r, side:side + 2 * CHUNKS, :] = field[r, (DEPTH - 2) * CHUNKS:, :]

    def rows_of(e):
        at = e * CHUNKS
        return pl.ds(at if isinstance(at, int) else pl.multiple_of(at, CHUNKS), CHUNKS)

    def level(ref, base, e, store):
        def load(r, at, q):
            return ref[r, rows_of(at + base), q * 128:(q + 1) * 128]

        def face(kind, at, q):
            return coef[kind, rows_of(at), q * 128:(q + 1) * 128]

        for r in range(RHS):
            here = [load(r, e, q) for q in range(RUN)]
            ahead, behind = beside(here)
            east = [face(2, e, q) for q in range(RUN)]
            _, west = beside(east)
            for q in range(RUN):
                near = face(1, e, q) * load(r, e + 1, q) + face(1, e - 1, q) * load(r, e - 1, q)
                near = near + (east[q] * ahead[q] + west[q] * behind[q])
                store(r, q, face(0, e, q) * here[q] + near)

    def sweep(ref, base, target, first, last, to=0):
        def step(e, _):
            def store(r, q, value):
                target[r, rows_of(e + to), q * 128:(q + 1) * 128] = value

            level(ref, base, e, store)
            return 0

        lax.fori_loop(first, last, step, 0, unroll=2)

    sweep(ends, 0, one, 1, 5)
    sweep(field, -PASSES, one, 5, TALL - 5)
    sweep(ends, -28, one, TALL - 5, TALL - 1)
    sweep(one, 0, two, 2, TALL - 2)
    sweep(two, 0, one, 3, TALL - 3)
    sweep(one, 0, outer, PASSES, 2 * PASSES, -PASSES)
    sweep(one, 0, outer, DEPTH, DEPTH + PASSES, -DEPTH + PASSES)

    def final(pair, _):
        e = 2 * PASSES + 2 * pair
        first = {}
        level(one, 0, e, lambda r, q, value: first.__setitem__((r, q), value))

        def store(r, q, value):
            both = jnp.concatenate([first[r, q], value], axis=0)
            at = pl.ds(pl.multiple_of(pair * 2 * CHUNKS, 2 * CHUNKS), 2 * CHUNKS)
            smooth[r, at, q * 128:(q + 1) * 128] = jnp.where(inside(q), both, 0.0).astype(BF)

        level(one, 0, e + 1, store)
        return 0

    lax.fori_loop(0, MIDDLE // (2 * CHUNKS), final, 0)


def diffuse(field, coef):
    return pl.pallas_call(
        diffuse_kernel,
        out_shape=(
            jax.ShapeDtypeStruct((RHS, MIDDLE, WIDE), BF),
            jax.ShapeDtypeStruct((RHS, OUTER, WIDE), F32),
        ),
        scratch_shapes=[
            pltpu.VMEM((RHS, 12 * CHUNKS, WIDE), F32),
            pltpu.VMEM((RHS, TALL * CHUNKS, WIDE), F32),
            pltpu.VMEM((RHS, TALL * CHUNKS, WIDE), F32),
        ],
        compiler_params=params(24),
        cost_estimate=cost(6 << 30, 8 << 20),
        name="diffuse",
    )(field, coef)


def finish_kernel(smooth, outer, rim, kappa, south, north, got, facts, out, border, values):
    def levels(base, inner):
        rows = []
        for j in range(PASSES):
            rows.append(jnp.concatenate([south[base + PASSES - 1 - j], north[base + PASSES - 1 - j]], axis=0))
        return [[x[:, q * 128:(q + 1) * 128] for q in range(RUN)] for x in rows + [inner[j] for j in range(RIM)]]

    v, k = levels(0, rim), levels(PASSES, kappa)
    count = PASSES + RIM
    across = [[jnp.sqrt(x * y) for x, y in zip(k[j], k[j + 1])] for j in range(count - 1)]
    east = [[jnp.sqrt(x * y) for x, y in zip(k[j], beside(k[j])[0])] for j in range(count - 1)]
    west = [beside(x)[1] for x in east]
    for step in range(1, PASSES + 1):
        new = list(v)
        for j in range(step, count - step):
            ahead, behind = beside(v[j])
            new[j] = []
            for q in range(RUN):
                own = 1.0 - ((across[j][q] + across[j - 1][q]) + (east[j][q] + west[j][q]))
                near = across[j][q] * v[j + 1][q] + across[j - 1][q] * v[j - 1][q]
                new[j].append(own * v[j][q] + (near + (east[j][q] * ahead[q] + west[j][q] * behind[q])))
        v = new
    sub = iota((CHUNKS, 1), 0)
    for r in range(RHS):
        for q in range(RUN):
            cols = slice(q * 128, (q + 1) * 128)
            for pair in range(PASSES):
                both = []
                for b in (2 * pair, 2 * pair + 1):
                    here = outer[r, b * CHUNKS:(b + 1) * CHUNKS, cols]
                    if b < PASSES:
                        here = jnp.where(sub == 0, v[PASSES + b][q][r:r + 1], here)
                    else:
                        j = PASSES + 2 * PASSES - 1 - b
                        here = jnp.where(sub == CHUNKS - 1, v[j][q][RHS + r:RHS + r + 1], here)
                    both.append(here)
                both = jnp.where(inside(q), jnp.concatenate(both, axis=0), 0.0).astype(BF)
                border[r, pair * 2 * CHUNKS:(pair + 1) * 2 * CHUNKS, cols] = both

    side = PASSES * CHUNKS
    for r in range(RHS):
        total = jnp.zeros((1, TOTAL), F32)
        for part, first in ((smooth[r], side), (border[r, :side], 0), (border[r, side:], ROWS - side)):
            shares = mm(part, got[...], NT)
            chosen = (iota(shares.shape, 0) + first).astype(F32) == facts[RHS:RHS + 1, :]
            total = total + jnp.sum(jnp.where(chosen, shares, 0.0), axis=0, keepdims=True)
        values[r:r + 1, :] = total
    total = jnp.zeros((DEVICES, 128), F32)
    mine = iota((128, TOTAL), 1) % CAP == iota((128, TOTAL), 0) // RHS
    owner = pick(iota((DEVICES, TOTAL), 1) // CAP == iota((DEVICES, TOTAL), 0))
    fan = pick(iota((128, RHS), 0) % RHS == iota((128, RHS), 1))
    for part in thirds(values[0:RHS, :]):
        many = jnp.where(mine, mm(fan, part), 0.0).astype(BF)
        total = total + mm(owner, many, NT)
    out[...] = total


def finish(smooth, outer, rim, kappa, south, north, got, facts):
    return pl.pallas_call(
        finish_kernel,
        out_shape=jax.ShapeDtypeStruct((DEVICES, 128), F32),
        scratch_shapes=[
            pltpu.VMEM((RHS, OUTER, WIDE), BF),
            pltpu.VMEM((8, TOTAL), F32),
        ],
        compiler_params=params(24),
        cost_estimate=cost(3 << 30, 10 << 20),
        name="finish",
    )(smooth, outer, rim, kappa, south, north, got, facts)


def unpack_kernel(values, target, rank, out):
    hit = pick(iota((DEVICES, OBS), 0) == target[...])
    total = jnp.zeros((CAP * RHS, OBS), F32)
    for part in thirds(values[:, :CAP * RHS]):
        total = total + mm(part, hit, TN)
    total = jnp.where((iota((CAP * RHS, OBS), 0) // RHS).astype(F32) == rank[0:1, :], total, 0.0)
    pair = (total[0:8] + total[8:16]) + (total[16:24] + total[24:32])
    out[...] = pair[0:RHS] + pair[RHS:]


def unpack(values, target, rank):
    return pl.pallas_call(
        unpack_kernel,
        out_shape=jax.ShapeDtypeStruct((RHS, OBS), F32),
        compiler_params=params(16),
        name="unpack",
    )(values, target, rank)


def shift(x, axis, step, closed):
    count = lax.axis_size(axis)
    pairs = [(i, (i + step) % count) for i in range(count) if closed or 0 <= i + step < count]
    return lax.ppermute(x, axis, pairs)


def body(footprints, dual_weights, target_device, target_block, obs_slot, diffusivity):
    target = target_device.reshape(1, OBS)
    packed, rank = pack(footprints, dual_weights.T, target, target_block.reshape(1, OBS), obs_slot.reshape(1, OBS))
    left = shift(diffusivity[:, CLON - PASSES:], "lon", 1, True)
    right = shift(diffusivity[:, :PASSES], "lon", -1, True)
    packed, left, right = lax.optimization_barrier((packed, left, right))
    coef, kappa = faces(diffusivity, left, right)
    got = lax.all_to_all(packed, ("lat", "lon"), split_axis=0, concat_axis=0, tiled=True)
    field, rim, low, high, facts = adjoint(got, kappa)
    south = shift(high, "lat", 1, False)
    north = shift(low, "lat", -1, False)
    smooth, outer = diffuse(field, coef)
    values = finish(smooth, outer, rim, kappa, south, north, got, facts)
    returned = lax.all_to_all(values, ("lat", "lon"), split_axis=0, concat_axis=0, tiled=True)
    return unpack(returned, target, rank).T


def solution(mesh):
    placed = (
        P(("lat", "lon"), None),
        P(("lat", "lon"), None),
        P(("lat", "lon"), None),
        P(("lat", "lon")),
        P(("lat", "lon")),
        P("lat", "lon"),
    )
    return jax.shard_map(
        body, mesh=mesh, in_specs=placed, out_specs=P(("lat", "lon"), None), check_vma=False
    )
```

```python
import jax
import jax.numpy as jnp
from jax import lax
from jax.experimental import pallas as pl
from jax.experimental.pallas import tpu as pltpu
from jax.sharding import PartitionSpec as P

SLOTS = 8
CLON = 128
PASSES = 4
RHS = 4
OBS = 512
CAP = 8
DEVICES = 128
LON = 16
ROWS = 256
CHUNKS = 8
DEPTH = ROWS // CHUNKS
TALL = DEPTH + 2 * PASSES
RUN = 9
SPAN = SLOTS * CLON
WIDE = RUN * 128
EAST = CLON + PASSES
TOTAL = DEVICES * CAP
RIM = 2 * PASSES
OUTER = 2 * PASSES * CHUNKS
MIDDLE = ROWS - OUTER
BF = jnp.bfloat16
F32 = jnp.float32
NT = ((1,), (1,))
TN = ((0,), (0,))


def iota(shape, dim):
    return lax.broadcasted_iota(jnp.int32, shape, dim)


def pick(cond):
    return jnp.where(cond, 1.0, 0.0).astype(BF)


def mm(a, b, dims=((1,), (0,))):
    return lax.dot_general(a, b, (dims, ((), ())), preferred_element_type=F32)


def thirds(x):
    hi = x.astype(BF)
    rest = x - hi.astype(F32)
    mid = rest.astype(BF)
    return hi, mid, (rest - mid.astype(F32)).astype(BF)


def params(mib):
    return pltpu.CompilerParams(vmem_limit_bytes=mib * 1024 * 1024)


def cost(flops, size):
    return pl.CostEstimate(flops=flops, bytes_accessed=size, transcendentals=0)


def lanes(shape, dim):
    lane = iota(shape, dim)
    q, k, s = lane // 128, lane % 128 // 8, lane % 8
    return k * RUN + q, s, q, k


def rolled(x, step):
    return pltpu.roll(x, step % 128, 1)


def beside(row):
    return row[1:] + [rolled(row[0], -SLOTS)], [rolled(row[-1], SLOTS)] + row[:-1]


PIECES = 4


def pack_kernel(prints_hbm, weights_hbm, target_hbm, block_hbm, slot_hbm, out_hbm, rank_out,
                prints, weights, target, block, slot, masked, meta, spread, wide, out, sems, out_sems):
    pairs = ((target_hbm, target), (weights_hbm, weights), (block_hbm, block), (slot_hbm, slot), (prints_hbm, prints))
    copies = [pltpu.make_async_copy(a, b, sems.at[i]) for i, (a, b) in enumerate(pairs)]
    for copy in copies:
        copy.start()
    e, s, q, k = lanes((1, WIDE), 1)
    base = s * CLON + e
    source = jnp.where(e < PASSES, base + CLON - PASSES, jnp.where(e < EAST, base - PASSES, base - EAST))
    source = jnp.where(e < EAST + PASSES, source, -1)
    spread[...] = pick(iota((SPAN, WIDE), 0) == source)
    before = pick(iota((OBS, OBS), 0) < iota((OBS, OBS), 1))
    for copy in copies[:4]:
        copy.wait()
    t = target[...]
    hit = pick(iota((DEVICES, OBS), 0) == t)
    earlier = mm(hit, before)
    rank = jnp.sum(hit.astype(F32) * earlier, axis=0, keepdims=True)
    rank_out[...] = jnp.broadcast_to(rank, (8, OBS))
    place = t * CAP + rank.astype(jnp.int32)
    blk = block[...]
    meta[...] = jnp.zeros_like(meta)
    meta[0:RHS, :] = weights[...].astype(F32)
    meta[4:5, :] = ((blk % DEPTH) * CHUNKS + blk // DEPTH).astype(F32)
    meta[5:6, :] = slot[...].astype(F32)
    facts = meta[...].astype(BF)
    slots = mm(facts, pick(iota((8, 128), 0) == 5), TN).astype(BF)
    where = pick(iota((TOTAL, OBS), 0) == place)
    copies[4].wait()
    for s in range(SLOTS):
        live = slots >= jnp.asarray(s, BF)
        piece = prints[:, s * CLON:(s + 1) * CLON]
        masked[:, s * CLON:(s + 1) * CLON] = jnp.where(live, piece, jnp.zeros_like(piece))
    e, s, q, k = lanes((1, WIDE), 1)
    fact = jnp.where((k == 15) & (q >= 1) & (q <= 3) & (s < 5), s, -1)
    wide[...] = (mm(masked[...], spread[...]) + mm(facts, pick(iota((8, WIDE), 0) == fact), TN)).astype(BF)
    e, s, q, k = lanes((1, 1, WIDE), 2)
    from_west = (e < PASSES) | ((k == 15) & (q == 2))
    from_east = ((e >= EAST) & (e < EAST + PASSES)) | ((k == 15) & (q == 3))
    sends = []
    size = TOTAL // PIECES
    for i in range(PIECES):
        rows = slice(i * size, (i + 1) * size)
        moved = mm(where[rows], wide[...]).reshape(size // (LON * CAP), LON * CAP, WIDE)
        up = jnp.concatenate([moved[:, -CAP:], moved[:, :-CAP]], axis=1)
        down = jnp.concatenate([moved[:, CAP:], moved[:, :CAP]], axis=1)
        result = jnp.where(from_west, up, jnp.where(from_east, down, moved))
        out[rows, :] = result.reshape(size, WIDE).astype(BF)
        sends.append(pltpu.make_async_copy(out.at[rows, :], out_hbm.at[rows, :], out_sems.at[i]))
        sends[-1].start()
    for send in sends:
        send.wait()


def pack(prints, weights, target, block, slot):
    hbm = pl.BlockSpec(memory_space=pltpu.HBM)
    return pl.pallas_call(
        pack_kernel,
        in_specs=[hbm] * 5,
        out_specs=(hbm, pl.BlockSpec(memory_space=pltpu.VMEM)),
        out_shape=(
            jax.ShapeDtypeStruct((TOTAL, WIDE), BF),
            jax.ShapeDtypeStruct((8, OBS), F32),
        ),
        scratch_shapes=[
            pltpu.VMEM((OBS, SPAN), BF),
            pltpu.VMEM((RHS, OBS), BF),
            pltpu.VMEM((1, OBS), jnp.int32),
            pltpu.VMEM((1, OBS), jnp.int32),
            pltpu.VMEM((1, OBS), jnp.int32),
            pltpu.VMEM((OBS, SPAN), BF),
            pltpu.VMEM((8, OBS), F32),
            pltpu.VMEM((SPAN, WIDE), BF),
            pltpu.VMEM((OBS, WIDE), BF),
            pltpu.VMEM((TOTAL, WIDE), BF),
            pltpu.SemaphoreType.DMA((5,)),
            pltpu.SemaphoreType.DMA((PIECES,)),
        ],
        compiler_params=params(60),
        cost_estimate=cost(2 * TOTAL * OBS * SPAN, 3 << 20),
        name="pack",
    )(prints, weights, target, block, slot)


def faces_kernel(own, first, second, coef, last, rim, wide):
    e, _, _, _ = lanes((1, WIDE), 1)
    even = lax.axis_index("lon") % 2 == 0

    def place(x, cond, shift):
        one = jnp.where(cond & (iota((CLON, WIDE), 0) == e + shift), 1.0, 0.0)
        return jnp.dot(jnp.sqrt(x), one, precision=lax.Precision.HIGHEST, preferred_element_type=F32)

    left = jnp.where(even, second[...], first[...])
    right = jnp.where(even, first[...], second[...])
    flat = place(own[...], (e >= PASSES) & (e < EAST), -PASSES)
    flat = flat + (place(left, e < PASSES, CLON - PASSES) + place(right, (e >= EAST) & (e < EAST + PASSES), -EAST))
    beyond = jnp.zeros((PASSES, 128), F32)
    for q in range(RUN):
        wide[q, :PASSES, :] = beyond
        wide[q, PASSES:PASSES + ROWS, :] = flat[:, q * 128:(q + 1) * 128]
        wide[q, PASSES + ROWS:, :] = beyond
    for j in range(RIM):
        rim[j, :RHS, :] = jnp.broadcast_to(flat[j:j + 1], (RHS, WIDE))
        rim[j, RHS:, :] = jnp.broadcast_to(flat[ROWS - 1 - j:ROWS - j], (RHS, WIDE))

    def level(e):
        return [wide[q, pl.ds(e, CHUNKS, stride=DEPTH), :] for q in range(RUN)]

    none = [jnp.zeros((CHUNKS, 128), F32)] * RUN
    here, south = level(0), none
    for e in range(TALL):
        north = level(e + 1) if e + 1 < TALL else none
        ahead, behind = beside(here)
        rows = slice(e * CHUNKS, (e + 1) * CHUNKS)
        for q in range(RUN):
            cols = slice(q * 128, (q + 1) * 128)
            mid = 1.0 - here[q] * ((north[q] + south[q]) + (ahead[q] + behind[q]))
            coef[0, rows, cols] = mid
            coef[1, rows, cols] = here[q] * here[q]
            if PASSES <= e < TALL - PASSES:
                inner = slice((e - PASSES) * CHUNKS, (e - PASSES + 1) * CHUNKS)
                some = here[q] > 0.0
                last[0, inner, cols] = jnp.where(some, mid / jnp.where(some, here[q], 1.0), 0.0)
                last[1, inner, cols] = here[q]
        here, south = north, here


def faces(own, first, second):
    return pl.pallas_call(
        faces_kernel,
        out_shape=(
            jax.ShapeDtypeStruct((2, TALL * CHUNKS, WIDE), F32),
            jax.ShapeDtypeStruct((2, ROWS, WIDE), F32),
            jax.ShapeDtypeStruct((RIM, 2 * RHS, WIDE), F32),
        ),
        scratch_shapes=[pltpu.VMEM((RUN, ROWS + 8, 128), F32)],
        compiler_params=params(16),
        cost_estimate=cost(1 << 30, 6 << 20),
        name="faces",
    )(own, first, second)


def adjoint_kernel(got, last, roots, field, rim, inner, outer, facts_out, own, west, east):
    column, fact = iota((16, 128), 0), iota((16, 128), 1) - 120
    facts = mm(pick((fact == column) & (column < 5)), got[:, 128:256], NT)
    facts = facts + mm(pick((fact == column - 5) & (column >= 5) & (column < 10)), got[:, 256:384], NT)
    facts = facts + mm(pick((fact == column - 10) & (column >= 10) & (column < 15)), got[:, 384:512], NT)
    facts_out[...] = facts
    for q in range(RUN):
        piece = got[:, q * 128:(q + 1) * 128]
        e = (iota((1, 128), 1) // 8) * RUN + q
        ones = lambda cond: jnp.broadcast_to(pick(cond), piece.shape)
        own[:, q * 128:(q + 1) * 128] = piece * ones((e >= PASSES) & (e < EAST))
        if q < PASSES:
            west[:, q * 128:(q + 1) * 128] = piece * ones(e < PASSES)
        if q in EASTERN:
            at = EASTERN.index(q) * 128
            east[:, at:at + 128] = piece * ones((e >= EAST) & (e < EAST + PASSES))
    row = iota((ROWS, TOTAL), 0).astype(F32)

    def spread(first, r):
        return jnp.where(row == facts[first + RHS:first + RHS + 1], facts[first + r:first + r + 1], 0.0).astype(BF)

    for r in range(RHS):
        total = mm(spread(0, r), own[...])
        before, after = mm(spread(5, r), west[...]), mm(spread(10, r), east[...])
        for q in range(RUN):
            cols = slice(q * 128, (q + 1) * 128)
            part = total[:, cols]
            if q < PASSES:
                part = part + before[:, cols]
            if q in EASTERN:
                at = EASTERN.index(q) * 128
                part = part + after[:, at:at + 128]
            field[r, :, cols] = part * last[1, :, cols]
        for j in range(RIM):
            rim[j, r:r + 1, :] = field[r, j * CHUNKS:j * CHUNKS + 1, :]
            end = (DEPTH - j) * CHUNKS
            rim[j, RHS + r:RHS + r + 1, :] = field[r, end - 1:end, :]
    even = lax.axis_index("lat") % 2 == 0
    for base, ref in ((0, rim), (PASSES, roots)):
        for j in range(PASSES):
            low, high = ref[j, :RHS, :], ref[j, RHS:, :]
            inner[base + j] = jnp.where(even, high, low)
            outer[base + j] = jnp.where(even, low, high)


EASTERN = [(EAST + i) % RUN for i in range(PASSES)]


def adjoint(got, last, roots):
    return pl.pallas_call(
        adjoint_kernel,
        out_shape=(
            jax.ShapeDtypeStruct((RHS, ROWS, WIDE), F32),
            jax.ShapeDtypeStruct((RIM, 2 * RHS, WIDE), F32),
            jax.ShapeDtypeStruct((2 * PASSES, RHS, WIDE), F32),
            jax.ShapeDtypeStruct((2 * PASSES, RHS, WIDE), F32),
            jax.ShapeDtypeStruct((16, TOTAL), F32),
        ),
        scratch_shapes=[
            pltpu.VMEM((TOTAL, WIDE), BF),
            pltpu.VMEM((TOTAL, PASSES * 128), BF),
            pltpu.VMEM((TOTAL, PASSES * 128), BF),
        ],
        compiler_params=params(20),
        cost_estimate=cost(5 << 30, 8 << 20),
        name="adjoint",
    )(got, last, roots)


def inside(q):
    e = (iota((1, 128), 1) // 8) * RUN + q
    return (e >= PASSES) & (e < EAST)


def diffuse_kernel(field, coef, last, smooth, outer, ends, one, two):
    side = 6 * CHUNKS
    for r in range(RHS):
        for e in range(PASSES):
            rows = slice((DEPTH - PASSES + e) * CHUNKS, (DEPTH - PASSES + e + 1) * CHUNKS)
            ends[r, e * CHUNKS:(e + 1) * CHUNKS, :] = pltpu.roll(field[r, rows, :], 1, 0)
            at = side + (2 + e) * CHUNKS
            ends[r, at:at + CHUNKS, :] = pltpu.roll(field[r, e * CHUNKS:(e + 1) * CHUNKS, :], CHUNKS - 1, 0)
        ends[r, PASSES * CHUNKS:side, :] = field[r, :2 * CHUNKS, :]
        ends[r, side:side + 2 * CHUNKS, :] = field[r, (DEPTH - 2) * CHUNKS:, :]

    def rows_of(e):
        at = e * CHUNKS
        return pl.ds(at if isinstance(at, int) else pl.multiple_of(at, CHUNKS), CHUNKS)

    def two_levels(ref, base, e, factor, lift, store):
        def load(r, at, q):
            return ref[r, rows_of(at + base), q * 128:(q + 1) * 128]

        levels = (e, e + 1)
        turned_west = [[rolled(load(r, at, RUN - 1), SLOTS) for at in levels] for r in range(RHS)]
        turned_east = [[rolled(load(r, at, 0), -SLOTS) for at in levels] for r in range(RHS)]
        behind, here = [[[load(r, at, q) for at in levels] for r in range(RHS)] for q in (0, 1)]
        for q in [*range(1, RUN), 0]:
            mid, near = [[factor[kind, rows_of(at + lift), q * 128:(q + 1) * 128] for at in levels] for kind in (0, 1)]
            if q == 0:
                behind = turned_west
                here, ahead = [[[load(r, at, i) for at in levels] for r in range(RHS)] for i in (0, 1)]
            elif q + 1 < RUN:
                ahead = [[load(r, at, q + 1) for at in levels] for r in range(RHS)]
            else:
                ahead = turned_east
            for r in range(RHS):
                column = [load(r, e - 1, q)] + here[r] + [load(r, e + 2, q)]
                for i in range(2):
                    total = (column[i + 2] + column[i]) + (ahead[r][i] + behind[r][i])
                    store(r, q, i, mid[i] * here[r][i] + near[i] * total)
            behind, here = here, ahead

    def sweep(ref, base, target, first, end, to=0, factor=coef, lift=0):
        def step(pair, _):
            e = first + 2 * pair

            def store(r, q, i, value):
                target[r, rows_of(e + i + to), q * 128:(q + 1) * 128] = value

            two_levels(ref, base, e, factor, lift, store)
            return 0

        lax.fori_loop(0, (end - first) // 2, step, 0, unroll=2)

    sweep(ends, 0, one, 1, 5)
    sweep(field, -PASSES, one, 5, TALL - 5)
    sweep(ends, -28, one, TALL - 5, TALL - 1)
    sweep(one, 0, two, 2, TALL - 2)
    sweep(two, 0, one, 3, TALL - 3)
    sweep(one, 0, outer, PASSES, 2 * PASSES, -PASSES, last, -PASSES)
    sweep(one, 0, outer, DEPTH, DEPTH + PASSES, -DEPTH + PASSES, last, -PASSES)

    def final(pair, _):
        first = {}

        def store(r, q, i, value):
            if i == 0:
                first[r, q] = value
                return
            both = jnp.concatenate([first.pop((r, q)), value], axis=0)
            at = pl.ds(pl.multiple_of(pair * 2 * CHUNKS, 2 * CHUNKS), 2 * CHUNKS)
            smooth[r, at, q * 128:(q + 1) * 128] = jnp.where(inside(q), both, 0.0).astype(BF)

        two_levels(one, 0, 2 * PASSES + 2 * pair, last, -PASSES, store)
        return 0

    lax.fori_loop(0, MIDDLE // (2 * CHUNKS), final, 0, unroll=2)


def diffuse(field, coef, last):
    return pl.pallas_call(
        diffuse_kernel,
        out_shape=(
            jax.ShapeDtypeStruct((RHS, MIDDLE, WIDE), BF),
            jax.ShapeDtypeStruct((RHS, OUTER, WIDE), F32),
        ),
        scratch_shapes=[
            pltpu.VMEM((RHS, 12 * CHUNKS, WIDE), F32),
            pltpu.VMEM((RHS, TALL * CHUNKS, WIDE), F32),
            pltpu.VMEM((RHS, TALL * CHUNKS, WIDE), F32),
        ],
        compiler_params=params(24),
        cost_estimate=cost(6 << 30, 8 << 20),
        name="diffuse",
    )(field, coef, last)


def finish_kernel(smooth, outer, rim, roots, inner, beyond, got, facts, out, border, values):
    even = lax.axis_index("lat") % 2 == 0

    def levels(base, own):
        rows = []
        for j in range(base + PASSES - 1, base - 1, -1):
            south = jnp.where(even, beyond[j], inner[j])
            north = jnp.where(even, inner[j], beyond[j])
            rows.append(jnp.concatenate([south, north], axis=0))
        return [[x[:, q * 128:(q + 1) * 128] for q in range(RUN)] for x in rows + [own[j] for j in range(RIM)]]

    def around(x, j):
        ahead, behind = beside(x[j])
        return [(x[j + 1][q] + x[j - 1][q]) + (ahead[q] + behind[q]) for q in range(RUN)]

    v, root = levels(0, rim), levels(PASSES, roots)
    count = PASSES + RIM
    mid = [None] + [[1.0 - x * y for x, y in zip(root[j], around(root, j))] for j in range(1, count - 1)]
    for step in range(1, PASSES + 1):
        new = list(v)
        for j in range(step, count - step):
            total = around(v, j)
            new[j] = [mid[j][q] * v[j][q] + (root[j][q] * root[j][q]) * total[q] for q in range(RUN)]
        v = new
    for j in range(PASSES, 2 * PASSES):
        some = [x > 0.0 for x in root[j]]
        v[j] = [jnp.where(some[q], v[j][q] / jnp.where(some[q], root[j][q], 1.0), 0.0) for q in range(RUN)]
    sub = iota((CHUNKS, 1), 0)
    for r in range(RHS):
        for q in range(RUN):
            cols = slice(q * 128, (q + 1) * 128)
            for pair in range(PASSES):
                both = []
                for b in (2 * pair, 2 * pair + 1):
                    here = outer[r, b * CHUNKS:(b + 1) * CHUNKS, cols]
                    if b < PASSES:
                        here = jnp.where(sub == 0, v[PASSES + b][q][r:r + 1], here)
                    else:
                        j = PASSES + 2 * PASSES - 1 - b
                        here = jnp.where(sub == CHUNKS - 1, v[j][q][RHS + r:RHS + r + 1], here)
                    both.append(here)
                both = jnp.where(inside(q), jnp.concatenate(both, axis=0), 0.0).astype(BF)
                border[r, pair * 2 * CHUNKS:(pair + 1) * 2 * CHUNKS, cols] = both

    side = PASSES * CHUNKS
    chosen = iota((ROWS, TOTAL), 0).astype(F32) == facts[RHS:RHS + 1, :]
    total = [0.0] * RHS
    for ref, spans in ((smooth, ((side, MIDDLE),)), (border, ((0, side), (ROWS - side, side)))):
        shares = mm(ref[...].reshape(-1, WIDE), got[...], NT)
        at = 0
        for r in range(RHS):
            for first, size in spans:
                part = jnp.where(chosen[first:first + size], shares[at:at + size], 0.0)
                total[r] = total[r] + jnp.sum(part, axis=0, keepdims=True)
                at += size
    for r in range(RHS):
        values[r:r + 1, :] = total[r]
        values[RHS + r:RHS + r + 1, :] = total[r]
    both = values[...]
    turn = iota((2 * RHS, TOTAL), 0) // RHS
    keep = [jnp.where(iota((2 * RHS, TOTAL), 1) % CAP == turn + 2 * i, 1.0, 0.0) for i in range(CAP // 2)]
    many = [part.astype(F32) * k for part in thirds(both) for k in keep]
    owner = pick(iota((DEVICES, TOTAL), 1) // CAP == iota((DEVICES, TOTAL), 0))
    sums = mm(owner, jnp.concatenate(many, axis=0).astype(BF), NT)
    size = CAP * RHS
    out[...] = jnp.zeros_like(out)
    out[:, :size] = (sums[:, :size] + sums[:, size:2 * size]) + sums[:, 2 * size:3 * size]


def finish(smooth, outer, rim, roots, inner, beyond, got, facts):
    return pl.pallas_call(
        finish_kernel,
        out_shape=jax.ShapeDtypeStruct((DEVICES, 128), F32),
        scratch_shapes=[
            pltpu.VMEM((RHS, OUTER, WIDE), BF),
            pltpu.VMEM((8, TOTAL), F32),
        ],
        compiler_params=params(24),
        cost_estimate=cost(3 << 30, 10 << 20),
        name="finish",
    )(smooth, outer, rim, roots, inner, beyond, got, facts)


def unpack_kernel(values, target, rank, out):
    hit = pick(iota((DEVICES, OBS), 0) == target[...])
    total = jnp.zeros((CAP * RHS, OBS), F32)
    for part in thirds(values[:, :CAP * RHS]):
        total = total + mm(part, hit, TN)
    total = jnp.where((iota((CAP * RHS, OBS), 0) // RHS).astype(F32) == rank[0:1, :], total, 0.0)
    pair = (total[0:8] + total[8:16]) + (total[16:24] + total[24:32])
    out[...] = pair[0:RHS] + pair[RHS:]


def unpack(values, target, rank):
    return pl.pallas_call(
        unpack_kernel,
        out_shape=jax.ShapeDtypeStruct((RHS, OBS), F32),
        compiler_params=params(16),
        name="unpack",
    )(values, target, rank)


def swap(x, axis, second, closed):
    count = lax.axis_size(axis)
    pairs = [(i, (i + 1) % count) for i in range(int(second), count, 2) if closed or i + 1 < count]
    return lax.ppermute(x, axis, pairs + [(j, i) for i, j in pairs])


def body(footprints, dual_weights, target_device, target_block, obs_slot, diffusivity):
    target = target_device.reshape(1, OBS)
    packed, rank = pack(footprints, dual_weights.T, target, target_block.reshape(1, OBS), obs_slot.reshape(1, OBS))
    first = swap(diffusivity, "lon", False, True)
    second = swap(diffusivity, "lon", True, True)
    packed, first, second = lax.optimization_barrier((packed, first, second))
    coef, last, roots = faces(diffusivity, first, second)
    got = lax.all_to_all(packed, ("lat", "lon"), split_axis=0, concat_axis=0, tiled=True)
    field, rim, inner, beyond, facts = adjoint(got, last, roots)
    inner = swap(inner, "lat", False, False)
    beyond = swap(beyond, "lat", True, False)
    smooth, outer = diffuse(field, coef, last)
    values = finish(smooth, outer, rim, roots, inner, beyond, got, facts)
    returned = lax.all_to_all(values, ("lat", "lon"), split_axis=0, concat_axis=0, tiled=True)
    return unpack(returned, target, rank).T


def solution(mesh):
    placed = (
        P(("lat", "lon"), None),
        P(("lat", "lon"), None),
        P(("lat", "lon"), None),
        P(("lat", "lon")),
        P(("lat", "lon")),
        P("lat", "lon"),
    )
    return jax.shard_map(
        body, mesh=mesh, in_specs=placed, out_specs=P(("lat", "lon"), None), check_vma=False
    )
```

```python
import jax
import jax.numpy as jnp
from jax import lax
from jax.experimental import pallas as pl
from jax.experimental.pallas import tpu as pltpu
from jax.sharding import PartitionSpec as P

SLOTS = 8
CLON = 128
PASSES = 4
RHS = 4
OBS = 512
CAP = 8
DEVICES = 128
LON = 16
ROWS = 256
CHUNKS = 8
DEPTH = ROWS // CHUNKS
TALL = DEPTH + 2
RUN = 9
SPAN = SLOTS * CLON
WIDE = RUN * 128
EAST = CLON + PASSES
TOTAL = DEVICES * CAP
RIM = 2 * PASSES
OUTER = 2 * PASSES * CHUNKS
MIDDLE = ROWS - OUTER
BF = jnp.bfloat16
F32 = jnp.float32
NT = ((1,), (1,))
TN = ((0,), (0,))


def iota(shape, dim):
    return lax.broadcasted_iota(jnp.int32, shape, dim)


def pick(cond):
    return jnp.where(cond, 1.0, 0.0).astype(BF)


def mm(a, b, dims=((1,), (0,))):
    return lax.dot_general(a, b, (dims, ((), ())), preferred_element_type=F32)


def thirds(x):
    hi = x.astype(BF)
    rest = x - hi.astype(F32)
    mid = rest.astype(BF)
    return hi, mid, (rest - mid.astype(F32)).astype(BF)


def params(mib):
    return pltpu.CompilerParams(vmem_limit_bytes=mib * 1024 * 1024)


def cost(flops, size):
    return pl.CostEstimate(flops=flops, bytes_accessed=size, transcendentals=0)


def lanes(shape, dim):
    lane = iota(shape, dim)
    q, k, s = lane // 128, lane % 128 // 8, lane % 8
    return k * RUN + q, s, q, k


def rolled(x, step):
    return pltpu.roll(x, step % 128, 1)


def beside(row):
    return row[1:] + [rolled(row[0], -SLOTS)], [rolled(row[-1], SLOTS)] + row[:-1]


PIECES = 4


def pack_kernel(prints_hbm, weights_hbm, target_hbm, block_hbm, slot_hbm, out_hbm, rank_out,
                prints, weights, target, block, slot, masked, meta, spread, wide, out, sems, out_sems):
    pairs = ((target_hbm, target), (weights_hbm, weights), (block_hbm, block), (slot_hbm, slot), (prints_hbm, prints))
    copies = [pltpu.make_async_copy(a, b, sems.at[i]) for i, (a, b) in enumerate(pairs)]
    for copy in copies:
        copy.start()
    e, s, q, k = lanes((1, WIDE), 1)
    base = s * CLON + e
    source = jnp.where(e < PASSES, base + CLON - PASSES, jnp.where(e < EAST, base - PASSES, base - EAST))
    source = jnp.where(e < EAST + PASSES, source, -1)
    spread[...] = pick(iota((SPAN, WIDE), 0) == source)
    before = pick(iota((OBS, OBS), 0) < iota((OBS, OBS), 1))
    for copy in copies[:4]:
        copy.wait()
    t = target[...]
    hit = pick(iota((DEVICES, OBS), 0) == t)
    earlier = mm(hit, before)
    rank = jnp.sum(hit.astype(F32) * earlier, axis=0, keepdims=True)
    rank_out[...] = jnp.broadcast_to(rank, (8, OBS))
    place = t * CAP + rank.astype(jnp.int32)
    blk = block[...]
    meta[...] = jnp.zeros_like(meta)
    meta[0:RHS, :] = weights[...].astype(F32)
    meta[4:5, :] = ((blk % DEPTH) * CHUNKS + blk // DEPTH).astype(F32)
    meta[5:6, :] = slot[...].astype(F32)
    facts = meta[...].astype(BF)
    slots = mm(facts, pick(iota((8, 128), 0) == 5), TN).astype(BF)
    where = pick(iota((TOTAL, OBS), 0) == place)
    copies[4].wait()
    for s in range(SLOTS):
        live = slots >= jnp.asarray(s, BF)
        piece = prints[:, s * CLON:(s + 1) * CLON]
        masked[:, s * CLON:(s + 1) * CLON] = jnp.where(live, piece, jnp.zeros_like(piece))
    e, s, q, k = lanes((1, WIDE), 1)
    fact = jnp.where((k == 15) & (q >= 1) & (q <= 3) & (s < 5), s, -1)
    wide[...] = (mm(masked[...], spread[...]) + mm(facts, pick(iota((8, WIDE), 0) == fact), TN)).astype(BF)
    e, s, q, k = lanes((1, 1, WIDE), 2)
    from_west = (e < PASSES) | ((k == 15) & (q == 2))
    from_east = ((e >= EAST) & (e < EAST + PASSES)) | ((k == 15) & (q == 3))
    sends = []
    size = TOTAL // PIECES
    for i in range(PIECES):
        rows = slice(i * size, (i + 1) * size)
        moved = mm(where[rows], wide[...]).reshape(size // (LON * CAP), LON * CAP, WIDE)
        up = jnp.concatenate([moved[:, -CAP:], moved[:, :-CAP]], axis=1)
        down = jnp.concatenate([moved[:, CAP:], moved[:, :CAP]], axis=1)
        result = jnp.where(from_west, up, jnp.where(from_east, down, moved))
        out[rows, :] = result.reshape(size, WIDE).astype(BF)
        sends.append(pltpu.make_async_copy(out.at[rows, :], out_hbm.at[rows, :], out_sems.at[i]))
        sends[-1].start()
    for send in sends:
        send.wait()


def pack(prints, weights, target, block, slot):
    hbm = pl.BlockSpec(memory_space=pltpu.HBM)
    return pl.pallas_call(
        pack_kernel,
        in_specs=[hbm] * 5,
        out_specs=(hbm, pl.BlockSpec(memory_space=pltpu.VMEM)),
        out_shape=(
            jax.ShapeDtypeStruct((TOTAL, WIDE), BF),
            jax.ShapeDtypeStruct((8, OBS), F32),
        ),
        scratch_shapes=[
            pltpu.VMEM((OBS, SPAN), BF),
            pltpu.VMEM((RHS, OBS), BF),
            pltpu.VMEM((1, OBS), jnp.int32),
            pltpu.VMEM((1, OBS), jnp.int32),
            pltpu.VMEM((1, OBS), jnp.int32),
            pltpu.VMEM((OBS, SPAN), BF),
            pltpu.VMEM((8, OBS), F32),
            pltpu.VMEM((SPAN, WIDE), BF),
            pltpu.VMEM((OBS, WIDE), BF),
            pltpu.VMEM((TOTAL, WIDE), BF),
            pltpu.SemaphoreType.DMA((5,)),
            pltpu.SemaphoreType.DMA((PIECES,)),
        ],
        compiler_params=params(60),
        cost_estimate=cost(2 * TOTAL * OBS * SPAN, 3 << 20),
        name="pack",
    )(prints, weights, target, block, slot)


def faces_kernel(own, first, second, coef, over, root, rim, wide):
    e, _, _, _ = lanes((1, WIDE), 1)
    even = lax.axis_index("lon") % 2 == 0

    def place(x, cond, shift):
        one = jnp.where(cond & (iota((CLON, WIDE), 0) == e + shift), 1.0, 0.0)
        return jnp.dot(jnp.sqrt(x), one, precision=lax.Precision.HIGHEST, preferred_element_type=F32)

    left = jnp.where(even, second[...], first[...])
    right = jnp.where(even, first[...], second[...])
    flat = place(own[...], (e >= PASSES) & (e < EAST), -PASSES)
    flat = flat + (place(left, e < PASSES, CLON - PASSES) + place(right, (e >= EAST) & (e < EAST + PASSES), -EAST))
    beyond = jnp.zeros((CHUNKS, 128), F32)
    for q in range(RUN):
        wide[q, :CHUNKS, :] = beyond
        wide[q, CHUNKS:CHUNKS + ROWS, :] = flat[:, q * 128:(q + 1) * 128]
        wide[q, CHUNKS + ROWS:, :] = beyond
    for j in range(RIM):
        rim[j, :RHS, :] = jnp.broadcast_to(flat[j:j + 1], (RHS, WIDE))
        rim[j, RHS:, :] = jnp.broadcast_to(flat[ROWS - 1 - j:ROWS - j], (RHS, WIDE))

    def level(b):
        return [wide[q, pl.ds(CHUNKS + b, CHUNKS, stride=DEPTH), :] for q in range(RUN)]

    south, here = level(-1), level(0)
    for b in range(DEPTH):
        north = level(b + 1)
        ahead, behind = beside(here)
        rows = slice(b * CHUNKS, (b + 1) * CHUNKS)
        for q in range(RUN):
            cols = slice(q * 128, (q + 1) * 128)
            mid = 1.0 - here[q] * ((north[q] + south[q]) + (ahead[q] + behind[q]))
            some = here[q] > 0.0
            coef[0, rows, cols] = mid
            coef[1, rows, cols] = here[q] * here[q]
            over[rows, cols] = jnp.where(some, mid / jnp.where(some, here[q], 1.0), 0.0)
            root[rows, cols] = here[q]
        south, here = here, north


def faces(own, first, second):
    return pl.pallas_call(
        faces_kernel,
        out_shape=(
            jax.ShapeDtypeStruct((2, ROWS, WIDE), F32),
            jax.ShapeDtypeStruct((ROWS, WIDE), F32),
            jax.ShapeDtypeStruct((ROWS, WIDE), F32),
            jax.ShapeDtypeStruct((RIM, 2 * RHS, WIDE), F32),
        ),
        scratch_shapes=[pltpu.VMEM((RUN, ROWS + 2 * CHUNKS, 128), F32)],
        compiler_params=params(12),
        cost_estimate=cost(1 << 30, 6 << 20),
        name="faces",
    )(own, first, second)


def surround(ref, r):
    last = DEPTH * CHUNKS
    ref[r, :CHUNKS, :] = pltpu.roll(ref[r, last:last + CHUNKS, :], 1, 0)
    ref[r, last + CHUNKS:, :] = pltpu.roll(ref[r, CHUNKS:2 * CHUNKS, :], CHUNKS - 1, 0)


def adjoint_kernel(got, root_any, roots, field, rim, inner, outer, facts_out, own, west, east, root, sem):
    copy = pltpu.make_async_copy(root_any, root, sem)
    copy.start()
    column, fact = iota((16, 128), 0), iota((16, 128), 1) - 120
    facts = mm(pick((fact == column) & (column < 5)), got[:, 128:256], NT)
    facts = facts + mm(pick((fact == column - 5) & (column >= 5) & (column < 10)), got[:, 256:384], NT)
    facts = facts + mm(pick((fact == column - 10) & (column >= 10) & (column < 15)), got[:, 384:512], NT)
    facts_out[...] = facts
    for q in range(RUN):
        piece = got[:, q * 128:(q + 1) * 128]
        e = (iota((1, 128), 1) // 8) * RUN + q
        ones = lambda cond: jnp.broadcast_to(pick(cond), piece.shape)
        own[:, q * 128:(q + 1) * 128] = piece * ones((e >= PASSES) & (e < EAST))
        if q < PASSES:
            west[:, q * 128:(q + 1) * 128] = piece * ones(e < PASSES)
        if q in EASTERN:
            at = EASTERN.index(q) * 128
            east[:, at:at + 128] = piece * ones((e >= EAST) & (e < EAST + PASSES))
    row = iota((ROWS, TOTAL), 0).astype(F32)

    def spread(first, r):
        return jnp.where(row == facts[first + RHS:first + RHS + 1], facts[first + r:first + r + 1], 0.0).astype(BF)

    for r in range(RHS):
        total = mm(spread(0, r), own[...])
        before, after = mm(spread(5, r), west[...]), mm(spread(10, r), east[...])
        if r == 0:
            copy.wait()
        for q in range(RUN):
            cols = slice(q * 128, (q + 1) * 128)
            part = total[:, cols]
            if q < PASSES:
                part = part + before[:, cols]
            if q in EASTERN:
                at = EASTERN.index(q) * 128
                part = part + after[:, at:at + 128]
            field[r, CHUNKS:CHUNKS + ROWS, cols] = part * root[:, cols]
        surround(field, r)
        for j in range(RIM):
            at = (j + 1) * CHUNKS
            rim[j, r:r + 1, :] = field[r, at:at + 1, :]
            end = (DEPTH + 1 - j) * CHUNKS
            rim[j, RHS + r:RHS + r + 1, :] = field[r, end - 1:end, :]
    even = lax.axis_index("lat") % 2 == 0
    for base, ref in ((0, rim), (PASSES, roots)):
        for j in range(PASSES):
            low, high = ref[j, :RHS, :], ref[j, RHS:, :]
            inner[base + j] = jnp.where(even, high, low)
            outer[base + j] = jnp.where(even, low, high)


EASTERN = [(EAST + i) % RUN for i in range(PASSES)]


def adjoint(got, root, roots):
    vmem = pl.BlockSpec(memory_space=pltpu.VMEM)
    return pl.pallas_call(
        adjoint_kernel,
        in_specs=[vmem, pl.BlockSpec(memory_space=pl.ANY), vmem],
        out_shape=(
            jax.ShapeDtypeStruct((RHS, TALL * CHUNKS, WIDE), F32),
            jax.ShapeDtypeStruct((RIM, 2 * RHS, WIDE), F32),
            jax.ShapeDtypeStruct((2 * PASSES, RHS, WIDE), F32),
            jax.ShapeDtypeStruct((2 * PASSES, RHS, WIDE), F32),
            jax.ShapeDtypeStruct((16, TOTAL), F32),
        ),
        scratch_shapes=[
            pltpu.VMEM((TOTAL, WIDE), BF),
            pltpu.VMEM((TOTAL, PASSES * 128), BF),
            pltpu.VMEM((TOTAL, PASSES * 128), BF),
            pltpu.VMEM((ROWS, WIDE), F32),
            pltpu.SemaphoreType.DMA(()),
        ],
        compiler_params=params(16),
        cost_estimate=cost(5 << 30, 8 << 20),
        name="adjoint",
    )(got, root, roots)


def inside(q):
    e = (iota((1, 128), 1) // 8) * RUN + q
    return (e >= PASSES) & (e < EAST)


def diffuse_kernel(field, coef, over, root, smooth, outer, one, two):
    usual, final = (coef.at[0], coef.at[1]), (over, root)

    def rows_of(e):
        at = e * CHUNKS
        return pl.ds(at if isinstance(at, int) else pl.multiple_of(at, CHUNKS), CHUNKS)

    def two_levels(ref, e, factor, store):
        def load(r, at, q):
            return ref[r, rows_of(at), q * 128:(q + 1) * 128]

        levels = (e, e + 1)
        turned_west = [[rolled(load(r, at, RUN - 1), SLOTS) for at in levels] for r in range(RHS)]
        turned_east = [[rolled(load(r, at, 0), -SLOTS) for at in levels] for r in range(RHS)]
        behind, here = [[[load(r, at, q) for at in levels] for r in range(RHS)] for q in (0, 1)]
        for q in [*range(1, RUN), 0]:
            mid, near = [[kind[rows_of(at - 1), q * 128:(q + 1) * 128] for at in levels] for kind in factor]
            if q == 0:
                behind = turned_west
                here, ahead = [[[load(r, at, i) for at in levels] for r in range(RHS)] for i in (0, 1)]
            elif q + 1 < RUN:
                ahead = [[load(r, at, q + 1) for at in levels] for r in range(RHS)]
            else:
                ahead = turned_east
            for r in range(RHS):
                column = [load(r, e - 1, q)] + here[r] + [load(r, e + 2, q)]
                for i in range(2):
                    total = (column[i + 2] + column[i]) + (ahead[r][i] + behind[r][i])
                    store(r, q, i, mid[i] * here[r][i] + near[i] * total)
            behind, here = here, ahead

    def sweep(ref, target, first, end, factor, to=0):
        def step(pair, _):
            e = first + 2 * pair

            def store(r, q, i, value):
                target[r, rows_of(e + i + to), q * 128:(q + 1) * 128] = value

            two_levels(ref, e, factor, store)
            return 0

        lax.fori_loop(0, (end - first) // 2, step, 0, unroll=2)

    for ref, target in ((field, one), (one, two), (two, one)):
        sweep(ref, target, 1, DEPTH + 1, usual)
        for r in range(RHS):
            surround(target, r)
    sweep(one, outer, 1, PASSES + 1, final, -1)
    sweep(one, outer, DEPTH + 1 - PASSES, DEPTH + 1, final, 2 * PASSES - 1 - DEPTH)

    def rounded(pair, _):
        first = {}

        def store(r, q, i, value):
            if i == 0:
                first[r, q] = value
                return
            both = jnp.concatenate([first.pop((r, q)), value], axis=0)
            at = pl.ds(pl.multiple_of(pair * 2 * CHUNKS, 2 * CHUNKS), 2 * CHUNKS)
            smooth[r, at, q * 128:(q + 1) * 128] = jnp.where(inside(q), both, 0.0).astype(BF)

        two_levels(one, PASSES + 1 + 2 * pair, final, store)
        return 0

    lax.fori_loop(0, MIDDLE // (2 * CHUNKS), rounded, 0, unroll=2)


def diffuse(field, coef, over, root):
    return pl.pallas_call(
        diffuse_kernel,
        out_shape=(
            jax.ShapeDtypeStruct((RHS, MIDDLE, WIDE), BF),
            jax.ShapeDtypeStruct((RHS, OUTER, WIDE), F32),
        ),
        scratch_shapes=[
            pltpu.VMEM((RHS, TALL * CHUNKS, WIDE), F32),
            pltpu.VMEM((RHS, TALL * CHUNKS, WIDE), F32),
        ],
        compiler_params=params(14),
        cost_estimate=cost(6 << 30, 8 << 20),
        name="diffuse",
    )(field, coef, over, root)


def finish_kernel(smooth, outer, rim, roots, inner, beyond, got, facts, out, border, values):
    even = lax.axis_index("lat") % 2 == 0

    def levels(base, own):
        rows = []
        for j in range(base + PASSES - 1, base - 1, -1):
            south = jnp.where(even, beyond[j], inner[j])
            north = jnp.where(even, inner[j], beyond[j])
            rows.append(jnp.concatenate([south, north], axis=0))
        return [[x[:, q * 128:(q + 1) * 128] for q in range(RUN)] for x in rows + [own[j] for j in range(RIM)]]

    def around(x, j):
        ahead, behind = beside(x[j])
        return [(x[j + 1][q] + x[j - 1][q]) + (ahead[q] + behind[q]) for q in range(RUN)]

    v, root = levels(0, rim), levels(PASSES, roots)
    count = PASSES + RIM
    mid = [None] + [[1.0 - x * y for x, y in zip(root[j], around(root, j))] for j in range(1, count - 1)]
    for step in range(1, PASSES + 1):
        new = list(v)
        for j in range(step, count - step):
            total = around(v, j)
            new[j] = [mid[j][q] * v[j][q] + (root[j][q] * root[j][q]) * total[q] for q in range(RUN)]
        v = new
    for j in range(PASSES, 2 * PASSES):
        some = [x > 0.0 for x in root[j]]
        v[j] = [jnp.where(some[q], v[j][q] / jnp.where(some[q], root[j][q], 1.0), 0.0) for q in range(RUN)]
    sub = iota((CHUNKS, 1), 0)
    for r in range(RHS):
        for q in range(RUN):
            cols = slice(q * 128, (q + 1) * 128)
            for pair in range(PASSES):
                both = []
                for b in (2 * pair, 2 * pair + 1):
                    here = outer[r, b * CHUNKS:(b + 1) * CHUNKS, cols]
                    if b < PASSES:
                        here = jnp.where(sub == 0, v[PASSES + b][q][r:r + 1], here)
                    else:
                        j = PASSES + 2 * PASSES - 1 - b
                        here = jnp.where(sub == CHUNKS - 1, v[j][q][RHS + r:RHS + r + 1], here)
                    both.append(here)
                both = jnp.where(inside(q), jnp.concatenate(both, axis=0), 0.0).astype(BF)
                border[r, pair * 2 * CHUNKS:(pair + 1) * 2 * CHUNKS, cols] = both

    side = PASSES * CHUNKS
    chosen = iota((ROWS, TOTAL), 0).astype(F32) == facts[RHS:RHS + 1, :]
    total = [0.0] * RHS
    for ref, spans in ((smooth, ((side, MIDDLE),)), (border, ((0, side), (ROWS - side, side)))):
        shares = mm(ref[...].reshape(-1, WIDE), got[...], NT)
        at = 0
        for r in range(RHS):
            for first, size in spans:
                part = jnp.where(chosen[first:first + size], shares[at:at + size], 0.0)
                total[r] = total[r] + jnp.sum(part, axis=0, keepdims=True)
                at += size
    for r in range(RHS):
        values[r:r + 1, :] = total[r]
        values[RHS + r:RHS + r + 1, :] = total[r]
    both = values[...]
    turn = iota((2 * RHS, TOTAL), 0) // RHS
    keep = [jnp.where(iota((2 * RHS, TOTAL), 1) % CAP == turn + 2 * i, 1.0, 0.0) for i in range(CAP // 2)]
    many = [part.astype(F32) * k for part in thirds(both) for k in keep]
    owner = pick(iota((DEVICES, TOTAL), 1) // CAP == iota((DEVICES, TOTAL), 0))
    sums = mm(owner, jnp.concatenate(many, axis=0).astype(BF), NT)
    size = CAP * RHS
    out[...] = jnp.zeros_like(out)
    out[:, :size] = (sums[:, :size] + sums[:, size:2 * size]) + sums[:, 2 * size:3 * size]


def finish(smooth, outer, rim, roots, inner, beyond, got, facts):
    return pl.pallas_call(
        finish_kernel,
        out_shape=jax.ShapeDtypeStruct((DEVICES, 128), F32),
        scratch_shapes=[
            pltpu.VMEM((RHS, OUTER, WIDE), BF),
            pltpu.VMEM((8, TOTAL), F32),
        ],
        compiler_params=params(16),
        cost_estimate=cost(3 << 30, 10 << 20),
        name="finish",
    )(smooth, outer, rim, roots, inner, beyond, got, facts)


def unpack_kernel(values, target, rank, out):
    hit = pick(iota((DEVICES, OBS), 0) == target[...])
    total = jnp.zeros((CAP * RHS, OBS), F32)
    for part in thirds(values[:, :CAP * RHS]):
        total = total + mm(part, hit, TN)
    total = jnp.where((iota((CAP * RHS, OBS), 0) // RHS).astype(F32) == rank[0:1, :], total, 0.0)
    pair = (total[0:8] + total[8:16]) + (total[16:24] + total[24:32])
    out[...] = pair[0:RHS] + pair[RHS:]


def unpack(values, target, rank):
    return pl.pallas_call(
        unpack_kernel,
        out_shape=jax.ShapeDtypeStruct((RHS, OBS), F32),
        compiler_params=params(8),
        name="unpack",
    )(values, target, rank)


def swap(x, axis, second, closed):
    count = lax.axis_size(axis)
    pairs = [(i, (i + 1) % count) for i in range(int(second), count, 2) if closed or i + 1 < count]
    return lax.ppermute(x, axis, pairs + [(j, i) for i, j in pairs])


def body(footprints, dual_weights, target_device, target_block, obs_slot, diffusivity):
    target = target_device.reshape(1, OBS)
    packed, rank = pack(footprints, dual_weights.T, target, target_block.reshape(1, OBS), obs_slot.reshape(1, OBS))
    first = swap(diffusivity, "lon", False, True)
    second = swap(diffusivity, "lon", True, True)
    packed, first, second = lax.optimization_barrier((packed, first, second))
    coef, over, root, roots = faces(diffusivity, first, second)
    got = lax.all_to_all(packed, ("lat", "lon"), split_axis=0, concat_axis=0, tiled=True)
    field, rim, inner, beyond, facts = adjoint(got, root, roots)
    inner = swap(inner, "lat", False, False)
    beyond = swap(beyond, "lat", True, False)
    smooth, outer = diffuse(field, coef, over, root)
    values = finish(smooth, outer, rim, roots, inner, beyond, got, facts)
    returned = lax.all_to_all(values, ("lat", "lon"), split_axis=0, concat_axis=0, tiled=True)
    return unpack(returned, target, rank).T


def solution(mesh):
    placed = (
        P(("lat", "lon"), None),
        P(("lat", "lon"), None),
        P(("lat", "lon"), None),
        P(("lat", "lon")),
        P(("lat", "lon")),
        P("lat", "lon"),
    )
    return jax.shard_map(
        body, mesh=mesh, in_specs=placed, out_specs=P(("lat", "lon"), None), check_vma=False
    )
```

```python
import jax
import jax.numpy as jnp
from jax import lax
from jax.experimental import pallas as pl
from jax.experimental.pallas import tpu as pltpu
from jax.sharding import PartitionSpec as P

SLOTS = 8
CLON = 128
PASSES = 4
RHS = 4
OBS = 512
CAP = 8
DEVICES = 128
LON = 16
ROWS = 256
CHUNKS = 8
DEPTH = ROWS // CHUNKS
TALL = DEPTH + 2
RUN = 9
FRONT = 3
SPAN = SLOTS * CLON
WIDE = RUN * 128
EAST = CLON + PASSES
TOTAL = DEVICES * CAP
RIM = 2 * PASSES
OUTER = 2 * PASSES * CHUNKS
MIDDLE = ROWS - OUTER
BF = jnp.bfloat16
F32 = jnp.float32
NT = ((1,), (1,))
TN = ((0,), (0,))


def iota(shape, dim):
    return lax.broadcasted_iota(jnp.int32, shape, dim)


def pick(cond):
    return jnp.where(cond, 1.0, 0.0).astype(BF)


def mm(a, b, dims=((1,), (0,))):
    return lax.dot_general(a, b, (dims, ((), ())), preferred_element_type=F32)


def thirds(x):
    hi = x.astype(BF)
    rest = x - hi.astype(F32)
    mid = rest.astype(BF)
    return hi, mid, (rest - mid.astype(F32)).astype(BF)


def params(mib):
    return pltpu.CompilerParams(vmem_limit_bytes=mib * 1024 * 1024)


def cost(flops, size):
    return pl.CostEstimate(flops=flops, bytes_accessed=size, transcendentals=0)


def lanes(shape, dim):
    lane = iota(shape, dim)
    q, k, s = lane // 128, lane % 128 // 8, lane % 8
    return k * RUN + q - FRONT, s, q, k


def rolled(x, step):
    return pltpu.roll(x, step % 128, 1)


def beside(row):
    return row[1:] + [rolled(row[0], -SLOTS)], [rolled(row[-1], SLOTS)] + row[:-1]


PIECES = 4


def pack_kernel(prints_hbm, weights_hbm, target_hbm, block_hbm, slot_hbm, out_hbm, rank_out,
                prints, weights, target, block, slot, masked, meta, spread, wide, out, sems, out_sems):
    pairs = ((target_hbm, target), (weights_hbm, weights), (block_hbm, block), (slot_hbm, slot), (prints_hbm, prints))
    copies = [pltpu.make_async_copy(a, b, sems.at[i]) for i, (a, b) in enumerate(pairs)]
    for copy in copies:
        copy.start()
    e, s, q, k = lanes((1, WIDE), 1)
    base = s * CLON + e
    source = jnp.where(e < PASSES, base + CLON - PASSES, jnp.where(e < EAST, base - PASSES, base - EAST))
    source = jnp.where((e >= 0) & (e < EAST + PASSES), source, -1)
    spread[...] = pick(iota((SPAN, WIDE), 0) == source)
    before = pick(iota((OBS, OBS), 0) < iota((OBS, OBS), 1))
    for copy in copies[:4]:
        copy.wait()
    blk = block[...]
    meta[...] = jnp.zeros_like(meta)
    meta[0:RHS, :] = weights[...].astype(F32)
    meta[4:5, :] = ((blk % DEPTH) * CHUNKS + blk // DEPTH).astype(F32)
    meta[5:6, :] = slot[...].astype(F32)
    facts = meta[...].astype(BF)
    slots = mm(facts, pick(iota((8, 128), 0) == 5), TN).astype(BF)
    t = target[...]
    hit = pick(iota((DEVICES, OBS), 0) == t)
    earlier = mm(hit, before)
    copies[4].wait()
    for s in range(SLOTS):
        live = slots >= jnp.asarray(s, BF)
        piece = prints[:, s * CLON:(s + 1) * CLON]
        masked[:, s * CLON:(s + 1) * CLON] = jnp.where(live, piece, jnp.zeros_like(piece))
    e, s, q, k = lanes((1, WIDE), 1)
    fact = jnp.where((k == 0) & (q < FRONT) & (s < 5), s, -1)
    wide[...] = (mm(masked[...], spread[...]) + mm(facts, pick(iota((8, WIDE), 0) == fact), TN)).astype(BF)
    rank = jnp.sum(hit.astype(F32) * earlier, axis=0, keepdims=True)
    rank_out[...] = jnp.broadcast_to(rank, (8, OBS))
    where = pick(iota((TOTAL, OBS), 0) == t * CAP + rank.astype(jnp.int32))
    e, s, q, k = lanes((1, 1, WIDE), 2)
    from_west = ((e >= 0) & (e < PASSES)) | ((k == 0) & (q == 1))
    from_east = ((e >= EAST) & (e < EAST + PASSES)) | ((k == 0) & (q == 2))
    sends = []
    size = TOTAL // PIECES
    for i in range(PIECES):
        rows = slice(i * size, (i + 1) * size)
        moved = mm(where[rows], wide[...]).reshape(size // (LON * CAP), LON * CAP, WIDE)
        up = jnp.concatenate([moved[:, -CAP:], moved[:, :-CAP]], axis=1)
        down = jnp.concatenate([moved[:, CAP:], moved[:, :CAP]], axis=1)
        result = jnp.where(from_west, up, jnp.where(from_east, down, moved))
        out[rows, :] = result.reshape(size, WIDE).astype(BF)
        sends.append(pltpu.make_async_copy(out.at[rows, :], out_hbm.at[rows, :], out_sems.at[i]))
        sends[-1].start()
    for send in sends:
        send.wait()


def pack(prints, weights, target, block, slot):
    hbm = pl.BlockSpec(memory_space=pltpu.HBM)
    return pl.pallas_call(
        pack_kernel,
        in_specs=[hbm] * 5,
        out_specs=(hbm, pl.BlockSpec(memory_space=pltpu.VMEM)),
        out_shape=(
            jax.ShapeDtypeStruct((TOTAL, WIDE), BF),
            jax.ShapeDtypeStruct((8, OBS), F32),
        ),
        scratch_shapes=[
            pltpu.VMEM((OBS, SPAN), BF),
            pltpu.VMEM((RHS, OBS), BF),
            pltpu.VMEM((1, OBS), jnp.int32),
            pltpu.VMEM((1, OBS), jnp.int32),
            pltpu.VMEM((1, OBS), jnp.int32),
            pltpu.VMEM((OBS, SPAN), BF),
            pltpu.VMEM((8, OBS), F32),
            pltpu.VMEM((SPAN, WIDE), BF),
            pltpu.VMEM((OBS, WIDE), BF),
            pltpu.VMEM((TOTAL, WIDE), BF),
            pltpu.SemaphoreType.DMA((5,)),
            pltpu.SemaphoreType.DMA((PIECES,)),
        ],
        compiler_params=params(60),
        cost_estimate=cost(2 * TOTAL * OBS * SPAN, 3 << 20),
        name="pack",
    )(prints, weights, target, block, slot)


def faces_kernel(own, first, second, coef, over, root, rim, wide):
    e, _, _, _ = lanes((1, WIDE), 1)
    even = lax.axis_index("lon") % 2 == 0

    def place(x, cond, shift):
        one = jnp.where(cond & (iota((CLON, WIDE), 0) == e + shift), 1.0, 0.0)
        return jnp.dot(jnp.sqrt(x), one, precision=lax.Precision.HIGHEST, preferred_element_type=F32)

    left = jnp.where(even, second[...], first[...])
    right = jnp.where(even, first[...], second[...])
    flat = place(own[...], (e >= PASSES) & (e < EAST), -PASSES)
    flat = flat + (place(left, (e >= 0) & (e < PASSES), CLON - PASSES) + place(right, (e >= EAST) & (e < EAST + PASSES), -EAST))
    beyond = jnp.zeros((CHUNKS, 128), F32)
    for q in range(RUN):
        wide[q, :CHUNKS, :] = beyond
        wide[q, CHUNKS:CHUNKS + ROWS, :] = flat[:, q * 128:(q + 1) * 128]
        wide[q, CHUNKS + ROWS:, :] = beyond
    for j in range(RIM):
        rim[j, :RHS, :] = jnp.broadcast_to(flat[j:j + 1], (RHS, WIDE))
        rim[j, RHS:, :] = jnp.broadcast_to(flat[ROWS - 1 - j:ROWS - j], (RHS, WIDE))

    def level(b):
        return [wide[q, pl.ds(CHUNKS + b, CHUNKS, stride=DEPTH), :] for q in range(RUN)]

    south, here = level(-1), level(0)
    for b in range(DEPTH):
        north = level(b + 1)
        ahead, behind = beside(here)
        rows = slice(b * CHUNKS, (b + 1) * CHUNKS)
        for q in range(RUN):
            cols = slice(q * 128, (q + 1) * 128)
            mid = 1.0 - here[q] * ((north[q] + south[q]) + (ahead[q] + behind[q]))
            some = here[q] > 0.0
            coef[0, rows, cols] = mid
            coef[1, rows, cols] = here[q] * here[q]
            over[rows, cols] = jnp.where(some, mid / jnp.where(some, here[q], 1.0), 0.0)
            root[rows, cols] = here[q]
        south, here = here, north


def faces(own, first, second):
    return pl.pallas_call(
        faces_kernel,
        out_shape=(
            jax.ShapeDtypeStruct((2, ROWS, WIDE), F32),
            jax.ShapeDtypeStruct((ROWS, WIDE), F32),
            jax.ShapeDtypeStruct((ROWS, WIDE), F32),
            jax.ShapeDtypeStruct((RIM, 2 * RHS, WIDE), F32),
        ),
        scratch_shapes=[pltpu.VMEM((RUN, ROWS + 2 * CHUNKS, 128), F32)],
        compiler_params=params(12),
        cost_estimate=cost(1 << 30, 6 << 20),
        name="faces",
    )(own, first, second)


def adjoint_kernel(got, roots, field, rim, inner, outer, facts_out):
    column, lane = iota((16, 128), 0), iota((16, 128), 1)
    facts = jnp.zeros((16, TOTAL), F32)
    for i in range(FRONT):
        mine = (lane == column - 5 * i) & (column >= 5 * i) & (column < 5 * i + 5)
        facts = facts + mm(pick(mine), got[:, i * 128:(i + 1) * 128], NT)
    facts_out[...] = facts
    row = iota((ROWS, TOTAL), 0).astype(F32)

    def spread(first, r):
        return jnp.where(row == facts[first + RHS:first + RHS + 1], facts[first + r:first + r + 1], 0.0).astype(BF)

    lane = iota((1, 128), 1)
    end = FRONT + PASSES
    for r in range(RHS):
        total = mm(spread(0, r), got[...])
        before = mm(spread(5, r), got[:, FRONT * 128:end * 128])
        after = mm(spread(10, r), got[:, :PASSES * 128])
        for q in range(RUN):
            cols = slice(q * 128, (q + 1) * 128)
            part = total[:, cols]
            if FRONT <= q < end:
                part = jnp.where(lane < SLOTS, before[:, (q - FRONT) * 128:(q - FRONT + 1) * 128], part)
            if q < PASSES:
                part = jnp.where(lane >= 128 - SLOTS, after[:, cols], part)
            field[r, :, cols] = part
        for j in range(RIM):
            at = j * CHUNKS
            rim[j, r:r + 1, :] = field[r, at:at + 1, :]
            at = (DEPTH - j) * CHUNKS - 1
            rim[j, RHS + r:RHS + r + 1, :] = field[r, at:at + 1, :]
    for j in range(RIM):
        rim[j] = rim[j] * roots[j]
    even = lax.axis_index("lat") % 2 == 0
    for base, ref in ((0, rim), (PASSES, roots)):
        for j in range(PASSES):
            low, high = ref[j, :RHS, :], ref[j, RHS:, :]
            inner[base + j] = jnp.where(even, high, low)
            outer[base + j] = jnp.where(even, low, high)


def adjoint(got, roots):
    return pl.pallas_call(
        adjoint_kernel,
        out_shape=(
            jax.ShapeDtypeStruct((RHS, ROWS, WIDE), F32),
            jax.ShapeDtypeStruct((RIM, 2 * RHS, WIDE), F32),
            jax.ShapeDtypeStruct((2 * PASSES, RHS, WIDE), F32),
            jax.ShapeDtypeStruct((2 * PASSES, RHS, WIDE), F32),
            jax.ShapeDtypeStruct((16, TOTAL), F32),
        ),
        compiler_params=params(16),
        cost_estimate=cost(5 << 30, 8 << 20),
        name="adjoint",
    )(got, roots)


def inside(q):
    e = (iota((1, 128), 1) // 8) * RUN + q - FRONT
    return (e >= PASSES) & (e < EAST)


def surround(ref, r):
    last = DEPTH * CHUNKS
    ref[r, :CHUNKS, :] = pltpu.roll(ref[r, last:last + CHUNKS, :], 1, 0)
    ref[r, last + CHUNKS:, :] = pltpu.roll(ref[r, CHUNKS:2 * CHUNKS, :], CHUNKS - 1, 0)


def diffuse_kernel(field, coef, over, root, smooth, outer, one, two):
    usual, final = (coef.at[0], coef.at[1]), (over, root)

    def rows_of(e):
        at = e * CHUNKS
        return pl.ds(at if isinstance(at, int) else pl.multiple_of(at, CHUNKS), CHUNKS)

    def two_levels(ref, e, factor, store):
        def load(r, at, q):
            return ref[r, rows_of(at), q * 128:(q + 1) * 128]

        levels = (e, e + 1)
        turned_west = [[rolled(load(r, at, RUN - 1), SLOTS) for at in levels] for r in range(RHS)]
        turned_east = [[rolled(load(r, at, 0), -SLOTS) for at in levels] for r in range(RHS)]
        behind, here = [[[load(r, at, q) for at in levels] for r in range(RHS)] for q in (0, 1)]
        for q in [*range(1, RUN), 0]:
            mid, near = [[kind[rows_of(at - 1), q * 128:(q + 1) * 128] for at in levels] for kind in factor]
            if q == 0:
                behind = turned_west
                here, ahead = [[[load(r, at, i) for at in levels] for r in range(RHS)] for i in (0, 1)]
            elif q + 1 < RUN:
                ahead = [[load(r, at, q + 1) for at in levels] for r in range(RHS)]
            else:
                ahead = turned_east
            for r in range(RHS):
                column = [load(r, e - 1, q)] + here[r] + [load(r, e + 2, q)]
                for i in range(2):
                    total = (column[i + 2] + column[i]) + (ahead[r][i] + behind[r][i])
                    store(r, q, i, mid[i] * here[r][i] + near[i] * total)
            behind, here = here, ahead

    def sweep(ref, target, first, end, factor, to=0):
        def step(pair, _):
            e = first + 2 * pair

            def store(r, q, i, value):
                target[r, rows_of(e + i + to), q * 128:(q + 1) * 128] = value

            two_levels(ref, e, factor, store)
            return 0

        lax.fori_loop(0, (end - first) // 2, step, 0, unroll=2)

    def scale(e, _):
        for q in range(RUN):
            cols = slice(q * 128, (q + 1) * 128)
            factor = root[rows_of(e), cols]
            for r in range(RHS):
                two[r, rows_of(e + 1), cols] = field[r, rows_of(e), cols] * factor
        return 0

    lax.fori_loop(0, DEPTH, scale, 0, unroll=2)
    for r in range(RHS):
        surround(two, r)
    for ref, target in ((two, one), (one, two), (two, one)):
        sweep(ref, target, 1, DEPTH + 1, usual)
        for r in range(RHS):
            surround(target, r)
    sweep(one, outer, 1, PASSES + 1, final, -1)
    sweep(one, outer, DEPTH + 1 - PASSES, DEPTH + 1, final, 2 * PASSES - 1 - DEPTH)

    def rounded(pair, _):
        first = {}

        def store(r, q, i, value):
            if i == 0:
                first[r, q] = value
                return
            both = jnp.concatenate([first.pop((r, q)), value], axis=0)
            at = pl.ds(pl.multiple_of(pair * 2 * CHUNKS, 2 * CHUNKS), 2 * CHUNKS)
            smooth[r, at, q * 128:(q + 1) * 128] = jnp.where(inside(q), both, 0.0).astype(BF)

        two_levels(one, PASSES + 1 + 2 * pair, final, store)
        return 0

    lax.fori_loop(0, MIDDLE // (2 * CHUNKS), rounded, 0, unroll=2)


def diffuse(field, coef, over, root):
    return pl.pallas_call(
        diffuse_kernel,
        out_shape=(
            jax.ShapeDtypeStruct((RHS, MIDDLE, WIDE), BF),
            jax.ShapeDtypeStruct((RHS, OUTER, WIDE), F32),
        ),
        scratch_shapes=[
            pltpu.VMEM((RHS, TALL * CHUNKS, WIDE), F32),
            pltpu.VMEM((RHS, TALL * CHUNKS, WIDE), F32),
        ],
        compiler_params=params(14),
        cost_estimate=cost(6 << 30, 8 << 20),
        name="diffuse",
    )(field, coef, over, root)


def finish_kernel(smooth, outer, rim, roots, inner, beyond, got, facts, out, border, values):
    even = lax.axis_index("lat") % 2 == 0

    def levels(base, own):
        rows = []
        for j in range(base + PASSES - 1, base - 1, -1):
            south = jnp.where(even, beyond[j], inner[j])
            north = jnp.where(even, inner[j], beyond[j])
            rows.append(jnp.concatenate([south, north], axis=0))
        return [[x[:, q * 128:(q + 1) * 128] for q in range(RUN)] for x in rows + [own[j] for j in range(RIM)]]

    def around(x, j):
        ahead, behind = beside(x[j])
        return [(x[j + 1][q] + x[j - 1][q]) + (ahead[q] + behind[q]) for q in range(RUN)]

    v, root = levels(0, rim), levels(PASSES, roots)
    count = PASSES + RIM
    mid = [None] + [[1.0 - x * y for x, y in zip(root[j], around(root, j))] for j in range(1, count - 1)]
    for step in range(1, PASSES + 1):
        new = list(v)
        for j in range(step, count - step):
            total = around(v, j)
            new[j] = [mid[j][q] * v[j][q] + (root[j][q] * root[j][q]) * total[q] for q in range(RUN)]
        v = new
    for j in range(PASSES, 2 * PASSES):
        some = [x > 0.0 for x in root[j]]
        v[j] = [jnp.where(some[q], v[j][q] / jnp.where(some[q], root[j][q], 1.0), 0.0) for q in range(RUN)]
    sub = iota((CHUNKS, 1), 0)
    for r in range(RHS):
        for q in range(RUN):
            cols = slice(q * 128, (q + 1) * 128)
            for pair in range(PASSES):
                both = []
                for b in (2 * pair, 2 * pair + 1):
                    here = outer[r, b * CHUNKS:(b + 1) * CHUNKS, cols]
                    if b < PASSES:
                        here = jnp.where(sub == 0, v[PASSES + b][q][r:r + 1], here)
                    else:
                        j = PASSES + 2 * PASSES - 1 - b
                        here = jnp.where(sub == CHUNKS - 1, v[j][q][RHS + r:RHS + r + 1], here)
                    both.append(here)
                both = jnp.where(inside(q), jnp.concatenate(both, axis=0), 0.0).astype(BF)
                border[r, pair * 2 * CHUNKS:(pair + 1) * 2 * CHUNKS, cols] = both

    side = PASSES * CHUNKS
    chosen = iota((ROWS, TOTAL), 0).astype(F32) == facts[RHS:RHS + 1, :]
    total = [0.0] * RHS
    for ref, spans in ((smooth, ((side, MIDDLE),)), (border, ((0, side), (ROWS - side, side)))):
        shares = mm(ref[...].reshape(-1, WIDE), got[...], NT)
        at = 0
        for r in range(RHS):
            for first, size in spans:
                part = jnp.where(chosen[first:first + size], shares[at:at + size], 0.0)
                total[r] = total[r] + jnp.sum(part, axis=0, keepdims=True)
                at += size
    for r in range(RHS):
        values[r:r + 1, :] = total[r]
        values[RHS + r:RHS + r + 1, :] = total[r]
    both = values[...]
    turn = iota((2 * RHS, TOTAL), 0) // RHS
    keep = [jnp.where(iota((2 * RHS, TOTAL), 1) % CAP == turn + 2 * i, 1.0, 0.0) for i in range(CAP // 2)]
    many = [part.astype(F32) * k for part in thirds(both) for k in keep]
    owner = pick(iota((DEVICES, TOTAL), 1) // CAP == iota((DEVICES, TOTAL), 0))
    sums = mm(owner, jnp.concatenate(many, axis=0).astype(BF), NT)
    size = CAP * RHS
    out[...] = jnp.zeros_like(out)
    out[:, :size] = (sums[:, :size] + sums[:, size:2 * size]) + sums[:, 2 * size:3 * size]


def finish(smooth, outer, rim, roots, inner, beyond, got, facts):
    return pl.pallas_call(
        finish_kernel,
        out_shape=jax.ShapeDtypeStruct((DEVICES, 128), F32),
        scratch_shapes=[
            pltpu.VMEM((RHS, OUTER, WIDE), BF),
            pltpu.VMEM((8, TOTAL), F32),
        ],
        compiler_params=params(16),
        cost_estimate=cost(3 << 30, 10 << 20),
        name="finish",
    )(smooth, outer, rim, roots, inner, beyond, got, facts)


def unpack_kernel(values, target, rank, out):
    hit = pick(iota((DEVICES, OBS), 0) == target[...])
    total = jnp.zeros((CAP * RHS, OBS), F32)
    for part in thirds(values[:, :CAP * RHS]):
        total = total + mm(part, hit, TN)
    total = jnp.where((iota((CAP * RHS, OBS), 0) // RHS).astype(F32) == rank[0:1, :], total, 0.0)
    pair = (total[0:8] + total[8:16]) + (total[16:24] + total[24:32])
    out[...] = pair[0:RHS] + pair[RHS:]


def unpack(values, target, rank):
    return pl.pallas_call(
        unpack_kernel,
        out_shape=jax.ShapeDtypeStruct((RHS, OBS), F32),
        compiler_params=params(8),
        name="unpack",
    )(values, target, rank)


def swap(x, axis, second, closed):
    count = lax.axis_size(axis)
    pairs = [(i, (i + 1) % count) for i in range(int(second), count, 2) if closed or i + 1 < count]
    return lax.ppermute(x, axis, pairs + [(j, i) for i, j in pairs])


def body(footprints, dual_weights, target_device, target_block, obs_slot, diffusivity):
    target = target_device.reshape(1, OBS)
    packed, rank = pack(footprints, dual_weights.T, target, target_block.reshape(1, OBS), obs_slot.reshape(1, OBS))
    first = swap(diffusivity, "lon", False, True)
    second = swap(diffusivity, "lon", True, True)
    packed, first, second = lax.optimization_barrier((packed, first, second))
    coef, over, root, roots = faces(diffusivity, first, second)
    got = lax.all_to_all(packed, ("lat", "lon"), split_axis=0, concat_axis=0, tiled=True)
    field, rim, inner, beyond, facts = adjoint(got, roots)
    inner = swap(inner, "lat", False, False)
    beyond = swap(beyond, "lat", True, False)
    smooth, outer = diffuse(field, coef, over, root)
    values = finish(smooth, outer, rim, roots, inner, beyond, got, facts)
    returned = lax.all_to_all(values, ("lat", "lon"), split_axis=0, concat_axis=0, tiled=True)
    return unpack(returned, target, rank).T


def solution(mesh):
    placed = (
        P(("lat", "lon"), None),
        P(("lat", "lon"), None),
        P(("lat", "lon"), None),
        P(("lat", "lon")),
        P(("lat", "lon")),
        P("lat", "lon"),
    )
    return jax.shard_map(
        body, mesh=mesh, in_specs=placed, out_specs=P(("lat", "lon"), None), check_vma=False
    )
```

```python
import jax
import jax.numpy as jnp
from jax import lax
from jax.experimental import pallas as pl
from jax.experimental.pallas import tpu as pltpu
from jax.sharding import PartitionSpec as P

SLOTS = 8
CLON = 128
PASSES = 4
RHS = 4
OBS = 512
CAP = 8
DEVICES = 128
LON = 16
ROWS = 256
CHUNKS = 8
DEPTH = ROWS // CHUNKS
TALL = DEPTH + 2
RUN = 9
FRONT = 3
SPAN = SLOTS * CLON
WIDE = RUN * 128
EAST = CLON + PASSES
TOTAL = DEVICES * CAP
RIM = 2 * PASSES
OUTER = 2 * PASSES * CHUNKS
MIDDLE = ROWS - OUTER
BF = jnp.bfloat16
F32 = jnp.float32
NT = ((1,), (1,))
TN = ((0,), (0,))


def iota(shape, dim):
    return lax.broadcasted_iota(jnp.int32, shape, dim)


def pick(cond):
    return jnp.where(cond, 1.0, 0.0).astype(BF)


def mm(a, b, dims=((1,), (0,))):
    return lax.dot_general(a, b, (dims, ((), ())), preferred_element_type=F32)


def thirds(x):
    hi = x.astype(BF)
    rest = x - hi.astype(F32)
    mid = rest.astype(BF)
    return hi, mid, (rest - mid.astype(F32)).astype(BF)


def params(mib):
    return pltpu.CompilerParams(vmem_limit_bytes=mib * 1024 * 1024)


def cost(flops, size):
    return pl.CostEstimate(flops=flops, bytes_accessed=size, transcendentals=0)


def lanes(shape, dim):
    lane = iota(shape, dim)
    q, k, s = lane // 128, lane % 128 // 8, lane % 8
    return k * RUN + q - FRONT, s, q, k


def rolled(x, step):
    return pltpu.roll(x, step % 128, 1)


def beside(row):
    return row[1:] + [rolled(row[0], -SLOTS)], [rolled(row[-1], SLOTS)] + row[:-1]


PIECES = 4


def pack_kernel(prints_hbm, weights_hbm, target_hbm, block_hbm, slot_hbm, out_hbm, rank_out,
                prints, weights, target, block, slot, masked, meta, spread, wide, out, sems, out_sems):
    pairs = ((target_hbm, target), (weights_hbm, weights), (block_hbm, block), (slot_hbm, slot), (prints_hbm, prints))
    copies = [pltpu.make_async_copy(a, b, sems.at[i]) for i, (a, b) in enumerate(pairs)]
    for copy in copies:
        copy.start()
    e, s, q, k = lanes((1, WIDE), 1)
    base = s * CLON + e
    source = jnp.where(e < PASSES, base + CLON - PASSES, jnp.where(e < EAST, base - PASSES, base - EAST))
    source = jnp.where((e >= 0) & (e < EAST + PASSES), source, -1)
    spread[...] = pick(iota((SPAN, WIDE), 0) == source)
    before = pick(iota((OBS, OBS), 0) < iota((OBS, OBS), 1))
    for copy in copies[:4]:
        copy.wait()
    blk = block[...]
    meta[...] = jnp.zeros_like(meta)
    meta[0:RHS, :] = weights[...].astype(F32)
    meta[4:5, :] = ((blk % DEPTH) * CHUNKS + blk // DEPTH).astype(F32)
    meta[5:6, :] = slot[...].astype(F32)
    facts = meta[...].astype(BF)
    slots = mm(facts, pick(iota((8, 128), 0) == 5), TN).astype(BF)
    t = target[...]
    hit = pick(iota((DEVICES, OBS), 0) == t)
    earlier = mm(hit, before)
    copies[4].wait()
    for s in range(SLOTS):
        live = slots >= jnp.asarray(s, BF)
        piece = prints[:, s * CLON:(s + 1) * CLON]
        masked[:, s * CLON:(s + 1) * CLON] = jnp.where(live, piece, jnp.zeros_like(piece))
    e, s, q, k = lanes((1, WIDE), 1)
    fact = jnp.where((k == 0) & (q < FRONT) & (s < 5), s, -1)
    wide[...] = (mm(masked[...], spread[...]) + mm(facts, pick(iota((8, WIDE), 0) == fact), TN)).astype(BF)
    rank = jnp.sum(hit.astype(F32) * earlier, axis=0, keepdims=True)
    rank_out[...] = jnp.broadcast_to(rank, (8, OBS))
    where = pick(iota((TOTAL, OBS), 0) == t * CAP + rank.astype(jnp.int32))
    e, s, q, k = lanes((1, 1, WIDE), 2)
    from_west = ((e >= 0) & (e < PASSES)) | ((k == 0) & (q == 1))
    from_east = ((e >= EAST) & (e < EAST + PASSES)) | ((k == 0) & (q == 2))
    sends = []
    size = TOTAL // PIECES
    for i in range(PIECES):
        rows = slice(i * size, (i + 1) * size)
        moved = mm(where[rows], wide[...]).reshape(size // (LON * CAP), LON * CAP, WIDE)
        up = jnp.concatenate([moved[:, -CAP:], moved[:, :-CAP]], axis=1)
        down = jnp.concatenate([moved[:, CAP:], moved[:, :CAP]], axis=1)
        result = jnp.where(from_west, up, jnp.where(from_east, down, moved))
        out[rows, :] = result.reshape(size, WIDE).astype(BF)
        sends.append(pltpu.make_async_copy(out.at[rows, :], out_hbm.at[rows, :], out_sems.at[i]))
        sends[-1].start()
    for send in sends:
        send.wait()


def pack(prints, weights, target, block, slot):
    hbm = pl.BlockSpec(memory_space=pltpu.HBM)
    return pl.pallas_call(
        pack_kernel,
        in_specs=[hbm] * 5,
        out_specs=(hbm, pl.BlockSpec(memory_space=pltpu.VMEM)),
        out_shape=(
            jax.ShapeDtypeStruct((TOTAL, WIDE), BF),
            jax.ShapeDtypeStruct((8, OBS), F32),
        ),
        scratch_shapes=[
            pltpu.VMEM((OBS, SPAN), BF),
            pltpu.VMEM((RHS, OBS), BF),
            pltpu.VMEM((1, OBS), jnp.int32),
            pltpu.VMEM((1, OBS), jnp.int32),
            pltpu.VMEM((1, OBS), jnp.int32),
            pltpu.VMEM((OBS, SPAN), BF),
            pltpu.VMEM((8, OBS), F32),
            pltpu.VMEM((SPAN, WIDE), BF),
            pltpu.VMEM((OBS, WIDE), BF),
            pltpu.VMEM((TOTAL, WIDE), BF),
            pltpu.SemaphoreType.DMA((5,)),
            pltpu.SemaphoreType.DMA((PIECES,)),
        ],
        compiler_params=params(60),
        cost_estimate=cost(2 * TOTAL * OBS * SPAN, 3 << 20),
        name="pack",
    )(prints, weights, target, block, slot)


def faces_kernel(own, first, second, coef, over, root, rim, wide):
    e, _, _, _ = lanes((1, WIDE), 1)
    even = lax.axis_index("lon") % 2 == 0

    def place(x, cond, shift):
        one = jnp.where(cond & (iota((CLON, WIDE), 0) == e + shift), 1.0, 0.0)
        return jnp.dot(jnp.sqrt(x), one, precision=lax.Precision.HIGHEST, preferred_element_type=F32)

    left = jnp.where(even, second[...], first[...])
    right = jnp.where(even, first[...], second[...])
    flat = place(own[...], (e >= PASSES) & (e < EAST), -PASSES)
    flat = flat + (place(left, (e >= 0) & (e < PASSES), CLON - PASSES) + place(right, (e >= EAST) & (e < EAST + PASSES), -EAST))
    beyond = jnp.zeros((CHUNKS, 128), F32)
    for q in range(RUN):
        wide[q, :CHUNKS, :] = beyond
        wide[q, CHUNKS:CHUNKS + ROWS, :] = flat[:, q * 128:(q + 1) * 128]
        wide[q, CHUNKS + ROWS:, :] = beyond
    for j in range(RIM):
        rim[j, :RHS, :] = jnp.broadcast_to(flat[j:j + 1], (RHS, WIDE))
        rim[j, RHS:, :] = jnp.broadcast_to(flat[ROWS - 1 - j:ROWS - j], (RHS, WIDE))

    def level(b):
        return [wide[q, pl.ds(CHUNKS + b, CHUNKS, stride=DEPTH), :] for q in range(RUN)]

    south, here = level(-1), level(0)
    for b in range(DEPTH):
        north = level(b + 1)
        ahead, behind = beside(here)
        rows = slice(b * CHUNKS, (b + 1) * CHUNKS)
        for q in range(RUN):
            cols = slice(q * 128, (q + 1) * 128)
            mid = 1.0 - here[q] * ((north[q] + south[q]) + (ahead[q] + behind[q]))
            some = here[q] > 0.0
            coef[0, rows, cols] = mid
            coef[1, rows, cols] = here[q] * here[q]
            over[rows, cols] = jnp.where(some, mid / jnp.where(some, here[q], 1.0), 0.0)
            root[rows, cols] = here[q]
        south, here = here, north


def faces(own, first, second):
    return pl.pallas_call(
        faces_kernel,
        out_shape=(
            jax.ShapeDtypeStruct((2, ROWS, WIDE), F32),
            jax.ShapeDtypeStruct((ROWS, WIDE), F32),
            jax.ShapeDtypeStruct((ROWS, WIDE), F32),
            jax.ShapeDtypeStruct((RIM, 2 * RHS, WIDE), F32),
        ),
        scratch_shapes=[pltpu.VMEM((RUN, ROWS + 2 * CHUNKS, 128), F32)],
        compiler_params=params(12),
        cost_estimate=cost(1 << 30, 6 << 20),
        name="faces",
    )(own, first, second)


def adjoint_kernel(got, roots, field, rim, inner, outer, facts_out):
    column, lane = iota((16, 128), 0), iota((16, 128), 1)
    facts = jnp.zeros((16, TOTAL), F32)
    for i in range(FRONT):
        mine = (lane == column - 5 * i) & (column >= 5 * i) & (column < 5 * i + 5)
        facts = facts + mm(pick(mine), got[:, i * 128:(i + 1) * 128], NT)
    facts_out[...] = facts
    row = iota((ROWS, TOTAL), 0).astype(F32)

    def border(first_tile, first_lane, tile, fact):
        source, lane = iota((PASSES * 128, 128), 0), iota((PASSES * 128, 128), 1)
        take = source == lane % 32 // SLOTS * 128 + first_lane + lane % SLOTS
        cells = mm(got[:, first_tile * 128:(first_tile + PASSES) * 128], pick(take))
        fan = pick(iota((128, 128), 0) == iota((128, 128), 1) // 32)
        cells = cells * mm(got[:, tile * 128:(tile + 1) * 128], fan)
        high = cells.astype(BF)
        low = (cells - high.astype(F32)).astype(BF)
        both = mm(pick(row == facts[fact:fact + 1]), jnp.concatenate([high, low], axis=1))
        return both[:, :128] + both[:, 128:]

    before = border(FRONT, 0, 1, 9)
    after = border(0, 128 - SLOTS, 2, 14)
    mine = row == facts[RHS:RHS + 1]
    lane = iota((1, 128), 1)
    end = FRONT + PASSES
    for r in range(RHS):
        total = mm(jnp.where(mine, facts[r:r + 1], 0.0).astype(BF), got[...])
        for q in range(RUN):
            cols = slice(q * 128, (q + 1) * 128)
            part = total[:, cols]
            if FRONT <= q < end:
                part = jnp.where(lane < SLOTS, rolled(before, -(r * 32 + (q - FRONT) * SLOTS)), part)
            if q < PASSES:
                part = jnp.where(lane >= 128 - SLOTS, rolled(after, -(r * 32 + (q + 1) * SLOTS)), part)
            field[r, :, cols] = part
        for j in range(RIM):
            at = j * CHUNKS
            rim[j, r:r + 1, :] = field[r, at:at + 1, :]
            at = (DEPTH - j) * CHUNKS - 1
            rim[j, RHS + r:RHS + r + 1, :] = field[r, at:at + 1, :]
    for j in range(RIM):
        rim[j] = rim[j] * roots[j]
    even = lax.axis_index("lat") % 2 == 0
    for base, ref in ((0, rim), (PASSES, roots)):
        for j in range(PASSES):
            low, high = ref[j, :RHS, :], ref[j, RHS:, :]
            inner[base + j] = jnp.where(even, high, low)
            outer[base + j] = jnp.where(even, low, high)


def adjoint(got, roots):
    return pl.pallas_call(
        adjoint_kernel,
        out_shape=(
            jax.ShapeDtypeStruct((RHS, ROWS, WIDE), F32),
            jax.ShapeDtypeStruct((RIM, 2 * RHS, WIDE), F32),
            jax.ShapeDtypeStruct((2 * PASSES, RHS, WIDE), F32),
            jax.ShapeDtypeStruct((2 * PASSES, RHS, WIDE), F32),
            jax.ShapeDtypeStruct((16, TOTAL), F32),
        ),
        compiler_params=params(16),
        cost_estimate=cost(5 << 30, 8 << 20),
        name="adjoint",
    )(got, roots)


def inside(q):
    e = (iota((1, 128), 1) // 8) * RUN + q - FRONT
    return (e >= PASSES) & (e < EAST)


def surround(ref, r):
    last = DEPTH * CHUNKS
    ref[r, :CHUNKS, :] = pltpu.roll(ref[r, last:last + CHUNKS, :], 1, 0)
    ref[r, last + CHUNKS:, :] = pltpu.roll(ref[r, CHUNKS:2 * CHUNKS, :], CHUNKS - 1, 0)


def diffuse_kernel(field, coef, over, root, smooth, outer, one, two):
    usual, final = (coef.at[0], coef.at[1]), (over, root)

    def rows_of(e):
        at = e * CHUNKS
        return pl.ds(at if isinstance(at, int) else pl.multiple_of(at, CHUNKS), CHUNKS)

    def two_levels(ref, e, factor, store):
        def load(r, at, q):
            return ref[r, rows_of(at), q * 128:(q + 1) * 128]

        levels = (e, e + 1)
        turned_west = [[rolled(load(r, at, RUN - 1), SLOTS) for at in levels] for r in range(RHS)]
        turned_east = [[rolled(load(r, at, 0), -SLOTS) for at in levels] for r in range(RHS)]
        behind, here = [[[load(r, at, q) for at in levels] for r in range(RHS)] for q in (0, 1)]
        for q in [*range(1, RUN), 0]:
            mid, near = [[kind[rows_of(at - 1), q * 128:(q + 1) * 128] for at in levels] for kind in factor]
            if q == 0:
                behind = turned_west
                here, ahead = [[[load(r, at, i) for at in levels] for r in range(RHS)] for i in (0, 1)]
            elif q + 1 < RUN:
                ahead = [[load(r, at, q + 1) for at in levels] for r in range(RHS)]
            else:
                ahead = turned_east
            for r in range(RHS):
                column = [load(r, e - 1, q)] + here[r] + [load(r, e + 2, q)]
                for i in range(2):
                    total = (column[i + 2] + column[i]) + (ahead[r][i] + behind[r][i])
                    store(r, q, i, mid[i] * here[r][i] + near[i] * total)
            behind, here = here, ahead

    def sweep(ref, target, first, end, factor, to=0):
        def step(pair, _):
            e = first + 2 * pair

            def store(r, q, i, value):
                target[r, rows_of(e + i + to), q * 128:(q + 1) * 128] = value

            two_levels(ref, e, factor, store)
            return 0

        lax.fori_loop(0, (end - first) // 2, step, 0, unroll=2)

    def scale(e, _):
        for q in range(RUN):
            cols = slice(q * 128, (q + 1) * 128)
            factor = root[rows_of(e), cols]
            for r in range(RHS):
                two[r, rows_of(e + 1), cols] = field[r, rows_of(e), cols] * factor
        return 0

    lax.fori_loop(0, DEPTH, scale, 0, unroll=2)
    for r in range(RHS):
        surround(two, r)
    for ref, target in ((two, one), (one, two), (two, one)):
        sweep(ref, target, 1, DEPTH + 1, usual)
        for r in range(RHS):
            surround(target, r)
    sweep(one, outer, 1, PASSES + 1, final, -1)
    sweep(one, outer, DEPTH + 1 - PASSES, DEPTH + 1, final, 2 * PASSES - 1 - DEPTH)

    def rounded(pair, _):
        first = {}

        def store(r, q, i, value):
            if i == 0:
                first[r, q] = value
                return
            both = jnp.concatenate([first.pop((r, q)), value], axis=0)
            at = pl.ds(pl.multiple_of(pair * 2 * CHUNKS, 2 * CHUNKS), 2 * CHUNKS)
            smooth[r, at, q * 128:(q + 1) * 128] = jnp.where(inside(q), both, 0.0).astype(BF)

        two_levels(one, PASSES + 1 + 2 * pair, final, store)
        return 0

    lax.fori_loop(0, MIDDLE // (2 * CHUNKS), rounded, 0, unroll=2)


def diffuse(field, coef, over, root):
    return pl.pallas_call(
        diffuse_kernel,
        out_shape=(
            jax.ShapeDtypeStruct((RHS, MIDDLE, WIDE), BF),
            jax.ShapeDtypeStruct((RHS, OUTER, WIDE), F32),
        ),
        scratch_shapes=[
            pltpu.VMEM((RHS, TALL * CHUNKS, WIDE), F32),
            pltpu.VMEM((RHS, TALL * CHUNKS, WIDE), F32),
        ],
        compiler_params=params(14),
        cost_estimate=cost(6 << 30, 8 << 20),
        name="diffuse",
    )(field, coef, over, root)


def finish_kernel(smooth, outer, rim, roots, inner, beyond, got, facts, out, border, values):
    even = lax.axis_index("lat") % 2 == 0

    def levels(base, own):
        rows = []
        for j in range(base + PASSES - 1, base - 1, -1):
            south = jnp.where(even, beyond[j], inner[j])
            north = jnp.where(even, inner[j], beyond[j])
            rows.append(jnp.concatenate([south, north], axis=0))
        return [[x[:, q * 128:(q + 1) * 128] for q in range(RUN)] for x in rows + [own[j] for j in range(RIM)]]

    def around(x, j):
        ahead, behind = beside(x[j])
        return [(x[j + 1][q] + x[j - 1][q]) + (ahead[q] + behind[q]) for q in range(RUN)]

    v, root = levels(0, rim), levels(PASSES, roots)
    count = PASSES + RIM
    mid = [None] + [[1.0 - x * y for x, y in zip(root[j], around(root, j))] for j in range(1, count - 1)]
    for step in range(1, PASSES + 1):
        new = list(v)
        for j in range(step, count - step):
            total = around(v, j)
            new[j] = [mid[j][q] * v[j][q] + (root[j][q] * root[j][q]) * total[q] for q in range(RUN)]
        v = new
    for j in range(PASSES, 2 * PASSES):
        some = [x > 0.0 for x in root[j]]
        v[j] = [jnp.where(some[q], v[j][q] / jnp.where(some[q], root[j][q], 1.0), 0.0) for q in range(RUN)]
    sub = iota((CHUNKS, 1), 0)
    for r in range(RHS):
        for q in range(RUN):
            cols = slice(q * 128, (q + 1) * 128)
            for pair in range(PASSES):
                both = []
                for b in (2 * pair, 2 * pair + 1):
                    here = outer[r, b * CHUNKS:(b + 1) * CHUNKS, cols]
                    if b < PASSES:
                        here = jnp.where(sub == 0, v[PASSES + b][q][r:r + 1], here)
                    else:
                        j = PASSES + 2 * PASSES - 1 - b
                        here = jnp.where(sub == CHUNKS - 1, v[j][q][RHS + r:RHS + r + 1], here)
                    both.append(here)
                both = jnp.where(inside(q), jnp.concatenate(both, axis=0), 0.0).astype(BF)
                border[r, pair * 2 * CHUNKS:(pair + 1) * 2 * CHUNKS, cols] = both

    side = PASSES * CHUNKS
    chosen = iota((ROWS, TOTAL), 0).astype(F32) == facts[RHS:RHS + 1, :]
    total = [0.0] * RHS
    for ref, spans in ((smooth, ((side, MIDDLE),)), (border, ((0, side), (ROWS - side, side)))):
        shares = mm(ref[...].reshape(-1, WIDE), got[...], NT)
        at = 0
        for r in range(RHS):
            for first, size in spans:
                part = jnp.where(chosen[first:first + size], shares[at:at + size], 0.0)
                total[r] = total[r] + jnp.sum(part, axis=0, keepdims=True)
                at += size
    for r in range(RHS):
        values[r:r + 1, :] = total[r]
        values[RHS + r:RHS + r + 1, :] = total[r]
    both = values[...]
    turn = iota((2 * RHS, TOTAL), 0) // RHS
    keep = [jnp.where(iota((2 * RHS, TOTAL), 1) % CAP == turn + 2 * i, 1.0, 0.0) for i in range(CAP // 2)]
    many = [part.astype(F32) * k for part in thirds(both) for k in keep]
    owner = pick(iota((DEVICES, TOTAL), 1) // CAP == iota((DEVICES, TOTAL), 0))
    sums = mm(owner, jnp.concatenate(many, axis=0).astype(BF), NT)
    size = CAP * RHS
    out[...] = jnp.zeros_like(out)
    out[:, :size] = (sums[:, :size] + sums[:, size:2 * size]) + sums[:, 2 * size:3 * size]


def finish(smooth, outer, rim, roots, inner, beyond, got, facts):
    return pl.pallas_call(
        finish_kernel,
        out_shape=jax.ShapeDtypeStruct((DEVICES, 128), F32),
        scratch_shapes=[
            pltpu.VMEM((RHS, OUTER, WIDE), BF),
            pltpu.VMEM((8, TOTAL), F32),
        ],
        compiler_params=params(16),
        cost_estimate=cost(3 << 30, 10 << 20),
        name="finish",
    )(smooth, outer, rim, roots, inner, beyond, got, facts)


def unpack_kernel(values, target, rank, out):
    hit = pick(iota((DEVICES, OBS), 0) == target[...])
    total = jnp.zeros((CAP * RHS, OBS), F32)
    for part in thirds(values[:, :CAP * RHS]):
        total = total + mm(part, hit, TN)
    total = jnp.where((iota((CAP * RHS, OBS), 0) // RHS).astype(F32) == rank[0:1, :], total, 0.0)
    pair = (total[0:8] + total[8:16]) + (total[16:24] + total[24:32])
    out[...] = pair[0:RHS] + pair[RHS:]


def unpack(values, target, rank):
    return pl.pallas_call(
        unpack_kernel,
        out_shape=jax.ShapeDtypeStruct((RHS, OBS), F32),
        compiler_params=params(8),
        name="unpack",
    )(values, target, rank)


def swap(x, axis, second, closed):
    count = lax.axis_size(axis)
    pairs = [(i, (i + 1) % count) for i in range(int(second), count, 2) if closed or i + 1 < count]
    return lax.ppermute(x, axis, pairs + [(j, i) for i, j in pairs])


def body(footprints, dual_weights, target_device, target_block, obs_slot, diffusivity):
    target = target_device.reshape(1, OBS)
    packed, rank = pack(footprints, dual_weights.T, target, target_block.reshape(1, OBS), obs_slot.reshape(1, OBS))
    first = swap(diffusivity, "lon", False, True)
    second = swap(diffusivity, "lon", True, True)
    packed, first, second = lax.optimization_barrier((packed, first, second))
    coef, over, root, roots = faces(diffusivity, first, second)
    got = lax.all_to_all(packed, ("lat", "lon"), split_axis=0, concat_axis=0, tiled=True)
    field, rim, inner, beyond, facts = adjoint(got, roots)
    inner = swap(inner, "lat", False, False)
    beyond = swap(beyond, "lat", True, False)
    smooth, outer = diffuse(field, coef, over, root)
    values = finish(smooth, outer, rim, roots, inner, beyond, got, facts)
    returned = lax.all_to_all(values, ("lat", "lon"), split_axis=0, concat_axis=0, tiled=True)
    return unpack(returned, target, rank).T


def solution(mesh):
    placed = (
        P(("lat", "lon"), None),
        P(("lat", "lon"), None),
        P(("lat", "lon"), None),
        P(("lat", "lon")),
        P(("lat", "lon")),
        P("lat", "lon"),
    )
    return jax.shard_map(
        body, mesh=mesh, in_specs=placed, out_specs=P(("lat", "lon"), None), check_vma=False
    )
```

```python
import jax
import jax.numpy as jnp
from jax import lax
from jax.experimental import pallas as pl
from jax.experimental.pallas import tpu as pltpu
from jax.sharding import PartitionSpec as P

SLOTS = 8
CLON = 128
PASSES = 4
RHS = 4
OBS = 512
CAP = 8
DEVICES = 128
LON = 16
ROWS = 256
CHUNKS = 8
DEPTH = ROWS // CHUNKS
TALL = DEPTH + 2
RUN = 9
FRONT = 3
SPAN = SLOTS * CLON
WIDE = RUN * 128
EAST = CLON + PASSES
TOTAL = DEVICES * CAP
RIM = 2 * PASSES
OUTER = 2 * PASSES * CHUNKS
MIDDLE = ROWS - OUTER
BF = jnp.bfloat16
F32 = jnp.float32
NT = ((1,), (1,))
TN = ((0,), (0,))


def iota(shape, dim):
    return lax.broadcasted_iota(jnp.int32, shape, dim)


def pick(cond):
    return jnp.where(cond, 1.0, 0.0).astype(BF)


def mm(a, b, dims=((1,), (0,))):
    return lax.dot_general(a, b, (dims, ((), ())), preferred_element_type=F32)


def thirds(x):
    hi = x.astype(BF)
    rest = x - hi.astype(F32)
    mid = rest.astype(BF)
    return hi, mid, (rest - mid.astype(F32)).astype(BF)


def params(mib):
    return pltpu.CompilerParams(vmem_limit_bytes=mib * 1024 * 1024)


def cost(flops, size):
    return pl.CostEstimate(flops=flops, bytes_accessed=size, transcendentals=0)


def lanes(shape, dim):
    lane = iota(shape, dim)
    q, k, s = lane // 128, lane % 128 // 8, lane % 8
    return k * RUN + q - FRONT, s, q, k


def rolled(x, step):
    return pltpu.roll(x, step % 128, 1)


def beside(row):
    return row[1:] + [rolled(row[0], -SLOTS)], [rolled(row[-1], SLOTS)] + row[:-1]


PIECES = 4


def pack_kernel(prints_hbm, weights_hbm, target_hbm, block_hbm, slot_hbm, out_hbm, rank_out,
                prints, weights, target, block, slot, masked, meta, spread, wide, out, sems, out_sems):
    pairs = ((target_hbm, target), (weights_hbm, weights), (block_hbm, block), (slot_hbm, slot), (prints_hbm, prints))
    copies = [pltpu.make_async_copy(a, b, sems.at[i]) for i, (a, b) in enumerate(pairs)]
    for copy in copies:
        copy.start()
    e, s, q, k = lanes((1, WIDE), 1)
    base = s * CLON + e
    source = jnp.where(e < PASSES, base + CLON - PASSES, jnp.where(e < EAST, base - PASSES, base - EAST))
    source = jnp.where((e >= 0) & (e < EAST + PASSES), source, -1)
    spread[...] = pick(iota((SPAN, WIDE), 0) == source)
    before = pick(iota((OBS, OBS), 0) < iota((OBS, OBS), 1))
    for copy in copies[:4]:
        copy.wait()
    blk = block[...]
    meta[...] = jnp.zeros_like(meta)
    meta[0:RHS, :] = weights[...].astype(F32)
    meta[4:5, :] = ((blk % DEPTH) * CHUNKS + blk // DEPTH).astype(F32)
    meta[5:6, :] = slot[...].astype(F32)
    facts = meta[...].astype(BF)
    slots = mm(facts, pick(iota((8, 128), 0) == 5), TN).astype(BF)
    t = target[...]
    hit = pick(iota((DEVICES, OBS), 0) == t)
    earlier = mm(hit, before)
    copies[4].wait()
    for s in range(SLOTS):
        live = slots >= jnp.asarray(s, BF)
        piece = prints[:, s * CLON:(s + 1) * CLON]
        masked[:, s * CLON:(s + 1) * CLON] = jnp.where(live, piece, jnp.zeros_like(piece))
    e, s, q, k = lanes((1, WIDE), 1)
    fact = jnp.where((k == 0) & (q < FRONT) & (s < 5), s, -1)
    wide[...] = (mm(masked[...], spread[...]) + mm(facts, pick(iota((8, WIDE), 0) == fact), TN)).astype(BF)
    rank = jnp.sum(hit.astype(F32) * earlier, axis=0, keepdims=True)
    rank_out[...] = jnp.broadcast_to(rank, (8, OBS))
    where = pick(iota((TOTAL, OBS), 0) == t * CAP + rank.astype(jnp.int32))
    e, s, q, k = lanes((1, 1, WIDE), 2)
    from_west = ((e >= 0) & (e < PASSES)) | ((k == 0) & (q == 1))
    from_east = ((e >= EAST) & (e < EAST + PASSES)) | ((k == 0) & (q == 2))
    sends = []
    size = TOTAL // PIECES
    for i in range(PIECES):
        rows = slice(i * size, (i + 1) * size)
        moved = mm(where[rows], wide[...]).reshape(size // (LON * CAP), LON * CAP, WIDE)
        up = jnp.concatenate([moved[:, -CAP:], moved[:, :-CAP]], axis=1)
        down = jnp.concatenate([moved[:, CAP:], moved[:, :CAP]], axis=1)
        result = jnp.where(from_west, up, jnp.where(from_east, down, moved))
        out[rows, :] = result.reshape(size, WIDE).astype(BF)
        sends.append(pltpu.make_async_copy(out.at[rows, :], out_hbm.at[rows, :], out_sems.at[i]))
        sends[-1].start()
    for send in sends:
        send.wait()


def pack(prints, weights, target, block, slot):
    hbm = pl.BlockSpec(memory_space=pltpu.HBM)
    return pl.pallas_call(
        pack_kernel,
        in_specs=[hbm] * 5,
        out_specs=(hbm, pl.BlockSpec(memory_space=pltpu.VMEM)),
        out_shape=(
            jax.ShapeDtypeStruct((TOTAL, WIDE), BF),
            jax.ShapeDtypeStruct((8, OBS), F32),
        ),
        scratch_shapes=[
            pltpu.VMEM((OBS, SPAN), BF),
            pltpu.VMEM((RHS, OBS), BF),
            pltpu.VMEM((1, OBS), jnp.int32),
            pltpu.VMEM((1, OBS), jnp.int32),
            pltpu.VMEM((1, OBS), jnp.int32),
            pltpu.VMEM((OBS, SPAN), BF),
            pltpu.VMEM((8, OBS), F32),
            pltpu.VMEM((SPAN, WIDE), BF),
            pltpu.VMEM((OBS, WIDE), BF),
            pltpu.VMEM((TOTAL, WIDE), BF),
            pltpu.SemaphoreType.DMA((5,)),
            pltpu.SemaphoreType.DMA((PIECES,)),
        ],
        compiler_params=params(60),
        cost_estimate=cost(2 * TOTAL * OBS * SPAN, 3 << 20),
        name="pack",
    )(prints, weights, target, block, slot)


def faces_kernel(own, first, second, coef, over, root, rim, wide):
    e, _, _, _ = lanes((1, WIDE), 1)
    even = lax.axis_index("lon") % 2 == 0

    def place(x, cond, shift):
        one = jnp.where(cond & (iota((CLON, WIDE), 0) == e + shift), 1.0, 0.0)
        return jnp.dot(jnp.sqrt(x), one, precision=lax.Precision.HIGHEST, preferred_element_type=F32)

    left = jnp.where(even, second[...], first[...])
    right = jnp.where(even, first[...], second[...])
    flat = place(own[...], (e >= PASSES) & (e < EAST), -PASSES)
    flat = flat + (place(left, (e >= 0) & (e < PASSES), CLON - PASSES) + place(right, (e >= EAST) & (e < EAST + PASSES), -EAST))
    beyond = jnp.zeros((CHUNKS, 128), F32)
    for q in range(RUN):
        wide[q, :CHUNKS, :] = beyond
        wide[q, CHUNKS:CHUNKS + ROWS, :] = flat[:, q * 128:(q + 1) * 128]
        wide[q, CHUNKS + ROWS:2 * CHUNKS + ROWS, :] = beyond
    for j in range(RIM):
        rim[j, :RHS, :] = jnp.broadcast_to(flat[j:j + 1], (RHS, WIDE))
        rim[j, RHS:, :] = jnp.broadcast_to(flat[ROWS - 1 - j:ROWS - j], (RHS, WIDE))

    def level(b):
        return [wide[q, pl.ds(CHUNKS + b, CHUNKS, stride=DEPTH), :] for q in range(RUN)]

    south, here = level(-1), level(0)
    for b in range(DEPTH):
        north = level(b + 1)
        ahead, behind = beside(here)
        rows = slice(b * CHUNKS, (b + 1) * CHUNKS)
        for q in range(RUN):
            cols = slice(q * 128, (q + 1) * 128)
            mid = 1.0 - here[q] * ((north[q] + south[q]) + (ahead[q] + behind[q]))
            some = here[q] > 0.0
            coef[0, rows, cols] = mid
            coef[1, rows, cols] = here[q] * here[q]
            over[rows, cols] = jnp.where(some, mid / jnp.where(some, here[q], 1.0), 0.0)
            root[rows, cols] = here[q]
        south, here = here, north


def faces(own, first, second):
    return pl.pallas_call(
        faces_kernel,
        out_shape=(
            jax.ShapeDtypeStruct((2, ROWS, WIDE), F32),
            jax.ShapeDtypeStruct((ROWS, WIDE), F32),
            jax.ShapeDtypeStruct((ROWS, WIDE), F32),
            jax.ShapeDtypeStruct((RIM, 2 * RHS, WIDE), F32),
        ),
        scratch_shapes=[pltpu.VMEM((RUN, ROWS + 2 * CHUNKS + DEPTH, 128), F32)],
        compiler_params=params(12),
        cost_estimate=cost(1 << 30, 6 << 20),
        name="faces",
    )(own, first, second)


def adjoint_kernel(got, roots, field, rim, inner, outer, facts_out):
    column, lane = iota((16, 128), 0), iota((16, 128), 1)
    facts = jnp.zeros((16, TOTAL), F32)
    for i in range(FRONT):
        mine = (lane == column - 5 * i) & (column >= 5 * i) & (column < 5 * i + 5)
        facts = facts + mm(pick(mine), got[:, i * 128:(i + 1) * 128], NT)
    facts_out[...] = facts
    row = iota((ROWS, TOTAL), 0).astype(F32)

    def border(first_tile, first_lane, tile, fact):
        source, lane = iota((PASSES * 128, 128), 0), iota((PASSES * 128, 128), 1)
        take = source == lane % 32 // SLOTS * 128 + first_lane + lane % SLOTS
        cells = mm(got[:, first_tile * 128:(first_tile + PASSES) * 128], pick(take))
        fan = pick(iota((128, 128), 0) == iota((128, 128), 1) // 32)
        cells = cells * mm(got[:, tile * 128:(tile + 1) * 128], fan)
        high = cells.astype(BF)
        low = (cells - high.astype(F32)).astype(BF)
        both = mm(pick(row == facts[fact:fact + 1]), jnp.concatenate([high, low], axis=1))
        return both[:, :128] + both[:, 128:]

    before = border(FRONT, 0, 1, 9)
    after = border(0, 128 - SLOTS, 2, 14)
    mine = row == facts[RHS:RHS + 1]
    lane = iota((1, 128), 1)
    end = FRONT + PASSES
    for r in range(RHS):
        total = mm(jnp.where(mine, facts[r:r + 1], 0.0).astype(BF), got[...])
        for q in range(RUN):
            cols = slice(q * 128, (q + 1) * 128)
            part = total[:, cols]
            if FRONT <= q < end:
                part = jnp.where(lane < SLOTS, rolled(before, -(r * 32 + (q - FRONT) * SLOTS)), part)
            if q < PASSES:
                part = jnp.where(lane >= 128 - SLOTS, rolled(after, -(r * 32 + (q + 1) * SLOTS)), part)
            field[r, :, cols] = part
        for j in range(RIM):
            at = j * CHUNKS
            rim[j, r:r + 1, :] = field[r, at:at + 1, :]
            at = (DEPTH - j) * CHUNKS - 1
            rim[j, RHS + r:RHS + r + 1, :] = field[r, at:at + 1, :]
    for j in range(RIM):
        rim[j] = rim[j] * roots[j]
    even = lax.axis_index("lat") % 2 == 0
    for base, ref in ((0, rim), (PASSES, roots)):
        for j in range(PASSES):
            low, high = ref[j, :RHS, :], ref[j, RHS:, :]
            inner[base + j] = jnp.where(even, high, low)
            outer[base + j] = jnp.where(even, low, high)


def adjoint(got, roots):
    return pl.pallas_call(
        adjoint_kernel,
        out_shape=(
            jax.ShapeDtypeStruct((RHS, ROWS, WIDE), F32),
            jax.ShapeDtypeStruct((RIM, 2 * RHS, WIDE), F32),
            jax.ShapeDtypeStruct((2 * PASSES, RHS, WIDE), F32),
            jax.ShapeDtypeStruct((2 * PASSES, RHS, WIDE), F32),
            jax.ShapeDtypeStruct((16, TOTAL), F32),
        ),
        compiler_params=params(16),
        cost_estimate=cost(5 << 30, 8 << 20),
        name="adjoint",
    )(got, roots)


def inside(q):
    e = (iota((1, 128), 1) // 8) * RUN + q - FRONT
    return (e >= PASSES) & (e < EAST)


def surround(ref, r):
    last = DEPTH * CHUNKS
    ref[r, :CHUNKS, :] = pltpu.roll(ref[r, last:last + CHUNKS, :], 1, 0)
    ref[r, last + CHUNKS:, :] = pltpu.roll(ref[r, CHUNKS:2 * CHUNKS, :], CHUNKS - 1, 0)


def diffuse_kernel(field, coef, over, root, smooth, outer, one, two):
    usual, final = (coef.at[0], coef.at[1]), (over, root)

    def rows_of(e):
        at = e * CHUNKS
        return pl.ds(at if isinstance(at, int) else pl.multiple_of(at, CHUNKS), CHUNKS)

    def some_levels(ref, e, factor, store, count):
        def load(r, at, q):
            return ref[r, rows_of(at), q * 128:(q + 1) * 128]

        levels = tuple(e + i for i in range(count))
        for group in ((0, 1), (2, 3)):
            turned_west = {r: [rolled(load(r, at, RUN - 1), SLOTS) for at in levels] for r in group}
            turned_east = {r: [rolled(load(r, at, 0), -SLOTS) for at in levels] for r in group}
            behind, here = [{r: [load(r, at, q) for at in levels] for r in group} for q in (0, 1)]
            for q in [*range(1, RUN), 0]:
                mid, near = [[kind[rows_of(at - 1), q * 128:(q + 1) * 128] for at in levels] for kind in factor]
                if q == 0:
                    behind = turned_west
                    here, ahead = [{r: [load(r, at, i) for at in levels] for r in group} for i in (0, 1)]
                elif q + 1 < RUN:
                    ahead = {r: [load(r, at, q + 1) for at in levels] for r in group}
                else:
                    ahead = turned_east
                for r in group:
                    column = [load(r, e - 1, q)] + here[r] + [load(r, e + count, q)]
                    for i in range(count):
                        total = (column[i + 2] + column[i]) + (ahead[r][i] + behind[r][i])
                        store(r, q, i, mid[i] * here[r][i] + near[i] * total)
                behind, here = here, ahead

    def sweep(ref, target, first, end, factor, to=0):
        def step(pair, _):
            e = first + 4 * pair

            def store(r, q, i, value):
                target[r, rows_of(e + i + to), q * 128:(q + 1) * 128] = value

            some_levels(ref, e, factor, store, 4)
            return 0

        lax.fori_loop(0, (end - first) // 4, step, 0)

    def scale(e, _):
        for q in range(RUN):
            cols = slice(q * 128, (q + 1) * 128)
            factor = root[rows_of(e), cols]
            for r in range(RHS):
                two[r, rows_of(e + 1), cols] = field[r, rows_of(e), cols] * factor
        return 0

    lax.fori_loop(0, DEPTH, scale, 0, unroll=2)
    for r in range(RHS):
        surround(two, r)
    for ref, target in ((two, one), (one, two), (two, one)):
        sweep(ref, target, 1, DEPTH + 1, usual)
        for r in range(RHS):
            surround(target, r)
    sweep(one, outer, 1, PASSES + 1, final, -1)
    sweep(one, outer, DEPTH + 1 - PASSES, DEPTH + 1, final, 2 * PASSES - 1 - DEPTH)

    def rounded(pair, _):
        first = {}

        def store(r, q, i, value):
            if i == 0:
                first[r, q] = value
                return
            both = jnp.concatenate([first.pop((r, q)), value], axis=0)
            at = pl.ds(pl.multiple_of(pair * 2 * CHUNKS, 2 * CHUNKS), 2 * CHUNKS)
            smooth[r, at, q * 128:(q + 1) * 128] = jnp.where(inside(q), both, 0.0).astype(BF)

        some_levels(one, PASSES + 1 + 2 * pair, final, store, 2)
        return 0

    lax.fori_loop(0, MIDDLE // (2 * CHUNKS), rounded, 0, unroll=2)


def diffuse(field, coef, over, root):
    return pl.pallas_call(
        diffuse_kernel,
        out_shape=(
            jax.ShapeDtypeStruct((RHS, MIDDLE, WIDE), BF),
            jax.ShapeDtypeStruct((RHS, OUTER, WIDE), F32),
        ),
        scratch_shapes=[
            pltpu.VMEM((RHS, TALL * CHUNKS, WIDE), F32),
            pltpu.VMEM((RHS, TALL * CHUNKS, WIDE), F32),
        ],
        compiler_params=params(14),
        cost_estimate=cost(6 << 30, 8 << 20),
        name="diffuse",
    )(field, coef, over, root)


def finish_kernel(smooth, outer, rim, roots, inner, beyond, got, facts, out, border, values):
    even = lax.axis_index("lat") % 2 == 0

    def levels(base, own):
        rows = []
        for j in range(base + PASSES - 1, base - 1, -1):
            south = jnp.where(even, beyond[j], inner[j])
            north = jnp.where(even, inner[j], beyond[j])
            rows.append(jnp.concatenate([south, north], axis=0))
        return [[x[:, q * 128:(q + 1) * 128] for q in range(RUN)] for x in rows + [own[j] for j in range(RIM)]]

    def around(x, j):
        ahead, behind = beside(x[j])
        return [(x[j + 1][q] + x[j - 1][q]) + (ahead[q] + behind[q]) for q in range(RUN)]

    v, root = levels(0, rim), levels(PASSES, roots)
    count = PASSES + RIM
    mid = [None] + [[1.0 - x * y for x, y in zip(root[j], around(root, j))] for j in range(1, count - 1)]
    for step in range(1, PASSES + 1):
        new = list(v)
        for j in range(step, count - step):
            total = around(v, j)
            new[j] = [mid[j][q] * v[j][q] + (root[j][q] * root[j][q]) * total[q] for q in range(RUN)]
        v = new
    for j in range(PASSES, 2 * PASSES):
        some = [x > 0.0 for x in root[j]]
        v[j] = [jnp.where(some[q], v[j][q] / jnp.where(some[q], root[j][q], 1.0), 0.0) for q in range(RUN)]
    sub = iota((CHUNKS, 1), 0)
    for r in range(RHS):
        for q in range(RUN):
            cols = slice(q * 128, (q + 1) * 128)
            for pair in range(PASSES):
                both = []
                for b in (2 * pair, 2 * pair + 1):
                    here = outer[r, b * CHUNKS:(b + 1) * CHUNKS, cols]
                    if b < PASSES:
                        here = jnp.where(sub == 0, v[PASSES + b][q][r:r + 1], here)
                    else:
                        j = PASSES + 2 * PASSES - 1 - b
                        here = jnp.where(sub == CHUNKS - 1, v[j][q][RHS + r:RHS + r + 1], here)
                    both.append(here)
                both = jnp.where(inside(q), jnp.concatenate(both, axis=0), 0.0).astype(BF)
                border[r, pair * 2 * CHUNKS:(pair + 1) * 2 * CHUNKS, cols] = both

    side = PASSES * CHUNKS
    chosen = iota((ROWS, TOTAL), 0).astype(F32) == facts[RHS:RHS + 1, :]
    total = [0.0] * RHS
    for ref, spans in ((smooth, ((side, MIDDLE),)), (border, ((0, side), (ROWS - side, side)))):
        shares = mm(ref[...].reshape(-1, WIDE), got[...], NT)
        at = 0
        for r in range(RHS):
            for first, size in spans:
                part = jnp.where(chosen[first:first + size], shares[at:at + size], 0.0)
                total[r] = total[r] + jnp.sum(part, axis=0, keepdims=True)
                at += size
    for r in range(RHS):
        values[r:r + 1, :] = total[r]
        values[RHS + r:RHS + r + 1, :] = total[r]
    both = values[...]
    turn = iota((2 * RHS, TOTAL), 0) // RHS
    keep = [jnp.where(iota((2 * RHS, TOTAL), 1) % CAP == turn + 2 * i, 1.0, 0.0) for i in range(CAP // 2)]
    many = [part.astype(F32) * k for part in thirds(both) for k in keep]
    owner = pick(iota((DEVICES, TOTAL), 1) // CAP == iota((DEVICES, TOTAL), 0))
    sums = mm(owner, jnp.concatenate(many, axis=0).astype(BF), NT)
    size = CAP * RHS
    out[...] = jnp.zeros_like(out)
    out[:, :size] = (sums[:, :size] + sums[:, size:2 * size]) + sums[:, 2 * size:3 * size]


def finish(smooth, outer, rim, roots, inner, beyond, got, facts):
    return pl.pallas_call(
        finish_kernel,
        out_shape=jax.ShapeDtypeStruct((DEVICES, 128), F32),
        scratch_shapes=[
            pltpu.VMEM((RHS, OUTER, WIDE), BF),
            pltpu.VMEM((8, TOTAL), F32),
        ],
        compiler_params=params(16),
        cost_estimate=cost(3 << 30, 10 << 20),
        name="finish",
    )(smooth, outer, rim, roots, inner, beyond, got, facts)


def unpack_kernel(values, target, rank, out):
    hit = pick(iota((DEVICES, OBS), 0) == target[...])
    total = jnp.zeros((CAP * RHS, OBS), F32)
    for part in thirds(values[:, :CAP * RHS]):
        total = total + mm(part, hit, TN)
    total = jnp.where((iota((CAP * RHS, OBS), 0) // RHS).astype(F32) == rank[0:1, :], total, 0.0)
    pair = (total[0:8] + total[8:16]) + (total[16:24] + total[24:32])
    out[...] = pair[0:RHS] + pair[RHS:]


def unpack(values, target, rank):
    return pl.pallas_call(
        unpack_kernel,
        out_shape=jax.ShapeDtypeStruct((RHS, OBS), F32),
        compiler_params=params(8),
        name="unpack",
    )(values, target, rank)


def swap(x, axis, second, closed):
    count = lax.axis_size(axis)
    pairs = [(i, (i + 1) % count) for i in range(int(second), count, 2) if closed or i + 1 < count]
    return lax.ppermute(x, axis, pairs + [(j, i) for i, j in pairs])


def body(footprints, dual_weights, target_device, target_block, obs_slot, diffusivity):
    target = target_device.reshape(1, OBS)
    packed, rank = pack(footprints, dual_weights.T, target, target_block.reshape(1, OBS), obs_slot.reshape(1, OBS))
    first = swap(diffusivity, "lon", False, True)
    second = swap(diffusivity, "lon", True, True)
    packed, first, second = lax.optimization_barrier((packed, first, second))
    coef, over, root, roots = faces(diffusivity, first, second)
    got = lax.all_to_all(packed, ("lat", "lon"), split_axis=0, concat_axis=0, tiled=True)
    field, rim, inner, beyond, facts = adjoint(got, roots)
    inner = swap(inner, "lat", False, False)
    beyond = swap(beyond, "lat", True, False)
    smooth, outer = diffuse(field, coef, over, root)
    values = finish(smooth, outer, rim, roots, inner, beyond, got, facts)
    returned = lax.all_to_all(values, ("lat", "lon"), split_axis=0, concat_axis=0, tiled=True)
    return unpack(returned, target, rank).T


def solution(mesh):
    placed = (
        P(("lat", "lon"), None),
        P(("lat", "lon"), None),
        P(("lat", "lon"), None),
        P(("lat", "lon")),
        P(("lat", "lon")),
        P("lat", "lon"),
    )
    return jax.shard_map(
        body, mesh=mesh, in_specs=placed, out_specs=P(("lat", "lon"), None), check_vma=False
    )
```

```python
import jax
import jax.numpy as jnp
from jax import lax
from jax.experimental import pallas as pl
from jax.experimental.pallas import tpu as pltpu
from jax.sharding import PartitionSpec as P

SLOTS = 8
CLON = 128
PASSES = 4
RHS = 4
OBS = 512
CAP = 8
DEVICES = 128
LON = 16
ROWS = 256
CHUNKS = 8
DEPTH = ROWS // CHUNKS
TALL = DEPTH + 2
RUN = 9
FRONT = 3
SPAN = SLOTS * CLON
WIDE = RUN * 128
EAST = CLON + PASSES
TOTAL = DEVICES * CAP
RIM = 2 * PASSES
OUTER = 2 * PASSES * CHUNKS
MIDDLE = ROWS - OUTER
BF = jnp.bfloat16
F32 = jnp.float32
NT = ((1,), (1,))
TN = ((0,), (0,))


def iota(shape, dim):
    return lax.broadcasted_iota(jnp.int32, shape, dim)


def pick(cond):
    return jnp.where(cond, 1.0, 0.0).astype(BF)


def mm(a, b, dims=((1,), (0,))):
    return lax.dot_general(a, b, (dims, ((), ())), preferred_element_type=F32)


def thirds(x):
    hi = x.astype(BF)
    rest = x - hi.astype(F32)
    mid = rest.astype(BF)
    return hi, mid, (rest - mid.astype(F32)).astype(BF)


def params(mib):
    return pltpu.CompilerParams(vmem_limit_bytes=mib * 1024 * 1024)


def cost(flops, size):
    return pl.CostEstimate(flops=flops, bytes_accessed=size, transcendentals=0)


def lanes(shape, dim):
    lane = iota(shape, dim)
    q, k, s = lane // 128, lane % 128 // 8, lane % 8
    return k * RUN + q - FRONT, s, q, k


def rolled(x, step):
    return pltpu.roll(x, step % 128, 1)


def beside(row):
    return row[1:] + [rolled(row[0], -SLOTS)], [rolled(row[-1], SLOTS)] + row[:-1]


PIECES = 8


def pack_kernel(prints_hbm, weights_hbm, target_hbm, block_hbm, slot_hbm, out_hbm, rank_out,
                prints, weights, target, block, slot, masked, meta, spread, wide, out, sems, out_sems):
    pairs = ((target_hbm, target), (weights_hbm, weights), (block_hbm, block), (slot_hbm, slot), (prints_hbm, prints))
    copies = [pltpu.make_async_copy(a, b, sems.at[i]) for i, (a, b) in enumerate(pairs[:4])]
    parts = [slice(i * OBS // 2, (i + 1) * OBS // 2) for i in range(2)]
    for i, part in enumerate(parts):
        copies.append(pltpu.make_async_copy(prints_hbm.at[part, :], prints.at[part, :], sems.at[4 + i]))
    for copy in copies:
        copy.start()
    e, s, q, k = lanes((1, WIDE), 1)
    base = s * CLON + e
    source = jnp.where(e < PASSES, base + CLON - PASSES, jnp.where(e < EAST, base - PASSES, base - EAST))
    source = jnp.where((e >= 0) & (e < EAST + PASSES), source, -1)
    spread[...] = pick(iota((SPAN, WIDE), 0) == source)
    before = pick(iota((OBS, OBS), 0) < iota((OBS, OBS), 1))
    for copy in copies[:4]:
        copy.wait()
    blk = block[...]
    meta[...] = jnp.zeros_like(meta)
    meta[0:RHS, :] = weights[...].astype(F32)
    meta[4:5, :] = ((blk % DEPTH) * CHUNKS + blk // DEPTH).astype(F32)
    meta[5:6, :] = slot[...].astype(F32)
    facts = meta[...].astype(BF)
    slots = mm(facts, pick(iota((8, 128), 0) == 5), TN).astype(BF)
    t = target[...]
    hit = pick(iota((DEVICES, OBS), 0) == t)
    earlier = mm(hit, before)
    e, s, q, k = lanes((1, WIDE), 1)
    fact = jnp.where((k == 0) & (q < FRONT) & (s < 5), s, -1)
    extra = mm(facts, pick(iota((8, WIDE), 0) == fact), TN)
    for copy, part in zip(copies[4:], parts):
        copy.wait()
        for s in range(SLOTS):
            live = slots[part] >= jnp.asarray(s, BF)
            piece = prints[part, s * CLON:(s + 1) * CLON]
            masked[part, s * CLON:(s + 1) * CLON] = jnp.where(live, piece, jnp.zeros_like(piece))
        wide[part, :] = (mm(masked[part, :], spread[...]) + extra[part]).astype(BF)
    rank = jnp.sum(hit.astype(F32) * earlier, axis=0, keepdims=True)
    rank_out[...] = jnp.broadcast_to(rank, (8, OBS))
    where = pick(iota((TOTAL, OBS), 0) == t * CAP + rank.astype(jnp.int32))
    e, s, q, k = lanes((1, 1, WIDE), 2)
    from_west = ((e >= 0) & (e < PASSES)) | ((k == 0) & (q == 1))
    from_east = ((e >= EAST) & (e < EAST + PASSES)) | ((k == 0) & (q == 2))
    sends = []
    size = TOTAL // PIECES
    for i in range(PIECES):
        rows = slice(i * size, (i + 1) * size)
        moved = mm(where[rows], wide[...]).reshape(size // (LON * CAP), LON * CAP, WIDE)
        up = jnp.concatenate([moved[:, -CAP:], moved[:, :-CAP]], axis=1)
        down = jnp.concatenate([moved[:, CAP:], moved[:, :CAP]], axis=1)
        result = jnp.where(from_west, up, jnp.where(from_east, down, moved))
        out[rows, :] = result.reshape(size, WIDE).astype(BF)
        sends.append(pltpu.make_async_copy(out.at[rows, :], out_hbm.at[rows, :], out_sems.at[i]))
        sends[-1].start()
    for send in sends:
        send.wait()


def pack(prints, weights, target, block, slot):
    hbm = pl.BlockSpec(memory_space=pltpu.HBM)
    return pl.pallas_call(
        pack_kernel,
        in_specs=[hbm] * 5,
        out_specs=(hbm, pl.BlockSpec(memory_space=pltpu.VMEM)),
        out_shape=(
            jax.ShapeDtypeStruct((TOTAL, WIDE), BF),
            jax.ShapeDtypeStruct((8, OBS), F32),
        ),
        scratch_shapes=[
            pltpu.VMEM((OBS, SPAN), BF),
            pltpu.VMEM((RHS, OBS), BF),
            pltpu.VMEM((1, OBS), jnp.int32),
            pltpu.VMEM((1, OBS), jnp.int32),
            pltpu.VMEM((1, OBS), jnp.int32),
            pltpu.VMEM((OBS, SPAN), BF),
            pltpu.VMEM((8, OBS), F32),
            pltpu.VMEM((SPAN, WIDE), BF),
            pltpu.VMEM((OBS, WIDE), BF),
            pltpu.VMEM((TOTAL, WIDE), BF),
            pltpu.SemaphoreType.DMA((6,)),
            pltpu.SemaphoreType.DMA((PIECES,)),
        ],
        compiler_params=params(60),
        cost_estimate=cost(2 * TOTAL * OBS * SPAN, 3 << 20),
        name="pack",
    )(prints, weights, target, block, slot)


def faces_kernel(own, first, second, coef, over, root, rim, wide):
    e, _, _, _ = lanes((1, WIDE), 1)
    even = lax.axis_index("lon") % 2 == 0

    def place(x, cond, shift):
        one = jnp.where(cond & (iota((CLON, WIDE), 0) == e + shift), 1.0, 0.0)
        return jnp.dot(jnp.sqrt(x), one, precision=lax.Precision.HIGHEST, preferred_element_type=F32)

    left = jnp.where(even, second[...], first[...])
    right = jnp.where(even, first[...], second[...])
    flat = place(own[...], (e >= PASSES) & (e < EAST), -PASSES)
    flat = flat + (place(left, (e >= 0) & (e < PASSES), CLON - PASSES) + place(right, (e >= EAST) & (e < EAST + PASSES), -EAST))
    beyond = jnp.zeros((CHUNKS, 128), F32)
    for q in range(RUN):
        wide[q, :CHUNKS, :] = beyond
        wide[q, CHUNKS:CHUNKS + ROWS, :] = flat[:, q * 128:(q + 1) * 128]
        wide[q, CHUNKS + ROWS:2 * CHUNKS + ROWS, :] = beyond
    for j in range(RIM):
        rim[j, :RHS, :] = jnp.broadcast_to(flat[j:j + 1], (RHS, WIDE))
        rim[j, RHS:, :] = jnp.broadcast_to(flat[ROWS - 1 - j:ROWS - j], (RHS, WIDE))

    def level(b):
        return [wide[q, pl.ds(CHUNKS + b, CHUNKS, stride=DEPTH), :] for q in range(RUN)]

    south, here = level(-1), level(0)
    for b in range(DEPTH):
        north = level(b + 1)
        ahead, behind = beside(here)
        rows = slice(b * CHUNKS, (b + 1) * CHUNKS)
        for q in range(RUN):
            cols = slice(q * 128, (q + 1) * 128)
            mid = 1.0 - here[q] * ((north[q] + south[q]) + (ahead[q] + behind[q]))
            some = here[q] > 0.0
            coef[0, rows, cols] = mid
            coef[1, rows, cols] = here[q] * here[q]
            over[rows, cols] = jnp.where(some, mid / jnp.where(some, here[q], 1.0), 0.0)
            root[rows, cols] = here[q]
        south, here = here, north


def faces(own, first, second):
    return pl.pallas_call(
        faces_kernel,
        out_shape=(
            jax.ShapeDtypeStruct((2, ROWS, WIDE), F32),
            jax.ShapeDtypeStruct((ROWS, WIDE), F32),
            jax.ShapeDtypeStruct((ROWS, WIDE), F32),
            jax.ShapeDtypeStruct((RIM, 2 * RHS, WIDE), F32),
        ),
        scratch_shapes=[pltpu.VMEM((RUN, ROWS + 2 * CHUNKS + DEPTH, 128), F32)],
        compiler_params=params(12),
        cost_estimate=cost(1 << 30, 6 << 20),
        name="faces",
    )(own, first, second)


def adjoint_kernel(got, roots, field, rim, inner, outer, facts_out):
    column, lane = iota((16, 128), 0), iota((16, 128), 1)
    facts = jnp.zeros((16, TOTAL), F32)
    for i in range(FRONT):
        mine = (lane == column - 5 * i) & (column >= 5 * i) & (column < 5 * i + 5)
        facts = facts + mm(pick(mine), got[:, i * 128:(i + 1) * 128], NT)
    facts_out[...] = facts
    row = iota((ROWS, TOTAL), 0).astype(F32)

    def border(first_tile, first_lane, tile, fact):
        source, lane = iota((PASSES * 128, 128), 0), iota((PASSES * 128, 128), 1)
        take = source == lane % 32 // SLOTS * 128 + first_lane + lane % SLOTS
        cells = mm(got[:, first_tile * 128:(first_tile + PASSES) * 128], pick(take))
        fan = pick(iota((128, 128), 0) == iota((128, 128), 1) // 32)
        cells = cells * mm(got[:, tile * 128:(tile + 1) * 128], fan)
        high = cells.astype(BF)
        low = (cells - high.astype(F32)).astype(BF)
        both = mm(pick(row == facts[fact:fact + 1]), jnp.concatenate([high, low], axis=1))
        return both[:, :128] + both[:, 128:]

    before = border(FRONT, 0, 1, 9)
    after = border(0, 128 - SLOTS, 2, 14)
    mine = row == facts[RHS:RHS + 1]
    lane = iota((1, 128), 1)
    end = FRONT + PASSES
    for r in range(RHS):
        total = mm(jnp.where(mine, facts[r:r + 1], 0.0).astype(BF), got[...])
        for q in range(RUN):
            cols = slice(q * 128, (q + 1) * 128)
            part = total[:, cols]
            if FRONT <= q < end:
                part = jnp.where(lane < SLOTS, rolled(before, -(r * 32 + (q - FRONT) * SLOTS)), part)
            if q < PASSES:
                part = jnp.where(lane >= 128 - SLOTS, rolled(after, -(r * 32 + (q + 1) * SLOTS)), part)
            field[r, :, cols] = part
        for j in range(RIM):
            at = j * CHUNKS
            rim[j, r:r + 1, :] = field[r, at:at + 1, :]
            at = (DEPTH - j) * CHUNKS - 1
            rim[j, RHS + r:RHS + r + 1, :] = field[r, at:at + 1, :]
    for j in range(RIM):
        rim[j] = rim[j] * roots[j]
    even = lax.axis_index("lat") % 2 == 0
    for base, ref in ((0, rim), (PASSES, roots)):
        for j in range(PASSES):
            low, high = ref[j, :RHS, :], ref[j, RHS:, :]
            inner[base + j] = jnp.where(even, high, low)
            outer[base + j] = jnp.where(even, low, high)


def adjoint(got, roots):
    return pl.pallas_call(
        adjoint_kernel,
        out_shape=(
            jax.ShapeDtypeStruct((RHS, ROWS, WIDE), F32),
            jax.ShapeDtypeStruct((RIM, 2 * RHS, WIDE), F32),
            jax.ShapeDtypeStruct((2 * PASSES, RHS, WIDE), F32),
            jax.ShapeDtypeStruct((2 * PASSES, RHS, WIDE), F32),
            jax.ShapeDtypeStruct((16, TOTAL), F32),
        ),
        compiler_params=params(16),
        cost_estimate=cost(5 << 30, 8 << 20),
        name="adjoint",
    )(got, roots)


def inside(q):
    e = (iota((1, 128), 1) // 8) * RUN + q - FRONT
    return (e >= PASSES) & (e < EAST)


def surround(ref, r):
    last = DEPTH * CHUNKS
    ref[r, :CHUNKS, :] = pltpu.roll(ref[r, last:last + CHUNKS, :], 1, 0)
    ref[r, last + CHUNKS:, :] = pltpu.roll(ref[r, CHUNKS:2 * CHUNKS, :], CHUNKS - 1, 0)


def diffuse_kernel(field, coef, over, root, smooth, outer, one, two):
    usual, final = (coef.at[0], coef.at[1]), (over, root)

    def rows_of(e):
        at = e * CHUNKS
        return pl.ds(at if isinstance(at, int) else pl.multiple_of(at, CHUNKS), CHUNKS)

    def some_levels(ref, e, factor, store, count):
        def load(r, at, q):
            return ref[r, rows_of(at), q * 128:(q + 1) * 128]

        levels = tuple(e + i for i in range(count))
        for group in ((0, 1), (2, 3)):
            turned_west = {r: [rolled(load(r, at, RUN - 1), SLOTS) for at in levels] for r in group}
            turned_east = {r: [rolled(load(r, at, 0), -SLOTS) for at in levels] for r in group}
            behind, here = [{r: [load(r, at, q) for at in levels] for r in group} for q in (0, 1)]
            for q in [*range(1, RUN), 0]:
                mid, near = [[kind[rows_of(at - 1), q * 128:(q + 1) * 128] for at in levels] for kind in factor]
                if q == 0:
                    behind = turned_west
                    here, ahead = [{r: [load(r, at, i) for at in levels] for r in group} for i in (0, 1)]
                elif q + 1 < RUN:
                    ahead = {r: [load(r, at, q + 1) for at in levels] for r in group}
                else:
                    ahead = turned_east
                for r in group:
                    column = [load(r, e - 1, q)] + here[r] + [load(r, e + count, q)]
                    for i in range(count):
                        total = (column[i + 2] + column[i]) + (ahead[r][i] + behind[r][i])
                        store(r, q, i, mid[i] * here[r][i] + near[i] * total)
                behind, here = here, ahead

    def sweep(ref, target, first, end, factor, to=0):
        def step(pair, _):
            e = first + 4 * pair

            def store(r, q, i, value):
                target[r, rows_of(e + i + to), q * 128:(q + 1) * 128] = value

            some_levels(ref, e, factor, store, 4)
            return 0

        lax.fori_loop(0, (end - first) // 4, step, 0)

    def scale(e, _):
        for q in range(RUN):
            cols = slice(q * 128, (q + 1) * 128)
            factor = root[rows_of(e), cols]
            for r in range(RHS):
                two[r, rows_of(e + 1), cols] = field[r, rows_of(e), cols] * factor
        return 0

    lax.fori_loop(0, DEPTH, scale, 0, unroll=2)
    for r in range(RHS):
        surround(two, r)
    for ref, target in ((two, one), (one, two), (two, one)):
        sweep(ref, target, 1, DEPTH + 1, usual)
        for r in range(RHS):
            surround(target, r)
    sweep(one, outer, 1, PASSES + 1, final, -1)
    sweep(one, outer, DEPTH + 1 - PASSES, DEPTH + 1, final, 2 * PASSES - 1 - DEPTH)

    def rounded(pair, _):
        first = {}

        def store(r, q, i, value):
            if i == 0:
                first[r, q] = value
                return
            both = jnp.concatenate([first.pop((r, q)), value], axis=0)
            at = pl.ds(pl.multiple_of(pair * 2 * CHUNKS, 2 * CHUNKS), 2 * CHUNKS)
            smooth[r, at, q * 128:(q + 1) * 128] = jnp.where(inside(q), both, 0.0).astype(BF)

        some_levels(one, PASSES + 1 + 2 * pair, final, store, 2)
        return 0

    lax.fori_loop(0, MIDDLE // (2 * CHUNKS), rounded, 0, unroll=2)


def diffuse(field, coef, over, root):
    return pl.pallas_call(
        diffuse_kernel,
        out_shape=(
            jax.ShapeDtypeStruct((RHS, MIDDLE, WIDE), BF),
            jax.ShapeDtypeStruct((RHS, OUTER, WIDE), F32),
        ),
        scratch_shapes=[
            pltpu.VMEM((RHS, TALL * CHUNKS, WIDE), F32),
            pltpu.VMEM((RHS, TALL * CHUNKS, WIDE), F32),
        ],
        compiler_params=params(14),
        cost_estimate=cost(6 << 30, 8 << 20),
        name="diffuse",
    )(field, coef, over, root)


def finish_kernel(smooth, outer, rim, roots, inner, beyond, got, facts, out, border, values):
    even = lax.axis_index("lat") % 2 == 0

    def levels(base, own):
        rows = []
        for j in range(base + PASSES - 1, base - 1, -1):
            south = jnp.where(even, beyond[j], inner[j])
            north = jnp.where(even, inner[j], beyond[j])
            rows.append(jnp.concatenate([south, north], axis=0))
        return [[x[:, q * 128:(q + 1) * 128] for q in range(RUN)] for x in rows + [own[j] for j in range(RIM)]]

    def around(x, j):
        ahead, behind = beside(x[j])
        return [(x[j + 1][q] + x[j - 1][q]) + (ahead[q] + behind[q]) for q in range(RUN)]

    v, root = levels(0, rim), levels(PASSES, roots)
    count = PASSES + RIM
    mid = [None] + [[1.0 - x * y for x, y in zip(root[j], around(root, j))] for j in range(1, count - 1)]
    for step in range(1, PASSES + 1):
        new = list(v)
        for j in range(step, count - step):
            total = around(v, j)
            new[j] = [mid[j][q] * v[j][q] + (root[j][q] * root[j][q]) * total[q] for q in range(RUN)]
        v = new
    for j in range(PASSES, 2 * PASSES):
        some = [x > 0.0 for x in root[j]]
        v[j] = [jnp.where(some[q], v[j][q] / jnp.where(some[q], root[j][q], 1.0), 0.0) for q in range(RUN)]
    sub = iota((CHUNKS, 1), 0)
    for r in range(RHS):
        for q in range(RUN):
            cols = slice(q * 128, (q + 1) * 128)
            for pair in range(PASSES):
                both = []
                for b in (2 * pair, 2 * pair + 1):
                    here = outer[r, b * CHUNKS:(b + 1) * CHUNKS, cols]
                    if b < PASSES:
                        here = jnp.where(sub == 0, v[PASSES + b][q][r:r + 1], here)
                    else:
                        j = PASSES + 2 * PASSES - 1 - b
                        here = jnp.where(sub == CHUNKS - 1, v[j][q][RHS + r:RHS + r + 1], here)
                    both.append(here)
                both = jnp.where(inside(q), jnp.concatenate(both, axis=0), 0.0).astype(BF)
                border[r, pair * 2 * CHUNKS:(pair + 1) * 2 * CHUNKS, cols] = both

    side = PASSES * CHUNKS
    chosen = iota((ROWS, TOTAL), 0).astype(F32) == facts[RHS:RHS + 1, :]
    total = [0.0] * RHS
    for ref, spans in ((smooth, ((side, MIDDLE),)), (border, ((0, side), (ROWS - side, side)))):
        shares = mm(ref[...].reshape(-1, WIDE), got[...], NT)
        at = 0
        for r in range(RHS):
            for first, size in spans:
                part = jnp.where(chosen[first:first + size], shares[at:at + size], 0.0)
                total[r] = total[r] + jnp.sum(part, axis=0, keepdims=True)
                at += size
    for r in range(RHS):
        values[r:r + 1, :] = total[r]
        values[RHS + r:RHS + r + 1, :] = total[r]
    both = values[...]
    turn = iota((2 * RHS, TOTAL), 0) // RHS
    keep = [jnp.where(iota((2 * RHS, TOTAL), 1) % CAP == turn + 2 * i, 1.0, 0.0) for i in range(CAP // 2)]
    many = [part.astype(F32) * k for part in thirds(both) for k in keep]
    owner = pick(iota((DEVICES, TOTAL), 1) // CAP == iota((DEVICES, TOTAL), 0))
    sums = mm(owner, jnp.concatenate(many, axis=0).astype(BF), NT)
    size = CAP * RHS
    out[...] = jnp.zeros_like(out)
    out[:, :size] = (sums[:, :size] + sums[:, size:2 * size]) + sums[:, 2 * size:3 * size]


def finish(smooth, outer, rim, roots, inner, beyond, got, facts):
    return pl.pallas_call(
        finish_kernel,
        out_shape=jax.ShapeDtypeStruct((DEVICES, 128), F32),
        scratch_shapes=[
            pltpu.VMEM((RHS, OUTER, WIDE), BF),
            pltpu.VMEM((8, TOTAL), F32),
        ],
        compiler_params=params(16),
        cost_estimate=cost(3 << 30, 10 << 20),
        name="finish",
    )(smooth, outer, rim, roots, inner, beyond, got, facts)


def unpack_kernel(values, target, rank, out):
    hit = pick(iota((DEVICES, OBS), 0) == target[...])
    total = jnp.zeros((CAP * RHS, OBS), F32)
    for part in thirds(values[:, :CAP * RHS]):
        total = total + mm(part, hit, TN)
    total = jnp.where((iota((CAP * RHS, OBS), 0) // RHS).astype(F32) == rank[0:1, :], total, 0.0)
    pair = (total[0:8] + total[8:16]) + (total[16:24] + total[24:32])
    out[...] = pair[0:RHS] + pair[RHS:]


def unpack(values, target, rank):
    return pl.pallas_call(
        unpack_kernel,
        out_shape=jax.ShapeDtypeStruct((RHS, OBS), F32),
        compiler_params=params(8),
        name="unpack",
    )(values, target, rank)


def swap(x, axis, second, closed):
    count = lax.axis_size(axis)
    pairs = [(i, (i + 1) % count) for i in range(int(second), count, 2) if closed or i + 1 < count]
    return lax.ppermute(x, axis, pairs + [(j, i) for i, j in pairs])


def body(footprints, dual_weights, target_device, target_block, obs_slot, diffusivity):
    target = target_device.reshape(1, OBS)
    packed, rank = pack(footprints, dual_weights.T, target, target_block.reshape(1, OBS), obs_slot.reshape(1, OBS))
    first = swap(diffusivity, "lon", False, True)
    second = swap(diffusivity, "lon", True, True)
    packed, first, second = lax.optimization_barrier((packed, first, second))
    coef, over, root, roots = faces(diffusivity, first, second)
    got = lax.all_to_all(packed, ("lat", "lon"), split_axis=0, concat_axis=0, tiled=True)
    field, rim, inner, beyond, facts = adjoint(got, roots)
    inner = swap(inner, "lat", False, False)
    beyond = swap(beyond, "lat", True, False)
    smooth, outer = diffuse(field, coef, over, root)
    values = finish(smooth, outer, rim, roots, inner, beyond, got, facts)
    returned = lax.all_to_all(values, ("lat", "lon"), split_axis=0, concat_axis=0, tiled=True)
    return unpack(returned, target, rank).T


def solution(mesh):
    placed = (
        P(("lat", "lon"), None),
        P(("lat", "lon"), None),
        P(("lat", "lon"), None),
        P(("lat", "lon")),
        P(("lat", "lon")),
        P("lat", "lon"),
    )
    return jax.shard_map(
        body, mesh=mesh, in_specs=placed, out_specs=P(("lat", "lon"), None), check_vma=False
    )
```

```python
import jax
import jax.numpy as jnp
from jax import lax
from jax.experimental import pallas as pl
from jax.experimental.pallas import tpu as pltpu
from jax.sharding import PartitionSpec as P

SLOTS = 8
CLON = 128
PASSES = 4
RHS = 4
OBS = 512
CAP = 8
DEVICES = 128
LON = 16
ROWS = 256
CHUNKS = 8
DEPTH = ROWS // CHUNKS
TALL = DEPTH + 2
RUN = 9
FRONT = 3
SPAN = SLOTS * CLON
WIDE = RUN * 128
EAST = CLON + PASSES
TOTAL = DEVICES * CAP
RIM = 2 * PASSES
OUTER = 2 * PASSES * CHUNKS
MIDDLE = ROWS - OUTER
BF = jnp.bfloat16
F32 = jnp.float32
NT = ((1,), (1,))
TN = ((0,), (0,))


def iota(shape, dim):
    return lax.broadcasted_iota(jnp.int32, shape, dim)


def pick(cond):
    return jnp.where(cond, 1.0, 0.0).astype(BF)


def mm(a, b, dims=((1,), (0,))):
    return lax.dot_general(a, b, (dims, ((), ())), preferred_element_type=F32)


def thirds(x):
    hi = x.astype(BF)
    rest = x - hi.astype(F32)
    mid = rest.astype(BF)
    return hi, mid, (rest - mid.astype(F32)).astype(BF)


def params(mib):
    return pltpu.CompilerParams(vmem_limit_bytes=mib * 1024 * 1024)


def cost(flops, size):
    return pl.CostEstimate(flops=flops, bytes_accessed=size, transcendentals=0)


def lanes(shape, dim):
    lane = iota(shape, dim)
    q, k, s = lane // 128, lane % 128 // 8, lane % 8
    return k * RUN + q - FRONT, s, q, k


def rolled(x, step):
    return pltpu.roll(x, step % 128, 1)


def beside(row):
    return row[1:] + [rolled(row[0], -SLOTS)], [rolled(row[-1], SLOTS)] + row[:-1]


PIECES = 8


def pack_kernel(prints_hbm, weights_hbm, target_hbm, block_hbm, slot_hbm, out_hbm, rank_out,
                prints, weights, target, block, slot, masked, meta, spread, wide, out, sems, out_sems):
    pairs = ((target_hbm, target), (weights_hbm, weights), (block_hbm, block), (slot_hbm, slot), (prints_hbm, prints))
    copies = [pltpu.make_async_copy(a, b, sems.at[i]) for i, (a, b) in enumerate(pairs[:4])]
    parts = [slice(i * OBS // 2, (i + 1) * OBS // 2) for i in range(2)]
    for i, part in enumerate(parts):
        copies.append(pltpu.make_async_copy(prints_hbm.at[part, :], prints.at[part, :], sems.at[4 + i]))
    for copy in copies:
        copy.start()
    e, s, q, k = lanes((1, WIDE), 1)
    base = s * CLON + e
    source = jnp.where(e < PASSES, base + CLON - PASSES, jnp.where(e < EAST, base - PASSES, base - EAST))
    source = jnp.where((e >= 0) & (e < EAST + PASSES), source, -1)
    spread[...] = pick(iota((SPAN, WIDE), 0) == source)
    before = pick(iota((OBS, OBS), 0) < iota((OBS, OBS), 1))
    for copy in copies[:4]:
        copy.wait()
    blk = block[...]
    meta[...] = jnp.zeros_like(meta)
    meta[0:RHS, :] = weights[...].astype(F32)
    meta[4:5, :] = ((blk % DEPTH) * CHUNKS + blk // DEPTH).astype(F32)
    meta[5:6, :] = slot[...].astype(F32)
    facts = meta[...].astype(BF)
    slots = mm(facts, pick(iota((8, 128), 0) == 5), TN).astype(BF)
    t = target[...]
    hit = pick(iota((DEVICES, OBS), 0) == t)
    earlier = mm(hit, before)
    e, s, q, k = lanes((1, WIDE), 1)
    fact = jnp.where((k == 0) & (q < FRONT) & (s < 5), s, -1)
    extra = mm(facts, pick(iota((8, WIDE), 0) == fact), TN)
    for copy, part in zip(copies[4:], parts):
        copy.wait()
        for s in range(SLOTS):
            live = slots[part] >= jnp.asarray(s, BF)
            piece = prints[part, s * CLON:(s + 1) * CLON]
            masked[part, s * CLON:(s + 1) * CLON] = jnp.where(live, piece, jnp.zeros_like(piece))
        wide[part, :] = (mm(masked[part, :], spread[...]) + extra[part]).astype(BF)
    rank = jnp.sum(hit.astype(F32) * earlier, axis=0, keepdims=True)
    rank_out[...] = jnp.broadcast_to(rank, (8, OBS))
    where = pick(iota((TOTAL, OBS), 0) == t * CAP + rank.astype(jnp.int32))
    e, s, q, k = lanes((1, 1, WIDE), 2)
    from_west = ((e >= 0) & (e < PASSES)) | ((k == 0) & (q == 1))
    from_east = ((e >= EAST) & (e < EAST + PASSES)) | ((k == 0) & (q == 2))
    sends = []
    size = TOTAL // PIECES
    for i in range(PIECES):
        rows = slice(i * size, (i + 1) * size)
        moved = mm(where[rows], wide[...]).reshape(size // (LON * CAP), LON * CAP, WIDE)
        up = jnp.concatenate([moved[:, -CAP:], moved[:, :-CAP]], axis=1)
        down = jnp.concatenate([moved[:, CAP:], moved[:, :CAP]], axis=1)
        result = jnp.where(from_west, up, jnp.where(from_east, down, moved))
        out[rows, :] = result.reshape(size, WIDE).astype(BF)
        sends.append(pltpu.make_async_copy(out.at[rows, :], out_hbm.at[rows, :], out_sems.at[i]))
        sends[-1].start()
    for send in sends:
        send.wait()


def pack(prints, weights, target, block, slot):
    hbm = pl.BlockSpec(memory_space=pltpu.HBM)
    return pl.pallas_call(
        pack_kernel,
        in_specs=[hbm] * 5,
        out_specs=(hbm, pl.BlockSpec(memory_space=pltpu.VMEM)),
        out_shape=(
            jax.ShapeDtypeStruct((TOTAL, WIDE), BF),
            jax.ShapeDtypeStruct((8, OBS), F32),
        ),
        scratch_shapes=[
            pltpu.VMEM((OBS, SPAN), BF),
            pltpu.VMEM((RHS, OBS), BF),
            pltpu.VMEM((1, OBS), jnp.int32),
            pltpu.VMEM((1, OBS), jnp.int32),
            pltpu.VMEM((1, OBS), jnp.int32),
            pltpu.VMEM((OBS, SPAN), BF),
            pltpu.VMEM((8, OBS), F32),
            pltpu.VMEM((SPAN, WIDE), BF),
            pltpu.VMEM((OBS, WIDE), BF),
            pltpu.VMEM((TOTAL, WIDE), BF),
            pltpu.SemaphoreType.DMA((6,)),
            pltpu.SemaphoreType.DMA((PIECES,)),
        ],
        compiler_params=params(60),
        cost_estimate=cost(2 * TOTAL * OBS * SPAN, 3 << 20),
        name="pack",
    )(prints, weights, target, block, slot)


def faces_kernel(own, first, second, coef, over, root, rim, wide):
    e, _, _, _ = lanes((1, WIDE), 1)
    even = lax.axis_index("lon") % 2 == 0

    def place(x, cond, shift):
        one = jnp.where(cond & (iota((CLON, WIDE), 0) == e + shift), 1.0, 0.0)
        return jnp.dot(jnp.sqrt(x), one, precision=lax.Precision.HIGHEST, preferred_element_type=F32)

    left = jnp.where(even, second[...], first[...])
    right = jnp.where(even, first[...], second[...])
    flat = place(own[...], (e >= PASSES) & (e < EAST), -PASSES)
    flat = flat + (place(left, (e >= 0) & (e < PASSES), CLON - PASSES) + place(right, (e >= EAST) & (e < EAST + PASSES), -EAST))
    beyond = jnp.zeros((CHUNKS, 128), F32)
    for q in range(RUN):
        wide[q, :CHUNKS, :] = beyond
        wide[q, CHUNKS:CHUNKS + ROWS, :] = flat[:, q * 128:(q + 1) * 128]
        wide[q, CHUNKS + ROWS:2 * CHUNKS + ROWS, :] = beyond
    for j in range(RIM):
        rim[j, :RHS, :] = jnp.broadcast_to(flat[j:j + 1], (RHS, WIDE))
        rim[j, RHS:, :] = jnp.broadcast_to(flat[ROWS - 1 - j:ROWS - j], (RHS, WIDE))

    def level(b):
        return [wide[q, pl.ds(CHUNKS + b, CHUNKS, stride=DEPTH), :] for q in range(RUN)]

    south, here = level(-1), level(0)
    for b in range(DEPTH):
        north = level(b + 1)
        ahead, behind = beside(here)
        rows = slice(b * CHUNKS, (b + 1) * CHUNKS)
        for q in range(RUN):
            cols = slice(q * 128, (q + 1) * 128)
            mid = 1.0 - here[q] * ((north[q] + south[q]) + (ahead[q] + behind[q]))
            some = here[q] > 0.0
            coef[0, rows, cols] = mid
            coef[1, rows, cols] = here[q] * here[q]
            over[rows, cols] = jnp.where(some, mid / jnp.where(some, here[q], 1.0), 0.0)
            root[rows, cols] = here[q]
        south, here = here, north


def faces(own, first, second):
    return pl.pallas_call(
        faces_kernel,
        out_shape=(
            jax.ShapeDtypeStruct((2, ROWS, WIDE), F32),
            jax.ShapeDtypeStruct((ROWS, WIDE), F32),
            jax.ShapeDtypeStruct((ROWS, WIDE), F32),
            jax.ShapeDtypeStruct((RIM, 2 * RHS, WIDE), F32),
        ),
        scratch_shapes=[pltpu.VMEM((RUN, ROWS + 2 * CHUNKS + DEPTH, 128), F32)],
        compiler_params=params(12),
        cost_estimate=cost(1 << 30, 6 << 20),
        name="faces",
    )(own, first, second)


def adjoint_kernel(got, roots, field, rim, inner, outer, facts_out):
    column, lane = iota((16, 128), 0), iota((16, 128), 1)
    facts = jnp.zeros((16, TOTAL), F32)
    for i in range(FRONT):
        mine = (lane == column - 5 * i) & (column >= 5 * i) & (column < 5 * i + 5)
        facts = facts + mm(pick(mine), got[:, i * 128:(i + 1) * 128], NT)
    facts_out[...] = facts
    row = iota((ROWS, TOTAL), 0).astype(F32)

    def border(first_tile, first_lane, tile, fact):
        source, lane = iota((PASSES * 128, 128), 0), iota((PASSES * 128, 128), 1)
        take = source == lane % 32 // SLOTS * 128 + first_lane + lane % SLOTS
        cells = mm(got[:, first_tile * 128:(first_tile + PASSES) * 128], pick(take))
        fan = pick(iota((128, 128), 0) == iota((128, 128), 1) // 32)
        cells = cells * mm(got[:, tile * 128:(tile + 1) * 128], fan)
        high = cells.astype(BF)
        low = (cells - high.astype(F32)).astype(BF)
        both = mm(pick(row == facts[fact:fact + 1]), jnp.concatenate([high, low], axis=1))
        return both[:, :128] + both[:, 128:]

    before = border(FRONT, 0, 1, 9)
    after = border(0, 128 - SLOTS, 2, 14)
    mine = row == facts[RHS:RHS + 1]
    lane = iota((1, 128), 1)
    end = FRONT + PASSES
    for r in range(RHS):
        total = mm(jnp.where(mine, facts[r:r + 1], 0.0).astype(BF), got[...])
        for q in range(RUN):
            cols = slice(q * 128, (q + 1) * 128)
            part = total[:, cols]
            if FRONT <= q < end:
                part = jnp.where(lane < SLOTS, rolled(before, -(r * 32 + (q - FRONT) * SLOTS)), part)
            if q < PASSES:
                part = jnp.where(lane >= 128 - SLOTS, rolled(after, -(r * 32 + (q + 1) * SLOTS)), part)
            field[r, :, cols] = part
        for j in range(RIM):
            at = j * CHUNKS
            rim[j, r:r + 1, :] = field[r, at:at + 1, :]
            at = (DEPTH - j) * CHUNKS - 1
            rim[j, RHS + r:RHS + r + 1, :] = field[r, at:at + 1, :]
    for j in range(RIM):
        rim[j] = rim[j] * roots[j]
    even = lax.axis_index("lat") % 2 == 0
    for base, ref in ((0, rim), (PASSES, roots)):
        for j in range(PASSES):
            low, high = ref[j, :RHS, :], ref[j, RHS:, :]
            inner[base + j] = jnp.where(even, high, low)
            outer[base + j] = jnp.where(even, low, high)


def adjoint(got, roots):
    return pl.pallas_call(
        adjoint_kernel,
        out_shape=(
            jax.ShapeDtypeStruct((RHS, ROWS, WIDE), F32),
            jax.ShapeDtypeStruct((RIM, 2 * RHS, WIDE), F32),
            jax.ShapeDtypeStruct((2 * PASSES, RHS, WIDE), F32),
            jax.ShapeDtypeStruct((2 * PASSES, RHS, WIDE), F32),
            jax.ShapeDtypeStruct((16, TOTAL), F32),
        ),
        compiler_params=params(16),
        cost_estimate=cost(5 << 30, 8 << 20),
        name="adjoint",
    )(got, roots)


def inside(q):
    e = (iota((1, 128), 1) // 8) * RUN + q - FRONT
    return (e >= PASSES) & (e < EAST)


def surround(ref, r):
    last = DEPTH * CHUNKS
    ref[r, :CHUNKS, :] = pltpu.roll(ref[r, last:last + CHUNKS, :], 1, 0)
    ref[r, last + CHUNKS:, :] = pltpu.roll(ref[r, CHUNKS:2 * CHUNKS, :], CHUNKS - 1, 0)


def diffuse_kernel(field, coef, over, root, smooth, outer, one, two):
    usual, final = (coef.at[0], coef.at[1]), (over, root)

    def rows_of(e):
        at = e * CHUNKS
        return pl.ds(at if isinstance(at, int) else pl.multiple_of(at, CHUNKS), CHUNKS)

    def some_levels(ref, e, factor, store, count):
        def load(r, at, q):
            return ref[r, rows_of(at), q * 128:(q + 1) * 128]

        levels = tuple(e + i for i in range(count))
        for group in ((0, 1), (2, 3)):
            turned_west = {r: [rolled(load(r, at, RUN - 1), SLOTS) for at in levels] for r in group}
            turned_east = {r: [rolled(load(r, at, 0), -SLOTS) for at in levels] for r in group}
            behind, here = [{r: [load(r, at, q) for at in levels] for r in group} for q in (0, 1)]
            for q in [*range(1, RUN), 0]:
                mid, near = [[kind[rows_of(at - 1), q * 128:(q + 1) * 128] for at in levels] for kind in factor]
                if q == 0:
                    behind = turned_west
                    here, ahead = [{r: [load(r, at, i) for at in levels] for r in group} for i in (0, 1)]
                elif q + 1 < RUN:
                    ahead = {r: [load(r, at, q + 1) for at in levels] for r in group}
                else:
                    ahead = turned_east
                for r in group:
                    column = [load(r, e - 1, q)] + here[r] + [load(r, e + count, q)]
                    for i in range(count):
                        total = (column[i + 2] + column[i]) + (ahead[r][i] + behind[r][i])
                        store(r, q, i, mid[i] * here[r][i] + near[i] * total)
                behind, here = here, ahead

    def sweep(ref, target, first, end, factor, to=0):
        def step(pair, _):
            e = first + 4 * pair

            def store(r, q, i, value):
                target[r, rows_of(e + i + to), q * 128:(q + 1) * 128] = value

            some_levels(ref, e, factor, store, 4)
            return 0

        lax.fori_loop(0, (end - first) // 4, step, 0)

    def scale(e, _):
        for q in range(RUN):
            cols = slice(q * 128, (q + 1) * 128)
            factor = root[rows_of(e), cols]
            for r in range(RHS):
                two[r, rows_of(e + 1), cols] = field[r, rows_of(e), cols] * factor
        return 0

    lax.fori_loop(0, DEPTH, scale, 0, unroll=2)
    for r in range(RHS):
        surround(two, r)
    for ref, target in ((two, one), (one, two), (two, one)):
        sweep(ref, target, 1, DEPTH + 1, usual)
        for r in range(RHS):
            surround(target, r)
    sweep(one, outer, 1, PASSES + 1, final, -1)
    sweep(one, outer, DEPTH + 1 - PASSES, DEPTH + 1, final, 2 * PASSES - 1 - DEPTH)

    def rounded(pair, _):
        first = {}

        def store(r, q, i, value):
            if i % 2 == 0:
                first[r, q] = value
                return
            both = jnp.concatenate([first.pop((r, q)), value], axis=0)
            at = pl.ds(pl.multiple_of((4 * pair + i - 1) * CHUNKS, 2 * CHUNKS), 2 * CHUNKS)
            smooth[r, at, q * 128:(q + 1) * 128] = jnp.where(inside(q), both, 0.0).astype(BF)

        some_levels(one, PASSES + 1 + 4 * pair, final, store, 4)
        return 0

    lax.fori_loop(0, MIDDLE // (4 * CHUNKS), rounded, 0)


def diffuse(field, coef, over, root):
    return pl.pallas_call(
        diffuse_kernel,
        out_shape=(
            jax.ShapeDtypeStruct((RHS, MIDDLE, WIDE), BF),
            jax.ShapeDtypeStruct((RHS, OUTER, WIDE), F32),
        ),
        scratch_shapes=[
            pltpu.VMEM((RHS, TALL * CHUNKS, WIDE), F32),
            pltpu.VMEM((RHS, TALL * CHUNKS, WIDE), F32),
        ],
        compiler_params=params(14),
        cost_estimate=cost(6 << 30, 8 << 20),
        name="diffuse",
    )(field, coef, over, root)


def finish_kernel(smooth, outer, rim, roots, inner, beyond, got, facts, out, border, values):
    even = lax.axis_index("lat") % 2 == 0

    def levels(base, own):
        rows = []
        for j in range(base + PASSES - 1, base - 1, -1):
            south = jnp.where(even, beyond[j], inner[j])
            north = jnp.where(even, inner[j], beyond[j])
            rows.append(jnp.concatenate([south, north], axis=0))
        return [[x[:, q * 128:(q + 1) * 128] for q in range(RUN)] for x in rows + [own[j] for j in range(RIM)]]

    def around(x, j):
        ahead, behind = beside(x[j])
        return [(x[j + 1][q] + x[j - 1][q]) + (ahead[q] + behind[q]) for q in range(RUN)]

    v, root = levels(0, rim), levels(PASSES, roots)
    count = PASSES + RIM
    mid = [None] + [[1.0 - x * y for x, y in zip(root[j], around(root, j))] for j in range(1, count - 1)]
    for step in range(1, PASSES + 1):
        new = list(v)
        for j in range(step, count - step):
            total = around(v, j)
            new[j] = [mid[j][q] * v[j][q] + (root[j][q] * root[j][q]) * total[q] for q in range(RUN)]
        v = new
    for j in range(PASSES, 2 * PASSES):
        some = [x > 0.0 for x in root[j]]
        v[j] = [jnp.where(some[q], v[j][q] / jnp.where(some[q], root[j][q], 1.0), 0.0) for q in range(RUN)]
    sub = iota((CHUNKS, 1), 0)
    for r in range(RHS):
        for q in range(RUN):
            cols = slice(q * 128, (q + 1) * 128)
            for pair in range(PASSES):
                both = []
                for b in (2 * pair, 2 * pair + 1):
                    here = outer[r, b * CHUNKS:(b + 1) * CHUNKS, cols]
                    if b < PASSES:
                        here = jnp.where(sub == 0, v[PASSES + b][q][r:r + 1], here)
                    else:
                        j = PASSES + 2 * PASSES - 1 - b
                        here = jnp.where(sub == CHUNKS - 1, v[j][q][RHS + r:RHS + r + 1], here)
                    both.append(here)
                both = jnp.where(inside(q), jnp.concatenate(both, axis=0), 0.0).astype(BF)
                border[r, pair * 2 * CHUNKS:(pair + 1) * 2 * CHUNKS, cols] = both

    side = PASSES * CHUNKS
    chosen = iota((ROWS, TOTAL), 0).astype(F32) == facts[RHS:RHS + 1, :]
    total = [0.0] * RHS
    for ref, spans in ((smooth, ((side, MIDDLE),)), (border, ((0, side), (ROWS - side, side)))):
        shares = mm(ref[...].reshape(-1, WIDE), got[...], NT)
        at = 0
        for r in range(RHS):
            for first, size in spans:
                part = jnp.where(chosen[first:first + size], shares[at:at + size], 0.0)
                total[r] = total[r] + jnp.sum(part, axis=0, keepdims=True)
                at += size
    for r in range(RHS):
        values[r:r + 1, :] = total[r]
        values[RHS + r:RHS + r + 1, :] = total[r]
    both = values[...]
    turn = iota((2 * RHS, TOTAL), 0) // RHS
    keep = [jnp.where(iota((2 * RHS, TOTAL), 1) % CAP == turn + 2 * i, 1.0, 0.0) for i in range(CAP // 2)]
    many = [part.astype(F32) * k for part in thirds(both) for k in keep]
    owner = pick(iota((DEVICES, TOTAL), 1) // CAP == iota((DEVICES, TOTAL), 0))
    sums = mm(owner, jnp.concatenate(many, axis=0).astype(BF), NT)
    size = CAP * RHS
    out[...] = jnp.zeros_like(out)
    out[:, :size] = (sums[:, :size] + sums[:, size:2 * size]) + sums[:, 2 * size:3 * size]


def finish(smooth, outer, rim, roots, inner, beyond, got, facts):
    return pl.pallas_call(
        finish_kernel,
        out_shape=jax.ShapeDtypeStruct((DEVICES, 128), F32),
        scratch_shapes=[
            pltpu.VMEM((RHS, OUTER, WIDE), BF),
            pltpu.VMEM((8, TOTAL), F32),
        ],
        compiler_params=params(16),
        cost_estimate=cost(3 << 30, 10 << 20),
        name="finish",
    )(smooth, outer, rim, roots, inner, beyond, got, facts)


def unpack_kernel(values, target, rank, out):
    hit = pick(iota((DEVICES, OBS), 0) == target[...])
    total = jnp.zeros((CAP * RHS, OBS), F32)
    for part in thirds(values[:, :CAP * RHS]):
        total = total + mm(part, hit, TN)
    total = jnp.where((iota((CAP * RHS, OBS), 0) // RHS).astype(F32) == rank[0:1, :], total, 0.0)
    pair = (total[0:8] + total[8:16]) + (total[16:24] + total[24:32])
    out[...] = pair[0:RHS] + pair[RHS:]


def unpack(values, target, rank):
    return pl.pallas_call(
        unpack_kernel,
        out_shape=jax.ShapeDtypeStruct((RHS, OBS), F32),
        compiler_params=params(8),
        name="unpack",
    )(values, target, rank)


def swap(x, axis, second, closed):
    count = lax.axis_size(axis)
    pairs = [(i, (i + 1) % count) for i in range(int(second), count, 2) if closed or i + 1 < count]
    return lax.ppermute(x, axis, pairs + [(j, i) for i, j in pairs])


def body(footprints, dual_weights, target_device, target_block, obs_slot, diffusivity):
    target = target_device.reshape(1, OBS)
    packed, rank = pack(footprints, dual_weights.T, target, target_block.reshape(1, OBS), obs_slot.reshape(1, OBS))
    first = swap(diffusivity, "lon", False, True)
    second = swap(diffusivity, "lon", True, True)
    packed, first, second = lax.optimization_barrier((packed, first, second))
    coef, over, root, roots = faces(diffusivity, first, second)
    got = lax.all_to_all(packed, ("lat", "lon"), split_axis=0, concat_axis=0, tiled=True)
    field, rim, inner, beyond, facts = adjoint(got, roots)
    inner = swap(inner, "lat", False, False)
    beyond = swap(beyond, "lat", True, False)
    smooth, outer = diffuse(field, coef, over, root)
    values = finish(smooth, outer, rim, roots, inner, beyond, got, facts)
    returned = lax.all_to_all(values, ("lat", "lon"), split_axis=0, concat_axis=0, tiled=True)
    return unpack(returned, target, rank).T


def solution(mesh):
    placed = (
        P(("lat", "lon"), None),
        P(("lat", "lon"), None),
        P(("lat", "lon"), None),
        P(("lat", "lon")),
        P(("lat", "lon")),
        P("lat", "lon"),
    )
    return jax.shard_map(
        body, mesh=mesh, in_specs=placed, out_specs=P(("lat", "lon"), None), check_vma=False
    )
```
